32 devices in a mesh: groups: 2 (over x), blk: 16 (over z, y, core).
Axes of the slice: x: 2, y: 2, z: 4, core: 2. Of those that a mesh axis runs over, the one named last changes fastest.
Arguments:
- records: bfloat16 [8192, 2048], P(('groups', 'blk')), parts along dimension 0, may hold values from -6 to 6
- dest: int32 [8192, 1], P(('groups', 'blk')), parts along dimension 0, may hold values from 0 to 15; in each aligned block of 256 rows (0 to 255, 256 to 511, ...) at most 32 rows name the same one
- slot: int32 [8192, 1], P(('groups', 'blk')), parts along dimension 0, may hold values from 0 to 255
- valid: int32 [8192, 1], P(('groups', 'blk')), parts along dimension 0, may hold values from 256 to 2048
- masks: int32 [2], replicated, may hold values from 1 to 15, as said below
Outputs:
- correlations: bfloat16 [2, 4096, 128, 128], P(None, ('groups', 'blk')), parts along dimension 1
The draws below stay inside these ranges and needn't reach their ends.
There are 2 independent parts, one for each index of `groups`. The reference program is written for one: setup_inputs(seed, part) draws one part's arguments, and reference() takes and returns one part's arrays. A program takes and returns all parts, laid end to end along the dimension named above; an argument that names none is the same for every part. Nothing has to cross between parts.
Inputs may be any that keep to these rules, and one draw needn't show every extreme that they name: `dest`: in the rows of one device no block is named more than 32 times. `masks`: 2 distinct numbers; one of them is 15.
All inputs are finite; a program needn't handle non-finite values.
Results may differ from the reference program's by a relative error of at most 0.0085.
Values may be sent and summed in bfloat16 or wider, within the bound.
A program may use at most 128 MiB of HBM per device.

```python
import math
import jax
import jax.numpy as jnp
import numpy as np
from jax import lax

CH = 128
NFFT = 2048
F = 256
LAGS = 128
W = 2
ROUNDS = 2
SEG_DEV = 256
CAP = 32
BLOCKS = 16
SEGMENTS = 4096
N_BLK = 16


def draw_masks(key, part):
    third = jax.random.fold_in(jax.random.fold_in(key, 11), 2)
    fourth = jax.random.fold_in(jax.random.fold_in(key, 11), 3)
    count = N_BLK - 1
    score = jax.random.randint(third, (count,), 0, 1 << 20, dtype=jnp.int32)
    score = score * N_BLK + jnp.arange(count, dtype=jnp.int32)
    score = score.at[count - 1].set(-1)
    picked = jnp.argsort(score, stable=True)[:ROUNDS].astype(jnp.int32) + 1
    order = jax.random.permutation(fourth, ROUNDS)
    return picked[order].astype(jnp.int32)


def touch_ends(drawn, key, smallest, top_value):
    longest = drawn.shape.index(max(drawn.shape))
    spots = []
    for shift in (0, 1):
        where = [jax.random.randint(jax.random.fold_in(key, axis), (), 0, length) for axis, length in enumerate(drawn.shape)]
        where[longest] = (where[longest] + shift) % drawn.shape[longest]
        spots.append(tuple(where))
    return drawn.at[spots[0]].set(smallest).at[spots[1]].set(top_value)


def levels(own_key, shape, cuts, low, largest):
    def one(axis_at, shards_of):
        heights = jax.random.uniform(jax.random.fold_in(jax.random.fold_in(own_key, 6), axis_at), (shards_of,), jnp.float32, low / len(cuts), largest / len(cuts))
        return jnp.repeat(jnp.exp(heights), shape[axis_at] // shards_of).reshape((-1,) + (1,) * (len(shape) - axis_at - 1))

    gain = one(*cuts[0])
    for cut in cuts[1:]:
        gain = gain * one(*cut)
    return gain


def assign_block(stream_key, own, number, rows, amount, top, reach, skew):
    sequence = jax.random.permutation(stream_key, amount)
    crowded, common = portions_of(amount, rows * top, reach, skew, True), portions_of(amount, rows * top, reach, skew, False)
    places = jnp.arange(amount)

    def named(lengths, offset_by):
        used = int((lengths > 0).sum())
        fixed = max(1, used // 4)
        passed = fixed + (places - fixed + offset_by * (used - fixed)) % max(1, amount - fixed)
        return jnp.zeros((amount,), jnp.int32).at[sequence[jnp.where(places < fixed, places, passed)]].set(jnp.asarray(lengths, jnp.int32))

    lengths = jnp.where(number % 4 == 0, named(crowded, number // 4), named(common, number - number // 4 - 1))
    mixed = jax.random.permutation(jax.random.fold_in(own, 3), amount)
    source_of, receiver = mixed[0:amount // 2 * 2:2], mixed[1:amount // 2 * 2:2]
    room = jnp.minimum(lengths[source_of] - 1, reach - lengths[receiver]) // 2
    room = jnp.where((source_of == sequence[0]) | (receiver == sequence[0]) | (lengths[receiver] == 0), 0, jnp.maximum(room, 0))
    passed = jax.random.randint(jax.random.fold_in(own, 4), (amount // 2,), 0, 1 << 20) % (room + 1)
    lengths = lengths.at[source_of].add(-passed).at[receiver].add(passed)
    items = jnp.searchsorted(jnp.cumsum(lengths), jnp.arange(rows * top), side="right").astype(jnp.int32)
    table = items.reshape(top, rows).T
    table = table[jax.random.permutation(jax.random.fold_in(own, 1), rows)]
    offset_by = jax.random.randint(jax.random.fold_in(own, 2), (rows, 1), 0, top)
    return jnp.take_along_axis(table, (jnp.arange(top)[None, :] + offset_by) % top, axis=1)


def portions_of(number_of, total, bound, skew, full):
    loads = [(1 << 20) // math.isqrt(grade ** skew) + 1 for grade in range(1, number_of + 1)]
    largest = bound if full else min(bound, max(-(-total // number_of), total * loads[0] // sum(loads)))
    least = 1 if total - largest >= number_of - 1 else 0
    holding, rest = [largest] + [least] * (number_of - 1), total - largest - least * (number_of - 1)
    while rest > 0:
        free = [i for i in range(1, number_of) if holding[i] < largest] or [i for i in range(1, number_of) if holding[i] < bound]
        mass, budget = sum([loads[i] for i in free]), rest
        for i in free:
            addition = min(bound - holding[i], max(1, budget * loads[i] // mass), rest)
            holding[i] = holding[i] + addition
            rest = rest - addition
    return np.array(holding)


def scatter_about(rng, shape, width, limit, cuts=(), kind=jnp.bfloat16):
    drawn = jax.random.normal(rng, shape, jnp.float32) * width
    if len(cuts) > 0:
        drawn = levels(rng, shape, cuts, -0.22, 0.18) * drawn
    return jnp.clip(drawn, min=-limit, max=limit).astype(kind)


def setup_inputs(seed: int = 0, part: int = 0) -> dict:
    arg_keys = jax.random.split(jax.random.key(seed), 6)
    part_keys = jax.random.split(jax.random.fold_in(arg_keys[5], part), 6)
    records = scatter_about(part_keys[0], (SEGMENTS, NFFT), 1.0, 6.0, ((0, 16),))
    dest_keys = jax.random.split(jax.random.fold_in(part_keys[1], 1), SEGMENTS // SEG_DEV)
    dest_turns = jax.random.permutation(jax.random.fold_in(part_keys[1], 3), SEGMENTS // SEG_DEV)
    dest = jax.vmap(lambda own, number: assign_block(jax.random.fold_in(part_keys[1], 2), own, number, SEG_DEV, BLOCKS, 1, CAP, 2))(dest_keys, dest_turns).reshape((SEGMENTS, 1))
    slot = touch_ends(jax.random.randint(part_keys[2], (SEGMENTS, 1), 0, CH * W), jax.random.fold_in(part_keys[2], 1), 0, (CH * W) - 1).astype(jnp.int32)
    valid = touch_ends(jax.random.randint(part_keys[3], (SEGMENTS, 1), NFFT // 8, NFFT + 1), jax.random.fold_in(part_keys[3], 1), NFFT // 8, NFFT).astype(jnp.int32)
    masks = draw_masks(jax.random.fold_in(arg_keys[5], 71), part)
    return dict(records=records, dest=dest, slot=slot, valid=valid, masks=masks)


def forward_table(nfft, bins):
    sample = jnp.arange(nfft, dtype=jnp.int32)[:, None]
    freq = jnp.arange(1, bins + 1, dtype=jnp.int32)[None, :]
    angle = (sample * freq % nfft).astype(jnp.float32) * (2.0 * math.pi / nfft)
    return jnp.concatenate([jnp.cos(angle), -jnp.sin(angle)], axis=1).astype(jnp.bfloat16)

def inverse_table(nfft, bins, lags):
    shift = (jnp.arange(lags, dtype=jnp.int32) - lags // 2) % nfft
    freq = jnp.arange(1, bins + 1, dtype=jnp.int32)[:, None]
    angle = (freq * shift[None, :] % nfft).astype(jnp.float32) * (2.0 * math.pi / nfft)
    return jnp.concatenate([jnp.cos(angle), -jnp.sin(angle)], axis=0).astype(jnp.bfloat16)

def correlate_pair(own, other, itable):
    bins = own.shape[2] // 2
    left = own.astype(jnp.float32)
    right = other.astype(jnp.float32)
    first = jnp.concatenate([left[..., :bins], left[..., bins:]], axis=1)
    second = jnp.concatenate([left[..., bins:], -left[..., :bins]], axis=1)
    both = jnp.concatenate([right[..., :bins], right[..., bins:]], axis=1)
    real_part = jnp.einsum('iwf,jwf->ijf', first, both)
    imag_part = jnp.einsum('iwf,jwf->ijf', second, both)
    cross = jnp.concatenate([real_part, imag_part], axis=-1).astype(jnp.bfloat16)
    chans = own.shape[0]
    scale = 1.0 / math.sqrt(own.shape[1] * bins)
    lagged = jnp.dot(cross.reshape(chans * chans, 2 * bins), itable, preferred_element_type=jnp.float32)
    return (lagged * scale).astype(jnp.bfloat16).reshape(chans, chans, -1)

def reference(records, dest, slot, valid, masks):
    window = jnp.arange(NFFT, dtype=jnp.int32)[None, :] < valid[:, 0:1]
    masked = records * window.astype(jnp.bfloat16)
    target = dest[:, 0] * (CH * W) + slot[:, 0]
    summed = jnp.zeros((BLOCKS * CH * W, NFFT), jnp.float32).at[target].add(masked.astype(jnp.float32))
    coverage = jnp.zeros((BLOCKS * CH * W, NFFT), jnp.float32).at[target].add(window.astype(jnp.float32))
    trace = summed / jnp.maximum(coverage, 1.0)
    meansq = lax.optimization_barrier(jnp.mean(trace * trace, axis=1, keepdims=True))
    normed = (trace * lax.rsqrt(meansq + 1e-06)).astype(jnp.bfloat16)
    spectrum = jnp.dot(normed, forward_table(NFFT, F), preferred_element_type=jnp.float32)
    real_part = spectrum[:, :F]
    imag_part = spectrum[:, F:]
    amplitude = lax.rsqrt(jnp.maximum(real_part * real_part + imag_part * imag_part, NFFT / 4.0))
    white = jnp.concatenate([real_part * amplitude, imag_part * amplitude], axis=1).astype(jnp.bfloat16)
    tiles = white.reshape(BLOCKS, CH, W, 2 * F)
    itable = inverse_table(NFFT, F, LAGS)
    results = []
    for step in range(ROUNDS):
        partner = jnp.arange(BLOCKS, dtype=jnp.int32) ^ masks[step]
        others = tiles[partner]
        out = lax.map(lambda pair: correlate_pair(pair[0], pair[1], itable), (tiles, others))
        results.append(out.reshape(BLOCKS * CH, CH, LAGS))
    return jnp.stack(results)
```

```python
import functools
import math

import jax
import jax.numpy as jnp
import numpy as np
from jax import lax
from jax.experimental import pallas as pl
from jax.experimental.pallas import tpu as pltpu
from jax.sharding import PartitionSpec as P

CH = 128
F = 256
LAGS = 128
W = 2
GROUP = 4
CHUNK = 256
PIECES = 4
GAP = 64.0
LEVELS = ((96, 96, 96, 80, 64, 64, 48, 32), (112, 112, 112, 96, 80, 64, 48, 32))
VMEM = pl.BlockSpec(memory_space=pltpu.VMEM)
SMEM = pl.BlockSpec(memory_space=pltpu.SMEM)
MESH = pl.DeviceIdType.MESH


def forward_table(nfft, bins):
    sample = np.arange(nfft, dtype=np.int64)[:, None]
    freq = np.arange(1, bins + 1, dtype=np.int64)[None, :]
    angle = (sample * freq % nfft).astype(np.float32) * np.float32(2.0 * math.pi / nfft)
    return np.concatenate([np.cos(angle), -np.sin(angle)], axis=1).astype(jnp.bfloat16)


def lag_table(nfft, bins, lags):
    shift = (np.arange(lags, dtype=np.int64) - lags // 2) % nfft
    freq = np.arange(1, bins + 1, dtype=np.int64)[None, :]
    angle = (freq * shift[:, None] % nfft).astype(np.float32) * np.float32(2.0 * math.pi / nfft)
    return np.concatenate([np.cos(angle), -np.sin(angle)], axis=1).astype(jnp.bfloat16)


def met_at(me, distance, owners):
    other = me
    for k in range(owners.bit_length() - 1):
        if distance >> k & 1:
            other = other + (1 << k) * (1 - 2 * lax.rem(lax.div(me, 1 << k), 2))
    return other


def gathered_at(distance):
    bits = GROUP.bit_length() - 1
    return sum((distance >> k & 1) << (bits - 1 - k) for k in range(bits))


def capacities(most, chunks):
    found = []
    for level in LEVELS:
        rows = [-(-level[c * len(level) // chunks] * most // (128 * 16)) * 16 for c in range(chunks)]
        rows = tuple(min(most, max(16, r)) for r in rows)
        if rows not in found:
            found.append(rows)
    full = (most,) * chunks
    return [rows for rows in found if rows != full] + [full]


def plan_kernel(
    records_ref, dest_ref, slot_ref, valid_ref,
    outgoing_ref, goal_ref, level_ref,
    outbox, inbox, levels, send_sem, recv_sem, level_sems,
):
    chunks, planes, most, wide = outgoing_ref.shape
    owners = planes * GROUP
    held = records_ref.shape[0]
    me, part = lax.axis_index("blk"), lax.axis_index("groups")
    parts = levels.shape[0]
    plane = lax.div(me, GROUP)

    barrier = pltpu.get_barrier_semaphore()
    for distance in range(1, owners):
        pl.semaphore_signal(
            barrier, inc=1, device_id={"blk": met_at(me, distance, owners)}, device_id_type=MESH
        )
    for distance in range(1, parts):
        pl.semaphore_signal(
            barrier, inc=1, device_id={"groups": lax.rem(part + distance, parts)}, device_id_type=MESH
        )

    dest, slot, valid = dest_ref[...], slot_ref[...], valid_ref[...]
    group, within = lax.div(dest, GROUP), lax.rem(dest, GROUP)
    key = valid * held + (held - 1 - lax.broadcasted_iota(jnp.int32, (1, held), 1))
    line = lax.broadcasted_iota(jnp.int32, (8, held), 0)
    columns = jnp.where(line == 0, group, jnp.where(line == 1, key, valid)).astype(jnp.float32).T
    key, group_row = key.astype(jnp.float32), group.astype(jnp.float32)
    ahead = (columns[:, 1:2] > key) & (columns[:, 0:1] == group_row)
    rank = jnp.sum(ahead.astype(jnp.float32), axis=0, keepdims=True).astype(jnp.int32)
    reach = lax.div(valid - 1, wide)
    level = jnp.zeros((1, held), jnp.float32)
    for rows in capacities(most, chunks)[:-1]:
        limit = jnp.zeros((1, held), jnp.int32)
        for c in range(chunks):
            limit = jnp.where(reach == c, rows[c], limit)
        level = level + jnp.max((rank >= limit).astype(jnp.float32), axis=1, keepdims=True)
    levels[0] = level[:, :128]

    pl.semaphore_wait(barrier, owners - 1 + parts - 1)
    sideways = []
    for distance in range(1, parts):
        sideways.append(
            pltpu.make_async_remote_copy(
                src_ref=levels.at[0],
                dst_ref=levels.at[distance],
                send_sem=level_sems.at[0, distance],
                recv_sem=level_sems.at[1, distance],
                device_id={"groups": lax.rem(part + distance, parts)},
                device_id_type=MESH,
            )
        )
        sideways[-1].start()

    lines = max(8, planes)
    named = lax.broadcasted_iota(jnp.int32, (lines, held), 0) == group
    ranked = (lax.broadcasted_iota(jnp.int32, (128, held), 0) == rank).astype(jnp.float32)
    ranked = ranked.astype(jnp.bfloat16)

    def spread(values):
        values = jnp.where(named, values, 0).astype(jnp.float32).astype(jnp.bfloat16)
        return lax.dot_general(
            values, ranked, (((1,), (1,)), ((), ())), preferred_element_type=jnp.float32
        )

    code = spread(within + 1) * 256.0 + spread(slot)
    for p in range(planes):
        outbox[p, 0:1, :] = code[p : p + 1]

    for copy in sideways:
        copy.wait()
    level = levels[0]
    for distance in range(1, parts):
        level = jnp.maximum(level, levels[distance])
    for p in range(planes):
        outbox[p, 1:2, :] = level
    copies = []
    for distance in range(owners - 1, 0, -1):
        other = met_at(me, distance, owners)
        copies.append(
            pltpu.make_async_remote_copy(
                src_ref=outbox.at[lax.div(other, GROUP)],
                dst_ref=inbox.at[gathered_at(distance % GROUP) * planes + plane],
                send_sem=send_sem.at[distance],
                recv_sem=recv_sem.at[distance],
                device_id={"blk": other},
                device_id_type=MESH,
            )
        )
        copies[-1].start()
    inbox[plane] = outbox[plane]

    spots = planes * most
    place = lax.broadcasted_iota(jnp.int32, (spots, held), 0) == group * most + rank
    place = place.astype(jnp.float32).astype(jnp.bfloat16)
    ends = columns[:, 2:3].astype(jnp.int32)
    for c in range(chunks):
        window = lax.broadcasted_iota(jnp.int32, (held, wide), 1) + c * wide < ends
        window = window.astype(jnp.float32).astype(jnp.bfloat16)
        data = records_ref[:, c * wide : (c + 1) * wide] * window + (GAP - GAP * window)
        packed = jnp.dot(place, data, preferred_element_type=jnp.float32)
        outgoing_ref[c] = packed.astype(jnp.bfloat16).reshape(planes, most, wide)

    for copy in copies:
        copy.wait()
    code = inbox[:, 0, :]
    level_ref[0] = jnp.max(inbox[:, 1, :]).astype(jnp.int32)
    kept = owners * most
    at = lax.broadcasted_iota(jnp.int32, (128, kept), 1)
    sown = lax.broadcasted_iota(jnp.int32, (128, kept), 0) == lax.rem(at, most)
    sown = sown.astype(jnp.float32).astype(jnp.bfloat16)
    owner = (code * (1.0 / 256.0)).astype(jnp.int32).astype(jnp.float32)
    slots = code - owner * 256.0
    at = lax.broadcasted_iota(jnp.int32, (owners, kept), 1)
    mine = lax.broadcasted_iota(jnp.int32, (owners, kept), 0) == lax.div(at, most)

    def line_up(values):
        values = jnp.dot(values.astype(jnp.bfloat16), sown, preferred_element_type=jnp.float32)
        return jnp.sum(jnp.where(mine, values, 0.0), axis=0, keepdims=True).astype(jnp.int32)

    slots = line_up(slots)
    goal = lax.rem(slots, W) * CH + lax.div(slots, W)
    goal_ref[...] = jnp.where(line_up(owner) == lax.rem(me, GROUP) + 1, goal, -1)


def deliver_kernel(
    caps, outgoing_ref, goal_ref, masks_ref, table_hbm,
    own_ref, met_ref,
    arrived, select, table, spectrum, energy, tile, leaving, landing,
    plane_send, plane_recv, gather_send, gather_recv, own_sem, table_sem,
    far_send, far_recv, hop_send, hop_recv,
):
    chunks, _, planes, most, wide = arrived.shape
    owners = planes * GROUP
    nfft = chunks * wide
    kept = owners * most
    me = lax.axis_index("blk")
    plane = lax.div(me, GROUP)
    last = owners - 1
    bits = list(range(owners.bit_length() - 3, -1, -1))
    steps = list(range(GROUP.bit_length() - 2, -1, -1))

    for c in range(chunks):
        if caps[c] < most:
            rest = arrived.at[c, :, :, caps[c] :, :]
            rest[...] = jnp.full(rest.shape, GAP, jnp.bfloat16)
    barrier = pltpu.get_barrier_semaphore()
    peers = {GROUP * d for d in range(1, planes)} | {1 << k for k in steps + bits} | {last}
    for distance in sorted(peers):
        pl.semaphore_signal(
            barrier, inc=1, device_id={"blk": met_at(me, distance, owners)}, device_id_type=MESH
        )
    fetch = pltpu.make_async_copy(table_hbm, table, table_sem)
    fetch.start()
    pl.semaphore_wait(barrier, len(peers))

    def send(distance, source, target, send_sem, recv_sem):
        copy = pltpu.make_async_remote_copy(
            src_ref=source,
            dst_ref=target,
            send_sem=send_sem,
            recv_sem=recv_sem,
            device_id={"blk": met_at(me, distance, owners)},
            device_id_type=MESH,
        )
        copy.start()
        return copy

    sent, local, gathers = {}, {}, {}

    def begin(c):
        rows = pl.ds(0, caps[c])
        for d in range(planes - 1, 0, -1):
            other = lax.div(met_at(me, GROUP * d, owners), GROUP)
            sent[c, d] = send(
                GROUP * d,
                outgoing_ref.at[c, other, rows],
                arrived.at[c, 0, plane, rows],
                plane_send.at[c, d],
                plane_recv.at[c, d],
            )
        local[c] = pltpu.make_async_copy(
            outgoing_ref.at[c, plane, rows], arrived.at[c, 0, plane, rows], own_sem.at[c]
        )
        local[c].start()

    def forward(c, step, part):
        low, count = (0, 1) if part == 0 else (1 << (part - 1), 1 << (part - 1))
        rows = pl.ds(0, caps[c])
        gathers[c, step, part] = send(
            1 << steps[step],
            arrived.at[c, pl.ds(low, count), :, rows],
            arrived.at[c, pl.ds(low + (1 << step), count), :, rows],
            gather_send.at[c, step, part],
            gather_recv.at[c, step, part],
        )

    goal = goal_ref[...]
    width = min(512, kept)
    for base in range(0, kept, width):
        chosen = lax.broadcasted_iota(jnp.int32, (CH * W, width), 0) == goal[:, base : base + width]
        select[:, base : base + width] = chosen.astype(jnp.float32).astype(jnp.bfloat16)

    def compute(c):
        data = arrived[c].reshape(kept, wide)
        window = jnp.minimum(jnp.maximum(GAP / 2 - data, 0.0), 1.0)
        total = jnp.dot(select[...], data * window, preferred_element_type=jnp.float32)
        count = jnp.dot(select[...], window, preferred_element_type=jnp.float32)
        trace = total / jnp.maximum(count, 1.0)
        squares = trace * trace
        squares = sum(squares[:, k : k + 128] for k in range(0, wide, 128))
        part = jnp.dot(
            trace.astype(jnp.bfloat16),
            table[c * wide : (c + 1) * wide, :],
            preferred_element_type=jnp.float32,
        )
        if c == 0:
            energy[...], spectrum[...] = squares, part
        else:
            energy[...] += squares
            spectrum[...] += part

    ahead = min(3, chunks)
    for c in range(ahead):
        begin(c)
    depth = len(steps)
    for turn in range(chunks + depth + 1):
        for stage in range(depth + 1, -1, -1):
            c = turn - stage
            if not 0 <= c < chunks:
                continue
            if stage == 0:
                for d in range(planes - 1, 0, -1):
                    sent[c, d].wait_recv()
                local[c].wait()
                if c + ahead < chunks:
                    begin(c + ahead)
                for step in range(depth):
                    forward(c, step, 0)
            elif stage <= depth:
                for part in range(stage):
                    gathers[c, stage - 1, part].wait_recv()
                for step in range(stage, depth):
                    forward(c, step, stage)
            if stage == depth:
                if c == 0:
                    fetch.wait()
                compute(c)

    second = masks_ref[0] ^ masks_ref[1] ^ last
    use_far = lax.div(second, 1 << (len(bits)))
    path = second + use_far * (last - 2 * second)
    size = CH // PIECES

    def choose(flag, yes, no):
        flag = jnp.full(yes.shape, flag.astype(jnp.float32), jnp.float32).astype(jnp.bfloat16)
        return yes * flag + no * (1 - flag)

    factor = lax.rsqrt(jnp.sum(energy[...], axis=1, keepdims=True) * (1.0 / nfft) + 1e-06)
    far = []
    for q in range(PIECES):
        rows = slice(q * size, (q + 1) * size)
        for w in range(W):
            at = slice(w * CH + q * size, w * CH + (q + 1) * size)
            parts = spectrum[at, :] * factor[at]
            real_part, imag_part = parts[:, :F], parts[:, F:]
            amplitude = lax.rsqrt(
                jnp.maximum(real_part * real_part + imag_part * imag_part, nfft / 4.0)
            )
            real_part = (real_part * amplitude).astype(jnp.bfloat16)
            imag_part = (imag_part * amplitude).astype(jnp.bfloat16)
            base = 2 * F * w
            tile[rows, base : base + F] = real_part
            tile[rows, base + F : base + 2 * F] = imag_part
            own_ref[rows, base : base + F] = real_part.astype(jnp.float32)
            own_ref[rows, base + F : base + 2 * F] = imag_part.astype(jnp.float32)
        rows = pl.ds(q * size, size)
        far.append(send(last, tile.at[rows], met_ref.at[rows], far_send.at[q], far_recv.at[q]))

    hops = {}
    for turn in range(PIECES + len(bits)):
        for stage in range(len(bits), -1, -1):
            q = turn - stage
            if not 0 <= q < PIECES:
                continue
            rows = slice(q * size, (q + 1) * size)
            if stage == 0:
                far[q].wait_recv()
                value = choose(use_far, met_ref[rows], tile[rows])
            else:
                hops[stage - 1, q].wait_recv()
                taken = lax.rem(lax.div(path, 1 << bits[stage - 1]), 2)
                value = choose(taken, landing[stage - 1, rows], leaving[stage - 1, rows])
            if stage == len(bits):
                met_ref[CH + q * size : CH + (q + 1) * size] = value
            else:
                leaving[stage, rows] = value
                spot = pl.ds(q * size, size)
                hops[stage, q] = send(
                    1 << bits[stage],
                    leaving.at[stage, spot],
                    landing.at[stage, spot],
                    hop_send.at[stage, q],
                    hop_recv.at[stage, q],
                )
    for copy in list(sent.values()) + list(gathers.values()) + far + list(hops.values()):
        copy.wait_send()


def correlate_kernel(masks_ref, own_ref, other_ref, table_ref, out_ref, turned, *, last):
    scale = 1.0 / math.sqrt(W * F)
    cosine, sine = table_ref[:, :F], table_ref[:, F:]
    far_round = (masks_ref[0] != last).astype(jnp.int32)
    slots, step = turned.shape[0], own_ref.shape[1]

    for index in range(step // 2):
        at = index % slots
        for half in range(2):
            mine = own_ref[0, index * 2 + half : index * 2 + half + 1, :].astype(jnp.bfloat16)
            rows = slice(half * LAGS, (half + 1) * LAGS)
            for w in range(W):
                base = 2 * F * w
                ur, ui = mine[:, base : base + F], mine[:, base + F : base + 2 * F]
                turned[at, rows, base : base + F] = cosine * ur + sine * ui
                turned[at, rows, base + F : base + 2 * F] = cosine * ui - sine * ur
        product = lax.dot_general(
            other_ref[...],
            turned[at],
            (((1,), (1,)), ((), ())),
            preferred_element_type=jnp.float32,
        )
        product = (product * scale).astype(jnp.bfloat16)
        for half in range(2):
            lags = slice(half * LAGS, (half + 1) * LAGS)
            out_ref[far_round, index * 2 + half] = product[:CH, lags]
            out_ref[1 - far_round, index * 2 + half] = product[CH:, lags]


def local(records, dest, slot, valid, masks):
    owners, parts = lax.axis_size("blk"), lax.axis_size("groups")
    held, nfft = records.shape
    rounds = masks.shape[0]
    planes, chunks = owners // GROUP, nfft // CHUNK
    most = max(16, GROUP * 2 * held // owners)
    width = 2 * F * W
    limit = 56 * 2**20
    outgoing, goal, level = pl.pallas_call(
        plan_kernel,
        out_shape=[
            jax.ShapeDtypeStruct((chunks, planes, most, CHUNK), jnp.bfloat16),
            jax.ShapeDtypeStruct((1, owners * most), jnp.int32),
            jax.ShapeDtypeStruct((1,), jnp.int32),
        ],
        in_specs=[VMEM] * 4,
        out_specs=[VMEM, VMEM, SMEM],
        scratch_shapes=[
            pltpu.VMEM((planes, 2, 128), jnp.float32),
            pltpu.VMEM((owners, 2, 128), jnp.float32),
            pltpu.VMEM((parts, 1, 128), jnp.float32),
            pltpu.SemaphoreType.DMA((owners,)),
            pltpu.SemaphoreType.DMA((owners,)),
            pltpu.SemaphoreType.DMA((2, parts)),
        ],
        compiler_params=pltpu.CompilerParams(
            vmem_limit_bytes=limit, collective_id=0, has_side_effects=True
        ),
        name="plan",
    )(records, dest.reshape(1, held), slot.reshape(1, held), valid.reshape(1, held))

    last = owners - 1
    hops = owners.bit_length() - 2
    depth = GROUP.bit_length() - 1

    def deliver(number, caps):
        def call(outgoing, goal, masks, table):
            return pl.pallas_call(
                functools.partial(deliver_kernel, caps),
                out_shape=[
                    jax.ShapeDtypeStruct((CH, width), jnp.float32),
                    jax.ShapeDtypeStruct((rounds * CH, width), jnp.bfloat16),
                ],
                in_specs=[pl.BlockSpec(memory_space=pl.ANY), VMEM, SMEM, pl.BlockSpec(memory_space=pl.ANY)],
                out_specs=[VMEM] * 2,
                scratch_shapes=[
                    pltpu.VMEM((chunks, GROUP, planes, most, CHUNK), jnp.bfloat16),
                    pltpu.VMEM((CH * W, owners * most), jnp.bfloat16),
                    pltpu.VMEM((nfft, 2 * F), jnp.bfloat16),
                    pltpu.VMEM((CH * W, 2 * F), jnp.float32),
                    pltpu.VMEM((CH * W, 128), jnp.float32),
                    pltpu.VMEM((CH, width), jnp.bfloat16),
                    pltpu.VMEM((hops, CH, width), jnp.bfloat16),
                    pltpu.VMEM((hops, CH, width), jnp.bfloat16),
                    pltpu.SemaphoreType.DMA((chunks, planes)),
                    pltpu.SemaphoreType.DMA((chunks, planes)),
                    pltpu.SemaphoreType.DMA((chunks, depth, depth)),
                    pltpu.SemaphoreType.DMA((chunks, depth, depth)),
                    pltpu.SemaphoreType.DMA((chunks,)),
                    pltpu.SemaphoreType.DMA,
                    pltpu.SemaphoreType.DMA((PIECES,)),
                    pltpu.SemaphoreType.DMA((PIECES,)),
                    pltpu.SemaphoreType.DMA((hops, PIECES)),
                    pltpu.SemaphoreType.DMA((hops, PIECES)),
                ],
                compiler_params=pltpu.CompilerParams(
                    vmem_limit_bytes=limit, collective_id=number, has_side_effects=True
                ),
                name=f"deliver{number}",
            )(outgoing, goal, masks, table)

        return call

    sizes = capacities(most, chunks)
    calls = [deliver(number + 1, caps) for number, caps in enumerate(sizes)]
    own, other = lax.switch(
        level[0], calls, outgoing, goal, masks, jnp.asarray(forward_table(nfft, F))
    )
    step = 16
    return pl.pallas_call(
        functools.partial(correlate_kernel, last=last),
        grid=(CH // step,),
        out_shape=jax.ShapeDtypeStruct((rounds, CH, CH, LAGS), jnp.bfloat16),
        in_specs=[
            SMEM,
            pl.BlockSpec((1, step, width), lambda i: (i, 0, 0)),
            pl.BlockSpec((rounds * CH, width), lambda i: (0, 0)),
            pl.BlockSpec((LAGS, 2 * F), lambda i: (0, 0)),
        ],
        out_specs=pl.BlockSpec((rounds, step, CH, LAGS), lambda i: (0, i, 0, 0)),
        scratch_shapes=[pltpu.VMEM((4, 2 * LAGS, width), jnp.bfloat16)],
        compiler_params=pltpu.CompilerParams(vmem_limit_bytes=limit),
        name="correlate",
    )(
        masks,
        own.reshape(CH // step, step, width),
        other,
        jnp.asarray(lag_table(nfft, F, LAGS)),
    )


def solution(mesh):
    return jax.shard_map(
        local,
        mesh=mesh,
        in_specs=(
            P(("groups", "blk"), None),
            P(("groups", "blk"), None),
            P(("groups", "blk"), None),
            P(("groups", "blk"), None),
            P(),
        ),
        out_specs=P(None, ("groups", "blk"), None, None),
        check_vma=False,
    )
```

```python
import functools
import math

import jax
import jax.numpy as jnp
import numpy as np
from jax import lax
from jax.experimental import pallas as pl
from jax.experimental.pallas import tpu as pltpu
from jax.sharding import PartitionSpec as P

CH = 128
F = 256
LAGS = 128
W = 2
GROUP = 4
CHUNK = 256
PIECES = 4
FLIGHT = 2
GAP = 64.0
LEVELS = ((96, 96, 96, 80, 64, 64, 48, 32), (112, 112, 112, 96, 80, 64, 48, 32))
VMEM = pl.BlockSpec(memory_space=pltpu.VMEM)
SMEM = pl.BlockSpec(memory_space=pltpu.SMEM)
MESH = pl.DeviceIdType.MESH


def forward_table(nfft, bins):
    sample = np.arange(nfft, dtype=np.int64)[:, None]
    freq = np.arange(1, bins + 1, dtype=np.int64)[None, :]
    angle = (sample * freq % nfft).astype(np.float32) * np.float32(2.0 * math.pi / nfft)
    return np.concatenate([np.cos(angle), -np.sin(angle)], axis=1).astype(jnp.bfloat16)


def lag_table(nfft, bins, lags):
    shift = (np.arange(lags, dtype=np.int64) - lags // 2) % nfft
    freq = np.arange(1, bins + 1, dtype=np.int64)[None, :]
    angle = (freq * shift[:, None] % nfft).astype(np.float32) * np.float32(2.0 * math.pi / nfft)
    return np.concatenate([np.cos(angle), -np.sin(angle)], axis=1).astype(jnp.bfloat16)


def met_at(me, distance, owners):
    other = me
    for k in range(owners.bit_length() - 1):
        if distance >> k & 1:
            other = other + (1 << k) * (1 - 2 * lax.rem(lax.div(me, 1 << k), 2))
    return other


def gathered_at(distance):
    bits = GROUP.bit_length() - 1
    return sum((distance >> k & 1) << (bits - 1 - k) for k in range(bits))


def capacities(most, chunks):
    found = []
    for level in LEVELS:
        rows = [-(-level[c * len(level) // chunks] * most // (128 * 16)) * 16 for c in range(chunks)]
        rows = tuple(min(most, max(16, r)) for r in rows)
        if rows not in found:
            found.append(rows)
    full = (most,) * chunks
    return [rows for rows in found if rows != full] + [full]


def plan_kernel(
    records_ref, dest_ref, slot_ref, valid_ref,
    outgoing_ref, goal_ref, level_ref,
    outbox, inbox, levels, send_sem, recv_sem, level_sems,
):
    chunks, planes, most, wide = outgoing_ref.shape
    owners = planes * GROUP
    held = records_ref.shape[0]
    me, part = lax.axis_index("blk"), lax.axis_index("groups")
    parts = levels.shape[0]
    shift = most.bit_length() - 1
    plane = lax.div(me, GROUP)

    barrier = pltpu.get_barrier_semaphore()
    for distance in range(1, owners):
        pl.semaphore_signal(
            barrier, inc=1, device_id={"blk": met_at(me, distance, owners)}, device_id_type=MESH
        )
    abroad = [
        (turn, distance, {"groups": lax.rem(part + turn, parts), "blk": met_at(me, distance, owners)})
        for turn in range(1, parts)
        for distance in range(owners)
    ]
    for _, _, other in abroad:
        pl.semaphore_signal(barrier, inc=1, device_id=other, device_id_type=MESH)

    dest, slot, valid = dest_ref[...], slot_ref[...], valid_ref[...]
    group, within = lax.div(dest, GROUP), lax.rem(dest, GROUP)
    key = valid * held + (held - 1 - lax.broadcasted_iota(jnp.int32, (1, held), 1))
    line = lax.broadcasted_iota(jnp.int32, (8, held), 0)
    columns = jnp.where(line == 0, group, jnp.where(line == 1, key, valid)).astype(jnp.float32).T
    key, group_row = key.astype(jnp.float32), group.astype(jnp.float32)
    ahead = (columns[:, 1:2] > key) & (columns[:, 0:1] == group_row)
    rank = jnp.sum(ahead.astype(jnp.float32), axis=0, keepdims=True).astype(jnp.int32)
    reach = lax.div(valid - 1, wide)
    level = jnp.zeros((1, held), jnp.float32)
    for rows in capacities(most, chunks)[:-1]:
        limit = jnp.zeros((1, held), jnp.int32)
        for c in range(chunks):
            limit = jnp.where(reach == c, rows[c], limit)
        level = level + jnp.max((rank >= limit).astype(jnp.float32), axis=1, keepdims=True)
    levels[0, 0] = level[:, :128]

    lines = max(8, planes)
    named = lax.broadcasted_iota(jnp.int32, (lines, held), 0) == group
    ranked = (lax.broadcasted_iota(jnp.int32, (128, held), 0) == rank).astype(jnp.float32)
    ranked = ranked.astype(jnp.bfloat16)

    def spread(values):
        values = jnp.where(named, values, 0).astype(jnp.float32).astype(jnp.bfloat16)
        return lax.dot_general(
            values, ranked, (((1,), (1,)), ((), ())), preferred_element_type=jnp.float32
        )

    code = spread(within + 1) * 256.0 + spread(slot)
    for p in range(planes):
        outbox[p, 0:1, :] = code[p : p + 1]
        outbox[p, 1:2, :] = level[:, :128]

    pl.semaphore_wait(barrier, owners * parts - 1)
    copies = []
    for turn, distance, other in abroad:
        copies.append(
            pltpu.make_async_remote_copy(
                src_ref=levels.at[0, 0],
                dst_ref=levels.at[turn, distance],
                send_sem=level_sems.at[0, turn, distance],
                recv_sem=level_sems.at[1, turn, distance],
                device_id=other,
                device_id_type=MESH,
            )
        )
        copies[-1].start()
    for distance in range(owners - 1, 0, -1):
        other = met_at(me, distance, owners)
        copies.append(
            pltpu.make_async_remote_copy(
                src_ref=outbox.at[lax.div(other, GROUP)],
                dst_ref=inbox.at[gathered_at(distance % GROUP) * planes + plane],
                send_sem=send_sem.at[distance],
                recv_sem=recv_sem.at[distance],
                device_id={"blk": other},
                device_id_type=MESH,
            )
        )
        copies[-1].start()
    inbox[plane] = outbox[plane]

    spots = planes * most
    place = lax.broadcasted_iota(jnp.int32, (spots, held), 0) == group * most + rank
    place = place.astype(jnp.float32).astype(jnp.bfloat16)
    ends = columns[:, 2:3].astype(jnp.int32)
    for c in range(chunks):
        window = lax.broadcasted_iota(jnp.int32, (held, wide), 1) + c * wide < ends
        window = window.astype(jnp.float32).astype(jnp.bfloat16)
        data = records_ref[:, c * wide : (c + 1) * wide] * window + (GAP - GAP * window)
        packed = jnp.dot(place, data, preferred_element_type=jnp.float32)
        outgoing_ref[c] = packed.astype(jnp.bfloat16).reshape(planes, most, wide)

    kept = owners * most
    at = lax.broadcasted_iota(jnp.int32, (128, kept), 1)
    sown = lax.broadcasted_iota(jnp.int32, (128, kept), 0) == at - (at >> shift << shift)
    sown = sown.astype(jnp.float32).astype(jnp.bfloat16)
    for copy in copies:
        copy.wait()
    code = inbox[:, 0, :]
    level = jnp.max(inbox[:, 1, :], axis=0, keepdims=True)
    for turn, distance, _ in abroad:
        level = jnp.maximum(level, levels[turn, distance])
    level_ref[0] = jnp.max(level).astype(jnp.int32)
    owner = (code * (1.0 / 256.0)).astype(jnp.int32).astype(jnp.float32)
    slots = code - owner * 256.0
    at = lax.broadcasted_iota(jnp.int32, (owners, kept), 1)
    mine = lax.broadcasted_iota(jnp.int32, (owners, kept), 0) == at >> shift

    def line_up(values):
        values = jnp.dot(values.astype(jnp.bfloat16), sown, preferred_element_type=jnp.float32)
        return jnp.sum(jnp.where(mine, values, 0.0), axis=0, keepdims=True).astype(jnp.int32)

    slots = line_up(slots)
    goal = (slots & (W - 1)) * CH + (slots >> (W.bit_length() - 1))
    goal_ref[...] = jnp.where(line_up(owner) == lax.rem(me, GROUP) + 1, goal, -1)


def deliver_kernel(
    caps, outgoing_ref, goal_ref, masks_ref, table_hbm,
    own_ref, met_ref,
    arrived, select, table, spectrum, energy, tile, leaving, landing,
    plane_send, plane_recv, gather_send, gather_recv, own_sem, table_sem,
    far_send, far_recv, hop_send, hop_recv,
):
    chunks, _, planes, most, wide = arrived.shape
    owners = planes * GROUP
    nfft = chunks * wide
    kept = owners * most
    me = lax.axis_index("blk")
    plane = lax.div(me, GROUP)
    last = owners - 1
    bits = list(range(owners.bit_length() - 3, -1, -1))
    steps = list(range(GROUP.bit_length() - 2, -1, -1))

    for c in range(chunks):
        if caps[c] < most:
            rest = arrived.at[c, :, :, caps[c] :, :]
            rest[...] = jnp.full(rest.shape, GAP, jnp.bfloat16)
    barrier = pltpu.get_barrier_semaphore()
    peers = {GROUP * d for d in range(1, planes)} | {1 << k for k in steps + bits} | {last}
    for distance in sorted(peers):
        pl.semaphore_signal(
            barrier, inc=1, device_id={"blk": met_at(me, distance, owners)}, device_id_type=MESH
        )
    fetch = pltpu.make_async_copy(table_hbm, table, table_sem)
    fetch.start()
    pl.semaphore_wait(barrier, len(peers))

    def send(distance, source, target, send_sem, recv_sem):
        copy = pltpu.make_async_remote_copy(
            src_ref=source,
            dst_ref=target,
            send_sem=send_sem,
            recv_sem=recv_sem,
            device_id={"blk": met_at(me, distance, owners)},
            device_id_type=MESH,
        )
        copy.start()
        return copy

    sent, local, gathers = {}, {}, {}

    def begin(c):
        rows = pl.ds(0, caps[c])
        for d in range(planes - 1, 0, -1):
            other = lax.div(met_at(me, GROUP * d, owners), GROUP)
            sent[c, d] = send(
                GROUP * d,
                outgoing_ref.at[c, other, rows],
                arrived.at[c, 0, plane, rows],
                plane_send.at[c, d],
                plane_recv.at[c, d],
            )
        local[c] = pltpu.make_async_copy(
            outgoing_ref.at[c, plane, rows], arrived.at[c, 0, plane, rows], own_sem.at[c]
        )
        local[c].start()

    def forward(c, step, spot, d):
        at = lax.div(met_at(me, GROUP * d, owners), GROUP)
        rows = pl.ds(0, caps[c])
        target = spot + (1 << step)
        gathers[c, target, d] = send(
            1 << steps[step],
            arrived.at[c, spot, at, rows],
            arrived.at[c, target, at, rows],
            gather_send.at[c, target, d],
            gather_recv.at[c, target, d],
        )

    goal = goal_ref[...]
    width = min(512, kept)
    for base in range(0, kept, width):
        chosen = lax.broadcasted_iota(jnp.int32, (CH * W, width), 0) == goal[:, base : base + width]
        select[:, base : base + width] = chosen.astype(jnp.float32).astype(jnp.bfloat16)

    def compute(c):
        data = arrived[c].reshape(kept, wide)
        window = jnp.minimum(jnp.maximum(GAP / 2 - data, 0.0), 1.0)
        total = jnp.dot(select[...], data * window, preferred_element_type=jnp.float32)
        count = jnp.dot(select[...], window, preferred_element_type=jnp.float32)
        trace = total / jnp.maximum(count, 1.0)
        squares = trace * trace
        squares = sum(squares[:, k : k + 128] for k in range(0, wide, 128))
        part = jnp.dot(
            trace.astype(jnp.bfloat16),
            table[c * wide : (c + 1) * wide, :],
            preferred_element_type=jnp.float32,
        )
        if c == 0:
            energy[...], spectrum[...] = squares, part
        else:
            energy[...] += squares
            spectrum[...] += part

    ahead = min(3, chunks)
    for c in range(ahead):
        begin(c)
    depth = len(steps)
    for turn in range(chunks + depth + 1):
        for stage in range(depth + 2):
            c = turn - stage
            if not 0 <= c < chunks:
                continue
            if stage == 0:
                for d in range(planes):
                    if d == 0:
                        local[c].wait()
                    else:
                        sent[c, d].wait_recv()
                    for step in range(depth):
                        forward(c, step, 0, d)
                if c + ahead < chunks:
                    begin(c + ahead)
            elif stage <= depth:
                for spot in range(1 << (stage - 1), 1 << stage):
                    for d in range(planes):
                        gathers[c, spot, d].wait_recv()
                        for step in range(stage, depth):
                            forward(c, step, spot, d)
            else:
                if c == 0:
                    fetch.wait()
                compute(c)

    second = masks_ref[0] ^ masks_ref[1] ^ last
    use_far = lax.div(second, 1 << (len(bits)))
    path = second + use_far * (last - 2 * second)
    size = CH // PIECES

    def choose(flag, yes, no):
        flag = jnp.full(yes.shape, flag.astype(jnp.float32), jnp.float32).astype(jnp.bfloat16)
        return yes * flag + no * (1 - flag)

    factor = lax.rsqrt(jnp.sum(energy[...], axis=1, keepdims=True) * (1.0 / nfft) + 1e-06)
    far = []

    def far_copy(q):
        rows = pl.ds(q * size, size)
        far.append(send(last, tile.at[rows], met_ref.at[rows], far_send.at[q], far_recv.at[q]))

    for q in range(PIECES):
        rows = slice(q * size, (q + 1) * size)
        for w in range(W):
            at = slice(w * CH + q * size, w * CH + (q + 1) * size)
            parts = spectrum[at, :] * factor[at]
            real_part, imag_part = parts[:, :F], parts[:, F:]
            amplitude = lax.rsqrt(
                jnp.maximum(real_part * real_part + imag_part * imag_part, nfft / 4.0)
            )
            real_part = (real_part * amplitude).astype(jnp.bfloat16)
            imag_part = (imag_part * amplitude).astype(jnp.bfloat16)
            base = 2 * F * w
            tile[rows, base : base + F] = real_part
            tile[rows, base + F : base + 2 * F] = imag_part
            own_ref[rows, base : base + F] = real_part.astype(jnp.float32)
            own_ref[rows, base + F : base + 2 * F] = imag_part.astype(jnp.float32)
        if q < FLIGHT:
            far_copy(q)

    hops = {}
    for turn in range(PIECES + len(bits)):
        for stage in range(len(bits) + 1):
            q = turn - stage
            if not 0 <= q < PIECES:
                continue
            rows = slice(q * size, (q + 1) * size)
            if stage == 0:
                far[q].wait_recv()
                if q + FLIGHT < PIECES:
                    far_copy(q + FLIGHT)
                value = choose(use_far, met_ref[rows], tile[rows])
            else:
                hops[stage - 1, q].wait_recv()
                taken = lax.rem(lax.div(path, 1 << bits[stage - 1]), 2)
                value = choose(taken, landing[stage - 1, rows], leaving[stage - 1, rows])
            if stage == len(bits):
                met_ref[CH + q * size : CH + (q + 1) * size] = value
            else:
                leaving[stage, rows] = value
                spot = pl.ds(q * size, size)
                hops[stage, q] = send(
                    1 << bits[stage],
                    leaving.at[stage, spot],
                    landing.at[stage, spot],
                    hop_send.at[stage, q],
                    hop_recv.at[stage, q],
                )
    for copy in list(sent.values()) + list(gathers.values()) + far + list(hops.values()):
        copy.wait_send()


def correlate_kernel(masks_ref, own_ref, other_ref, table_ref, out_ref, turned, *, last):
    scale = 1.0 / math.sqrt(W * F)
    cosine, sine = table_ref[:, :F], table_ref[:, F:]
    far_round = (masks_ref[0] != last).astype(jnp.int32)
    slots, step = turned.shape[0], own_ref.shape[1]

    for index in range(step // 2):
        at = index % slots
        for half in range(2):
            mine = own_ref[0, index * 2 + half : index * 2 + half + 1, :].astype(jnp.bfloat16)
            rows = slice(half * LAGS, (half + 1) * LAGS)
            for w in range(W):
                base = 2 * F * w
                ur, ui = mine[:, base : base + F], mine[:, base + F : base + 2 * F]
                turned[at, rows, base : base + F] = cosine * ur + sine * ui
                turned[at, rows, base + F : base + 2 * F] = cosine * ui - sine * ur
        product = lax.dot_general(
            other_ref[...],
            turned[at],
            (((1,), (1,)), ((), ())),
            preferred_element_type=jnp.float32,
        )
        product = (product * scale).astype(jnp.bfloat16)
        for half in range(2):
            lags = slice(half * LAGS, (half + 1) * LAGS)
            out_ref[far_round, index * 2 + half] = product[:CH, lags]
            out_ref[1 - far_round, index * 2 + half] = product[CH:, lags]


def local(records, dest, slot, valid, masks):
    owners, parts = lax.axis_size("blk"), lax.axis_size("groups")
    held, nfft = records.shape
    rounds = masks.shape[0]
    planes, chunks = owners // GROUP, nfft // CHUNK
    most = max(16, GROUP * 2 * held // owners)
    width = 2 * F * W
    limit = 56 * 2**20
    outgoing, goal, level = pl.pallas_call(
        plan_kernel,
        out_shape=[
            jax.ShapeDtypeStruct((chunks, planes, most, CHUNK), jnp.bfloat16),
            jax.ShapeDtypeStruct((1, owners * most), jnp.int32),
            jax.ShapeDtypeStruct((1,), jnp.int32),
        ],
        in_specs=[VMEM] * 4,
        out_specs=[VMEM, VMEM, SMEM],
        scratch_shapes=[
            pltpu.VMEM((planes, 2, 128), jnp.float32),
            pltpu.VMEM((owners, 2, 128), jnp.float32),
            pltpu.VMEM((parts, owners, 1, 128), jnp.float32),
            pltpu.SemaphoreType.DMA((owners,)),
            pltpu.SemaphoreType.DMA((owners,)),
            pltpu.SemaphoreType.DMA((2, parts, owners)),
        ],
        compiler_params=pltpu.CompilerParams(
            vmem_limit_bytes=limit, collective_id=0, has_side_effects=True
        ),
        name="plan",
    )(records, dest.reshape(1, held), slot.reshape(1, held), valid.reshape(1, held))

    last = owners - 1
    hops = owners.bit_length() - 2
    depth = GROUP.bit_length() - 1

    def deliver(number, caps):
        def call(outgoing, goal, masks, table):
            return pl.pallas_call(
                functools.partial(deliver_kernel, caps),
                out_shape=[
                    jax.ShapeDtypeStruct((CH, width), jnp.float32),
                    jax.ShapeDtypeStruct((rounds * CH, width), jnp.bfloat16),
                ],
                in_specs=[pl.BlockSpec(memory_space=pl.ANY), VMEM, SMEM, pl.BlockSpec(memory_space=pl.ANY)],
                out_specs=[VMEM] * 2,
                scratch_shapes=[
                    pltpu.VMEM((chunks, GROUP, planes, most, CHUNK), jnp.bfloat16),
                    pltpu.VMEM((CH * W, owners * most), jnp.bfloat16),
                    pltpu.VMEM((nfft, 2 * F), jnp.bfloat16),
                    pltpu.VMEM((CH * W, 2 * F), jnp.float32),
                    pltpu.VMEM((CH * W, 128), jnp.float32),
                    pltpu.VMEM((CH, width), jnp.bfloat16),
                    pltpu.VMEM((hops, CH, width), jnp.bfloat16),
                    pltpu.VMEM((hops, CH, width), jnp.bfloat16),
                    pltpu.SemaphoreType.DMA((chunks, planes)),
                    pltpu.SemaphoreType.DMA((chunks, planes)),
                    pltpu.SemaphoreType.DMA((chunks, GROUP, planes)),
                    pltpu.SemaphoreType.DMA((chunks, GROUP, planes)),
                    pltpu.SemaphoreType.DMA((chunks,)),
                    pltpu.SemaphoreType.DMA,
                    pltpu.SemaphoreType.DMA((PIECES,)),
                    pltpu.SemaphoreType.DMA((PIECES,)),
                    pltpu.SemaphoreType.DMA((hops, PIECES)),
                    pltpu.SemaphoreType.DMA((hops, PIECES)),
                ],
                compiler_params=pltpu.CompilerParams(
                    vmem_limit_bytes=limit, collective_id=number, has_side_effects=True
                ),
                name=f"deliver{number}",
            )(outgoing, goal, masks, table)

        return call

    sizes = capacities(most, chunks)
    calls = [deliver(number + 1, caps) for number, caps in enumerate(sizes)]
    own, other = lax.switch(
        level[0], calls, outgoing, goal, masks, jnp.asarray(forward_table(nfft, F))
    )
    step = 16
    return pl.pallas_call(
        functools.partial(correlate_kernel, last=last),
        grid=(CH // step,),
        out_shape=jax.ShapeDtypeStruct((rounds, CH, CH, LAGS), jnp.bfloat16),
        in_specs=[
            SMEM,
            pl.BlockSpec((1, step, width), lambda i: (i, 0, 0)),
            pl.BlockSpec((rounds * CH, width), lambda i: (0, 0)),
            pl.BlockSpec((LAGS, 2 * F), lambda i: (0, 0)),
        ],
        out_specs=pl.BlockSpec((rounds, step, CH, LAGS), lambda i: (0, i, 0, 0)),
        scratch_shapes=[pltpu.VMEM((4, 2 * LAGS, width), jnp.bfloat16)],
        compiler_params=pltpu.CompilerParams(vmem_limit_bytes=limit),
        name="correlate",
    )(
        masks,
        own.reshape(CH // step, step, width),
        other,
        jnp.asarray(lag_table(nfft, F, LAGS)),
    )


def solution(mesh):
    return jax.shard_map(
        local,
        mesh=mesh,
        in_specs=(
            P(("groups", "blk"), None),
            P(("groups", "blk"), None),
            P(("groups", "blk"), None),
            P(("groups", "blk"), None),
            P(),
        ),
        out_specs=P(None, ("groups", "blk"), None, None),
        check_vma=False,
    )
```

```python
import functools
import math

import jax
import jax.numpy as jnp
import numpy as np
from jax import lax
from jax.experimental import pallas as pl
from jax.experimental.pallas import tpu as pltpu
from jax.sharding import PartitionSpec as P

CH = 128
F = 256
LAGS = 128
W = 2
GROUP = 4
CHUNK = 256
AHEAD = 2
PIECES = 8
FLIGHT = 4
LAG = 3
GAP = 64.0
LEVELS = (
    (96, 96, 96, 80, 64, 64, 48, 32),
    (112, 112, 96, 80, 80, 64, 48, 32),
    (128, 128, 112, 96, 80, 64, 48, 32),
)
VMEM = pl.BlockSpec(memory_space=pltpu.VMEM)
SMEM = pl.BlockSpec(memory_space=pltpu.SMEM)
HBM = pl.BlockSpec(memory_space=pl.ANY)
MESH = pl.DeviceIdType.MESH


def forward_table(nfft, bins):
    sample = np.arange(nfft, dtype=np.int64)[:, None]
    freq = np.arange(1, bins + 1, dtype=np.int64)[None, :]
    angle = (sample * freq % nfft).astype(np.float32) * np.float32(2.0 * math.pi / nfft)
    return np.concatenate([np.cos(angle), -np.sin(angle)], axis=1).astype(jnp.bfloat16)


def lag_table(nfft, bins, lags):
    shift = (np.arange(lags, dtype=np.int64) - lags // 2) % nfft
    freq = np.arange(1, bins + 1, dtype=np.int64)[None, :]
    angle = (freq * shift[:, None] % nfft).astype(np.float32) * np.float32(2.0 * math.pi / nfft)
    return np.concatenate([np.cos(angle), -np.sin(angle)], axis=1).astype(jnp.bfloat16)


def met_at(me, distance, owners):
    other = me
    for k in range(owners.bit_length() - 1):
        if distance >> k & 1:
            other = other + (1 << k) * (1 - 2 * lax.rem(lax.div(me, 1 << k), 2))
    return other


def gathered_at(distance):
    bits = GROUP.bit_length() - 1
    return sum((distance >> k & 1) << (bits - 1 - k) for k in range(bits))


def capacities(most, chunks):
    found = []
    for level in LEVELS:
        rows = [-(-level[c * len(level) // chunks] * most // (128 * 16)) * 16 for c in range(chunks)]
        rows = tuple(min(most, max(16, r)) for r in rows)
        if rows not in found:
            found.append(rows)
    full = (most,) * chunks
    return [rows for rows in found if rows != full] + [full]


def plan_kernel(
    records_ref, dest_ref, slot_ref, valid_ref,
    outgoing_ref, first_ref, goal_ref, level_ref,
    outbox, inbox, levels, send_sem, recv_sem, level_sems, first_sems, own_sem,
):
    chunks, planes, most, wide = outgoing_ref.shape
    owners = planes * GROUP
    held = records_ref.shape[0]
    me, part = lax.axis_index("blk"), lax.axis_index("groups")
    parts = levels.shape[0]
    shift = most.bit_length() - 1
    plane = lax.div(me, GROUP)

    barrier = pltpu.get_barrier_semaphore()
    for distance in range(1, owners):
        pl.semaphore_signal(
            barrier, inc=1, device_id={"blk": met_at(me, distance, owners)}, device_id_type=MESH
        )
    abroad = [
        (turn, distance, {"groups": lax.rem(part + turn, parts), "blk": met_at(me, distance, owners)})
        for turn in range(1, parts)
        for distance in range(owners)
    ]
    for _, _, other in abroad:
        pl.semaphore_signal(barrier, inc=1, device_id=other, device_id_type=MESH)

    dest, slot, valid = dest_ref[...], slot_ref[...], valid_ref[...]
    group, within = lax.div(dest, GROUP), lax.rem(dest, GROUP)
    key = valid * held + (held - 1 - lax.broadcasted_iota(jnp.int32, (1, held), 1))
    line = lax.broadcasted_iota(jnp.int32, (8, held), 0)
    columns = jnp.where(line == 0, group, jnp.where(line == 1, key, valid)).astype(jnp.float32).T
    key, group_row = key.astype(jnp.float32), group.astype(jnp.float32)
    ahead = (columns[:, 1:2] > key) & (columns[:, 0:1] == group_row)
    rank = jnp.sum(ahead.astype(jnp.float32), axis=0, keepdims=True).astype(jnp.int32)
    reach = lax.div(valid - 1, wide)
    level = jnp.zeros((1, held), jnp.float32)
    for rows in capacities(most, chunks)[:-1]:
        limit = jnp.zeros((1, held), jnp.int32)
        for c in range(chunks):
            limit = jnp.where(reach == c, rows[c], limit)
        level = level + jnp.max((rank >= limit).astype(jnp.float32), axis=1, keepdims=True)
    levels[0, 0] = level[:, :128]

    lines = max(8, planes)
    named = lax.broadcasted_iota(jnp.int32, (lines, held), 0) == group
    ranked = (lax.broadcasted_iota(jnp.int32, (128, held), 0) == rank).astype(jnp.float32)
    ranked = ranked.astype(jnp.bfloat16)

    def spread(values):
        values = jnp.where(named, values, 0).astype(jnp.float32).astype(jnp.bfloat16)
        return lax.dot_general(
            values, ranked, (((1,), (1,)), ((), ())), preferred_element_type=jnp.float32
        )

    code = spread(within + 1) * 256.0 + spread(slot)
    for p in range(planes):
        outbox[p, 0:1, :] = code[p : p + 1]
        outbox[p, 1:2, :] = level[:, :128]

    spots = planes * most
    place = lax.broadcasted_iota(jnp.int32, (spots, held), 0) == group * most + rank
    place = place.astype(jnp.float32).astype(jnp.bfloat16)
    ends = columns[:, 2:3].astype(jnp.int32)

    def pack(c):
        window = lax.broadcasted_iota(jnp.int32, (held, wide), 1) + c * wide < ends
        window = window.astype(jnp.float32).astype(jnp.bfloat16)
        data = records_ref[:, c * wide : (c + 1) * wide] * window + (GAP - GAP * window)
        packed = jnp.dot(place, data, preferred_element_type=jnp.float32)
        outgoing_ref[c] = packed.astype(jnp.bfloat16).reshape(planes, most, wide)

    pack(0)
    pl.semaphore_wait(barrier, owners * parts - 1)
    copies = []
    for turn, distance, other in abroad:
        copies.append(
            pltpu.make_async_remote_copy(
                src_ref=levels.at[0, 0],
                dst_ref=levels.at[turn, distance],
                send_sem=level_sems.at[0, turn, distance],
                recv_sem=level_sems.at[1, turn, distance],
                device_id=other,
                device_id_type=MESH,
            )
        )
        copies[-1].start()
    for distance in range(owners - 1, 0, -1):
        other = met_at(me, distance, owners)
        copies.append(
            pltpu.make_async_remote_copy(
                src_ref=outbox.at[lax.div(other, GROUP)],
                dst_ref=inbox.at[gathered_at(distance % GROUP) * planes + plane],
                send_sem=send_sem.at[distance],
                recv_sem=recv_sem.at[distance],
                device_id={"blk": other},
                device_id_type=MESH,
            )
        )
        copies[-1].start()
    for d in range(planes - 1, 0, -1):
        other = met_at(me, GROUP * d, owners)
        copies.append(
            pltpu.make_async_remote_copy(
                src_ref=outgoing_ref.at[0, lax.div(other, GROUP)],
                dst_ref=first_ref.at[plane],
                send_sem=first_sems.at[0, d],
                recv_sem=first_sems.at[1, d],
                device_id={"blk": other},
                device_id_type=MESH,
            )
        )
        copies[-1].start()
    copies.append(pltpu.make_async_copy(outgoing_ref.at[0, plane], first_ref.at[plane], own_sem))
    copies[-1].start()
    inbox[plane] = outbox[plane]

    for c in range(1, chunks):
        pack(c)

    kept = owners * most
    at = lax.broadcasted_iota(jnp.int32, (128, kept), 1)
    sown = lax.broadcasted_iota(jnp.int32, (128, kept), 0) == at - (at >> shift << shift)
    sown = sown.astype(jnp.float32).astype(jnp.bfloat16)
    for copy in copies[:-planes]:
        copy.wait()
    code = inbox[:, 0, :]
    level = jnp.max(inbox[:, 1, :], axis=0, keepdims=True)
    for turn, distance, _ in abroad:
        level = jnp.maximum(level, levels[turn, distance])
    level_ref[0] = jnp.max(level).astype(jnp.int32)
    owner = (code * (1.0 / 256.0)).astype(jnp.int32).astype(jnp.float32)
    slots = code - owner * 256.0
    at = lax.broadcasted_iota(jnp.int32, (owners, kept), 1)
    mine = lax.broadcasted_iota(jnp.int32, (owners, kept), 0) == at >> shift

    def line_up(values):
        values = jnp.dot(values.astype(jnp.bfloat16), sown, preferred_element_type=jnp.float32)
        return jnp.sum(jnp.where(mine, values, 0.0), axis=0, keepdims=True).astype(jnp.int32)

    slots = line_up(slots)
    goal = (slots & (W - 1)) * CH + (slots >> (W.bit_length() - 1))
    goal_ref[...] = jnp.where(line_up(owner) == lax.rem(me, GROUP) + 1, goal, -1)
    for copy in copies[-planes:]:
        copy.wait()


def deliver_kernel(
    caps, outgoing_ref, first_ref, goal_ref, masks_ref, table_hbm,
    own_ref, met_ref,
    arrived, select, table, spectrum, energy, tile, leaving, landing,
    plane_send, plane_recv, gather_send, gather_recv, own_sem, table_sem,
    far_send, far_recv, hop_send, hop_recv,
):
    chunks, _, planes, most, wide = arrived.shape
    owners = planes * GROUP
    nfft = chunks * wide
    kept = owners * most
    me = lax.axis_index("blk")
    plane = lax.div(me, GROUP)
    last = owners - 1
    bits = list(range(owners.bit_length() - 3, -1, -1))
    steps = list(range(GROUP.bit_length() - 2, -1, -1))
    depth = len(steps)

    barrier = pltpu.get_barrier_semaphore()
    peers = {GROUP * d for d in range(1, planes)} | {1 << k for k in steps + bits} | {last}
    for distance in sorted(peers):
        pl.semaphore_signal(
            barrier, inc=1, device_id={"blk": met_at(me, distance, owners)}, device_id_type=MESH
        )
    fetch = pltpu.make_async_copy(table_hbm, table, table_sem)
    fetch.start()
    pl.semaphore_wait(barrier, len(peers))

    def send(distance, source, target, send_sem, recv_sem):
        copy = pltpu.make_async_remote_copy(
            src_ref=source,
            dst_ref=target,
            send_sem=send_sem,
            recv_sem=recv_sem,
            device_id={"blk": met_at(me, distance, owners)},
            device_id_type=MESH,
        )
        copy.start()
        return copy

    sent, local, gathers = {}, {}, {}

    def begin(c):
        rows = pl.ds(0, caps[c])
        for d in range(planes - 1, 0, -1):
            other = lax.div(met_at(me, GROUP * d, owners), GROUP)
            sent[c, d] = send(
                GROUP * d,
                outgoing_ref.at[c, other, rows],
                arrived.at[c, 0, plane, rows],
                plane_send.at[c, d],
                plane_recv.at[c, d],
            )
        local[c] = pltpu.make_async_copy(
            outgoing_ref.at[c, plane, rows], arrived.at[c, 0, plane, rows], own_sem.at[c]
        )
        local[c].start()

    def forward_first():
        rows = pl.ds(0, caps[0])
        local[0] = pltpu.make_async_copy(
            first_ref.at[:, rows], arrived.at[0, 0, :, rows], own_sem.at[0]
        )
        for step in range(depth):
            gathers[0, step, 0] = send(
                1 << steps[step],
                first_ref.at[:, rows],
                arrived.at[0, 1 << step, :, rows],
                gather_send.at[0, step, 0],
                gather_recv.at[0, step, 0],
            )
        local[0].start()

    def forward(c, step, part):
        low, count = (0, 1) if part == 0 else (1 << (part - 1), 1 << (part - 1))
        rows = pl.ds(0, caps[c])
        gathers[c, step, part] = send(
            1 << steps[step],
            arrived.at[c, pl.ds(low, count), :, rows],
            arrived.at[c, pl.ds(low + (1 << step), count), :, rows],
            gather_send.at[c, step, part],
            gather_recv.at[c, step, part],
        )

    ahead = min(AHEAD, chunks - 1)
    forward_first()
    for c in range(1, 1 + ahead):
        begin(c)
    for c in range(chunks):
        if caps[c] < most:
            rest = arrived.at[c, :, :, caps[c] :, :]
            rest[...] = jnp.full(rest.shape, GAP, jnp.bfloat16)
    goal = goal_ref[...]
    width = min(512, kept)
    for base in range(0, kept, width):
        chosen = lax.broadcasted_iota(jnp.int32, (CH * W, width), 0) == goal[:, base : base + width]
        select[:, base : base + width] = chosen.astype(jnp.float32).astype(jnp.bfloat16)

    def compute(c):
        data = arrived[c].reshape(kept, wide)
        window = jnp.minimum(jnp.maximum(GAP / 2 - data, 0.0), 1.0)
        total = jnp.dot(select[...], data * window, preferred_element_type=jnp.float32)
        count = jnp.dot(select[...], window, preferred_element_type=jnp.float32)
        trace = total / jnp.maximum(count, 1.0)
        squares = trace * trace
        squares = sum(squares[:, k : k + 128] for k in range(0, wide, 128))
        part = jnp.dot(
            trace.astype(jnp.bfloat16),
            table[c * wide : (c + 1) * wide, :],
            preferred_element_type=jnp.float32,
        )
        if c == 0:
            energy[...], spectrum[...] = squares, part
        else:
            energy[...] += squares
            spectrum[...] += part

    for turn in range(1, chunks + depth + 1):
        for stage in range(depth + 2):
            c = turn - stage
            if not 0 <= c < chunks:
                continue
            if stage == 0:
                if c + ahead < chunks:
                    begin(c + ahead)
                for d in range(planes - 1, 0, -1):
                    sent[c, d].wait_recv()
                local[c].wait()
                for step in range(depth):
                    forward(c, step, 0)
            elif stage <= depth:
                for part in range(stage):
                    gathers[c, stage - 1, part].wait_recv()
                for step in range(stage, depth):
                    forward(c, step, stage)
            else:
                if c == 0:
                    fetch.wait()
                    local[0].wait()
                compute(c)

    second = masks_ref[0] ^ masks_ref[1] ^ last
    use_far = lax.div(second, 1 << (len(bits)))
    path = second + use_far * (last - 2 * second)
    size = CH // PIECES

    def choose(flag, yes, no):
        flag = jnp.full(yes.shape, flag.astype(jnp.float32), jnp.float32).astype(jnp.bfloat16)
        return yes * flag + no * (1 - flag)

    factor = lax.rsqrt(jnp.sum(energy[...], axis=1, keepdims=True) * (1.0 / nfft) + 1e-06)
    far = []

    def far_copy(q):
        rows = pl.ds(q * size, size)
        far.append(send(last, tile.at[rows], met_ref.at[rows], far_send.at[q], far_recv.at[q]))

    for q in range(PIECES):
        rows = slice(q * size, (q + 1) * size)
        for w in range(W):
            at = slice(w * CH + q * size, w * CH + (q + 1) * size)
            parts = spectrum[at, :] * factor[at]
            real_part, imag_part = parts[:, :F], parts[:, F:]
            amplitude = lax.rsqrt(
                jnp.maximum(real_part * real_part + imag_part * imag_part, nfft / 4.0)
            )
            real_part = (real_part * amplitude).astype(jnp.bfloat16)
            imag_part = (imag_part * amplitude).astype(jnp.bfloat16)
            base = 2 * F * w
            tile[rows, base : base + F] = real_part
            tile[rows, base + F : base + 2 * F] = imag_part
            own_ref[rows, base : base + F] = real_part.astype(jnp.float32)
            own_ref[rows, base + F : base + 2 * F] = imag_part.astype(jnp.float32)
        if q < FLIGHT:
            far_copy(q)

    hops = {}
    for turn in range(PIECES + LAG * len(bits)):
        for stage in range(len(bits) + 1):
            q = turn - LAG * stage
            if not 0 <= q < PIECES:
                continue
            rows = slice(q * size, (q + 1) * size)
            if stage == 0:
                far[q].wait_recv()
                if q + FLIGHT < PIECES:
                    far_copy(q + FLIGHT)
                value = choose(use_far, met_ref[rows], tile[rows])
            else:
                hops[stage - 1, q].wait_recv()
                taken = lax.rem(lax.div(path, 1 << bits[stage - 1]), 2)
                value = choose(taken, landing[stage - 1, rows], leaving[stage - 1, rows])
            if stage == len(bits):
                met_ref[CH + q * size : CH + (q + 1) * size] = value
            else:
                leaving[stage, rows] = value
                spot = pl.ds(q * size, size)
                hops[stage, q] = send(
                    1 << bits[stage],
                    leaving.at[stage, spot],
                    landing.at[stage, spot],
                    hop_send.at[stage, q],
                    hop_recv.at[stage, q],
                )
    for copy in list(sent.values()) + list(gathers.values()) + far + list(hops.values()):
        copy.wait_send()


def correlate_kernel(masks_ref, own_ref, other_ref, table_ref, out_ref, turned, *, last):
    scale = 1.0 / math.sqrt(W * F)
    cosine, sine = table_ref[:, :F], table_ref[:, F:]
    far_round = (masks_ref[0] != last).astype(jnp.int32)
    slots, step = turned.shape[0], own_ref.shape[1]

    for index in range(step // 2):
        at = index % slots
        for half in range(2):
            mine = own_ref[0, index * 2 + half : index * 2 + half + 1, :].astype(jnp.bfloat16)
            rows = slice(half * LAGS, (half + 1) * LAGS)
            for w in range(W):
                base = 2 * F * w
                ur, ui = mine[:, base : base + F], mine[:, base + F : base + 2 * F]
                turned[at, rows, base : base + F] = cosine * ur + sine * ui
                turned[at, rows, base + F : base + 2 * F] = cosine * ui - sine * ur
        product = lax.dot_general(
            other_ref[...],
            turned[at],
            (((1,), (1,)), ((), ())),
            preferred_element_type=jnp.float32,
        )
        product = (product * scale).astype(jnp.bfloat16)
        for half in range(2):
            lags = slice(half * LAGS, (half + 1) * LAGS)
            out_ref[far_round, index * 2 + half] = product[:CH, lags]
            out_ref[1 - far_round, index * 2 + half] = product[CH:, lags]


def local(records, dest, slot, valid, masks):
    owners, parts = lax.axis_size("blk"), lax.axis_size("groups")
    held, nfft = records.shape
    rounds = masks.shape[0]
    planes, chunks = owners // GROUP, nfft // CHUNK
    most = max(16, GROUP * 2 * held // owners)
    width = 2 * F * W
    limit = 56 * 2**20
    outgoing, first, goal, level = pl.pallas_call(
        plan_kernel,
        out_shape=[
            jax.ShapeDtypeStruct((chunks, planes, most, CHUNK), jnp.bfloat16),
            jax.ShapeDtypeStruct((planes, most, CHUNK), jnp.bfloat16),
            jax.ShapeDtypeStruct((1, owners * most), jnp.int32),
            jax.ShapeDtypeStruct((1,), jnp.int32),
        ],
        in_specs=[VMEM] * 4,
        out_specs=[VMEM, VMEM, VMEM, SMEM],
        scratch_shapes=[
            pltpu.VMEM((planes, 2, 128), jnp.float32),
            pltpu.VMEM((owners, 2, 128), jnp.float32),
            pltpu.VMEM((parts, owners, 1, 128), jnp.float32),
            pltpu.SemaphoreType.DMA((owners,)),
            pltpu.SemaphoreType.DMA((owners,)),
            pltpu.SemaphoreType.DMA((2, parts, owners)),
            pltpu.SemaphoreType.DMA((2, planes)),
            pltpu.SemaphoreType.DMA,
        ],
        compiler_params=pltpu.CompilerParams(
            vmem_limit_bytes=limit, collective_id=0, has_side_effects=True
        ),
        name="plan",
    )(records, dest.reshape(1, held), slot.reshape(1, held), valid.reshape(1, held))

    last = owners - 1
    hops = owners.bit_length() - 2
    depth = GROUP.bit_length() - 1

    def deliver(number, caps):
        def call(outgoing, first, goal, masks, table):
            return pl.pallas_call(
                functools.partial(deliver_kernel, caps),
                out_shape=[
                    jax.ShapeDtypeStruct((CH, width), jnp.float32),
                    jax.ShapeDtypeStruct((rounds * CH, width), jnp.bfloat16),
                ],
                in_specs=[HBM, HBM, VMEM, SMEM, HBM],
                out_specs=[VMEM] * 2,
                scratch_shapes=[
                    pltpu.VMEM((chunks, GROUP, planes, most, CHUNK), jnp.bfloat16),
                    pltpu.VMEM((CH * W, owners * most), jnp.bfloat16),
                    pltpu.VMEM((nfft, 2 * F), jnp.bfloat16),
                    pltpu.VMEM((CH * W, 2 * F), jnp.float32),
                    pltpu.VMEM((CH * W, 128), jnp.float32),
                    pltpu.VMEM((CH, width), jnp.bfloat16),
                    pltpu.VMEM((hops, CH, width), jnp.bfloat16),
                    pltpu.VMEM((hops, CH, width), jnp.bfloat16),
                    pltpu.SemaphoreType.DMA((chunks, planes)),
                    pltpu.SemaphoreType.DMA((chunks, planes)),
                    pltpu.SemaphoreType.DMA((chunks, depth, depth)),
                    pltpu.SemaphoreType.DMA((chunks, depth, depth)),
                    pltpu.SemaphoreType.DMA((chunks,)),
                    pltpu.SemaphoreType.DMA,
                    pltpu.SemaphoreType.DMA((PIECES,)),
                    pltpu.SemaphoreType.DMA((PIECES,)),
                    pltpu.SemaphoreType.DMA((hops, PIECES)),
                    pltpu.SemaphoreType.DMA((hops, PIECES)),
                ],
                compiler_params=pltpu.CompilerParams(
                    vmem_limit_bytes=limit, collective_id=number, has_side_effects=True
                ),
                name=f"deliver{number}",
            )(outgoing, first, goal, masks, table)

        return call

    sizes = capacities(most, chunks)
    calls = [deliver(number + 1, caps) for number, caps in enumerate(sizes)]
    own, other = lax.switch(
        level[0], calls, outgoing, first, goal, masks, jnp.asarray(forward_table(nfft, F))
    )
    step = 32
    return pl.pallas_call(
        functools.partial(correlate_kernel, last=last),
        grid=(CH // step,),
        out_shape=jax.ShapeDtypeStruct((rounds, CH, CH, LAGS), jnp.bfloat16),
        in_specs=[
            SMEM,
            pl.BlockSpec((1, step, width), lambda i: (i, 0, 0)),
            pl.BlockSpec((rounds * CH, width), lambda i: (0, 0)),
            pl.BlockSpec((LAGS, 2 * F), lambda i: (0, 0)),
        ],
        out_specs=pl.BlockSpec((rounds, step, CH, LAGS), lambda i: (0, i, 0, 0)),
        scratch_shapes=[pltpu.VMEM((4, 2 * LAGS, width), jnp.bfloat16)],
        compiler_params=pltpu.CompilerParams(vmem_limit_bytes=limit),
        name="correlate",
    )(
        masks,
        own.reshape(CH // step, step, width),
        other,
        jnp.asarray(lag_table(nfft, F, LAGS)),
    )


def solution(mesh):
    return jax.shard_map(
        local,
        mesh=mesh,
        in_specs=(
            P(("groups", "blk"), None),
            P(("groups", "blk"), None),
            P(("groups", "blk"), None),
            P(("groups", "blk"), None),
            P(),
        ),
        out_specs=P(None, ("groups", "blk"), None, None),
        check_vma=False,
    )
```

```python
import functools
import math

import jax
import jax.numpy as jnp
import numpy as np
from jax import lax
from jax.experimental import pallas as pl
from jax.experimental.pallas import tpu as pltpu
from jax.sharding import PartitionSpec as P

CH = 128
F = 256
LAGS = 128
W = 2
GROUP = 4
CHUNK = 256
AHEAD = 2
PIECES = 8
FLIGHT = 4
LAG = 3
GAP = 64.0
LEVELS = (
    ((96, 96, 96, 80, 64, 64, 48, 32), (64, 64, 64, 64, 48, 48, 32, 16)),
    ((112, 112, 96, 80, 80, 64, 48, 32), (64, 64, 64, 64, 48, 48, 32, 32)),
    ((128, 128, 112, 96, 80, 64, 64, 48), (64, 64, 64, 64, 64, 48, 48, 32)),
)
VMEM = pl.BlockSpec(memory_space=pltpu.VMEM)
SMEM = pl.BlockSpec(memory_space=pltpu.SMEM)
HBM = pl.BlockSpec(memory_space=pl.ANY)
MESH = pl.DeviceIdType.MESH


def forward_table(nfft, bins):
    sample = np.arange(nfft, dtype=np.int64)[:, None]
    freq = np.arange(1, bins + 1, dtype=np.int64)[None, :]
    angle = (sample * freq % nfft).astype(np.float32) * np.float32(2.0 * math.pi / nfft)
    return np.concatenate([np.cos(angle), -np.sin(angle)], axis=1).astype(jnp.bfloat16)


def lag_table(nfft, bins, lags):
    shift = (np.arange(lags, dtype=np.int64) - lags // 2) % nfft
    freq = np.arange(1, bins + 1, dtype=np.int64)[None, :]
    angle = (freq * shift[:, None] % nfft).astype(np.float32) * np.float32(2.0 * math.pi / nfft)
    return np.concatenate([np.cos(angle), -np.sin(angle)], axis=1).astype(jnp.bfloat16)


def met_at(me, distance, owners):
    other = me
    for k in range(owners.bit_length() - 1):
        if distance >> k & 1:
            other = other + (1 << k) * (1 - 2 * lax.rem(lax.div(me, 1 << k), 2))
    return other


def gathered_at(distance):
    bits = GROUP.bit_length() - 1
    return sum((distance >> k & 1) << (bits - 1 - k) for k in range(bits))


def split_at(planes, most):
    return planes == 4 and most >= 32


def capacities(most, chunks):
    def scaled(level, bound, unit):
        rows = [-(-level[c * len(level) // chunks] * bound // (unit * 16)) * 16 for c in range(chunks)]
        return tuple(min(bound, max(16, r)) for r in rows)

    full = ((most,) * chunks, (most // 2,) * chunks)
    found = []
    for far, near in LEVELS:
        rows = (scaled(far, most, 128), scaled(near, most // 2, 64))
        if rows not in found and rows[0] != full[0]:
            found.append(rows)
    return found + [full]


def first_sends(planes, split):
    if not split:
        return [(d, 0, False) for d in range(planes - 1, -1, -1)]
    other = GROUP // 2
    return [(3, 0, False), (2, 0, False), (1, 0, True), (1, other, True), (0, other, True), (0, 0, True)]


def plan_kernel(
    records_ref, dest_ref, slot_ref, valid_ref,
    outgoing_ref, first_ref, goal_ref, level_ref,
    outbox, inbox, levels, send_sem, recv_sem, level_sems, first_sems, own_sem,
):
    chunks, planes, most, wide = outgoing_ref.shape
    owners = planes * GROUP
    held = records_ref.shape[0]
    me, part = lax.axis_index("blk"), lax.axis_index("groups")
    parts = levels.shape[0]
    shift = most.bit_length() - 1
    plane = lax.div(me, GROUP)

    barrier = pltpu.get_barrier_semaphore()
    for distance in range(1, owners):
        pl.semaphore_signal(
            barrier, inc=1, device_id={"blk": met_at(me, distance, owners)}, device_id_type=MESH
        )
    abroad = [
        (turn, distance, {"groups": lax.rem(part + turn, parts), "blk": met_at(me, distance, owners)})
        for turn in range(1, parts)
        for distance in range(owners)
    ]
    for _, _, other in abroad:
        pl.semaphore_signal(barrier, inc=1, device_id=other, device_id_type=MESH)

    dest, slot, valid = dest_ref[...], slot_ref[...], valid_ref[...]
    group, within = lax.div(dest, GROUP), lax.rem(dest, GROUP)
    key = valid * held + (held - 1 - lax.broadcasted_iota(jnp.int32, (1, held), 1))
    line = lax.broadcasted_iota(jnp.int32, (8, held), 0)
    split = split_at(planes, most)
    half = most // 2
    chip = lax.div(within, GROUP // 2)
    if split:
        near = (group >> 1) == lax.div(plane, 2)
    else:
        near = group < 0
    kind = group * 4 + jnp.where(near, 1 + chip, 0)
    columns = jnp.where(line == 0, kind, jnp.where(line == 1, key, valid)).astype(jnp.float32).T
    key, kind = key.astype(jnp.float32), kind.astype(jnp.float32)
    ahead = (columns[:, 1:2] > key) & (columns[:, 0:1] == kind)
    rank = jnp.sum(ahead.astype(jnp.float32), axis=0, keepdims=True).astype(jnp.int32)
    reach = lax.div(valid - 1, wide)
    level = jnp.zeros((1, held), jnp.float32)
    for far_rows, near_rows in capacities(most, chunks)[:-1]:
        limit = jnp.zeros((1, held), jnp.int32)
        for c in range(chunks):
            limit = jnp.where(reach == c, jnp.where(near, near_rows[c], far_rows[c]), limit)
        level = level + jnp.max((rank >= limit).astype(jnp.float32), axis=1, keepdims=True)
    levels[0, 0] = level[:, :128]
    rank = rank + jnp.where(near, chip * half, 0)

    lines = max(8, planes)
    named = lax.broadcasted_iota(jnp.int32, (lines, held), 0) == group
    ranked = (lax.broadcasted_iota(jnp.int32, (128, held), 0) == rank).astype(jnp.float32)
    ranked = ranked.astype(jnp.bfloat16)

    def spread(values):
        values = jnp.where(named, values, 0).astype(jnp.float32).astype(jnp.bfloat16)
        return lax.dot_general(
            values, ranked, (((1,), (1,)), ((), ())), preferred_element_type=jnp.float32
        )

    code = spread(within + 1) * 256.0 + spread(slot)
    for p in range(planes):
        outbox[p, 0:1, :] = code[p : p + 1]
        outbox[p, 1:2, :] = level[:, :128]

    spots = planes * most
    place = lax.broadcasted_iota(jnp.int32, (spots, held), 0) == group * most + rank
    place = place.astype(jnp.float32).astype(jnp.bfloat16)
    ends = columns[:, 2:3].astype(jnp.int32)

    def pack(c):
        window = lax.broadcasted_iota(jnp.int32, (held, wide), 1) + c * wide < ends
        window = window.astype(jnp.float32).astype(jnp.bfloat16)
        data = records_ref[:, c * wide : (c + 1) * wide] * window + (GAP - GAP * window)
        packed = jnp.dot(place, data, preferred_element_type=jnp.float32)
        outgoing_ref[c] = packed.astype(jnp.bfloat16).reshape(planes, most, wide)

    pack(0)
    pl.semaphore_wait(barrier, owners * parts - 1)
    copies = []
    for turn, distance, other in abroad:
        copies.append(
            pltpu.make_async_remote_copy(
                src_ref=levels.at[0, 0],
                dst_ref=levels.at[turn, distance],
                send_sem=level_sems.at[0, turn, distance],
                recv_sem=level_sems.at[1, turn, distance],
                device_id=other,
                device_id_type=MESH,
            )
        )
        copies[-1].start()
    for distance in range(owners - 1, 0, -1):
        other = met_at(me, distance, owners)
        copies.append(
            pltpu.make_async_remote_copy(
                src_ref=outbox.at[lax.div(other, GROUP)],
                dst_ref=inbox.at[gathered_at(distance % GROUP) * planes + plane],
                send_sem=send_sem.at[distance],
                recv_sem=recv_sem.at[distance],
                device_id={"blk": other},
                device_id_type=MESH,
            )
        )
        copies[-1].start()
    row = lax.rem(lax.div(me, GROUP // 2), 2)
    first = []
    for index, (d, turned, near) in enumerate(first_sends(planes, split)):
        other = met_at(me, GROUP * d + turned, owners)
        rows = pl.ds(0, most)
        if near:
            at = row if turned == 0 else 1 - row
            rows = pl.ds(pl.multiple_of(at * half, 16), half)
        source = outgoing_ref.at[0, lax.div(other, GROUP), rows]
        target = first_ref.at[1 if turned else 0, plane, rows]
        if d == 0 and turned == 0:
            first.append(pltpu.make_async_copy(source, target, own_sem))
        else:
            first.append(
                pltpu.make_async_remote_copy(
                    src_ref=source,
                    dst_ref=target,
                    send_sem=first_sems.at[0, index],
                    recv_sem=first_sems.at[1, index],
                    device_id={"blk": other},
                    device_id_type=MESH,
                )
            )
        first[-1].start()
    inbox[plane] = outbox[plane]

    for c in range(1, chunks):
        pack(c)

    kept = owners * most
    at = lax.broadcasted_iota(jnp.int32, (128, kept), 1)
    sown = lax.broadcasted_iota(jnp.int32, (128, kept), 0) == at - (at >> shift << shift)
    sown = sown.astype(jnp.float32).astype(jnp.bfloat16)
    for copy in copies:
        copy.wait()
    code = inbox[:, 0, :]
    level = jnp.max(inbox[:, 1, :], axis=0, keepdims=True)
    for turn, distance, _ in abroad:
        level = jnp.maximum(level, levels[turn, distance])
    level_ref[0] = jnp.max(level).astype(jnp.int32)
    owner = (code * (1.0 / 256.0)).astype(jnp.int32).astype(jnp.float32)
    slots = code - owner * 256.0
    at = lax.broadcasted_iota(jnp.int32, (owners, kept), 1)
    mine = lax.broadcasted_iota(jnp.int32, (owners, kept), 0) == at >> shift

    def line_up(values):
        values = jnp.dot(values.astype(jnp.bfloat16), sown, preferred_element_type=jnp.float32)
        return jnp.sum(jnp.where(mine, values, 0.0), axis=0, keepdims=True).astype(jnp.int32)

    slots = line_up(slots)
    goal = (slots & (W - 1)) * CH + (slots >> (W.bit_length() - 1))
    goal_ref[...] = jnp.where(line_up(owner) == lax.rem(me, GROUP) + 1, goal, -1)
    for copy in first:
        copy.wait()


def deliver_kernel(
    caps, outgoing_ref, first_ref, goal_ref, masks_ref, table_hbm,
    own_ref, met_ref,
    arrived, select, table, spectrum, energy, tile, leaving, landing,
    plane_send, plane_recv, gather_send, gather_recv, own_sem, table_sem,
    far_send, far_recv, hop_send, hop_recv,
):
    chunks, _, planes, most, wide = arrived.shape
    owners = planes * GROUP
    nfft = chunks * wide
    kept = owners * most
    me = lax.axis_index("blk")
    plane = lax.div(me, GROUP)
    last = owners - 1
    bits = list(range(owners.bit_length() - 3, -1, -1))
    split = split_at(planes, most)
    half = most // 2
    row = lax.rem(lax.div(me, GROUP // 2), 2)
    near_base = lax.div(plane, 2) * 2
    far_planes = pl.ds(2 - near_base, 2) if split else pl.ds(0, planes)
    near_planes = pl.ds(near_base, 2)

    barrier = pltpu.get_barrier_semaphore()
    sends = first_sends(planes, split)
    peers = {GROUP * d + turned for d, turned, _ in sends} - {0}
    peers |= {GROUP // 2, 1} | {1 << k for k in bits} | {last}
    for distance in sorted(peers):
        pl.semaphore_signal(
            barrier, inc=1, device_id={"blk": met_at(me, distance, owners)}, device_id_type=MESH
        )
    fetch = pltpu.make_async_copy(table_hbm, table, table_sem)
    fetch.start()
    pl.semaphore_wait(barrier, len(peers))

    def send(distance, source, target, send_sem, recv_sem):
        copy = pltpu.make_async_remote_copy(
            src_ref=source,
            dst_ref=target,
            send_sem=send_sem,
            recv_sem=recv_sem,
            device_id={"blk": met_at(me, distance, owners)},
            device_id_type=MESH,
        )
        copy.start()
        return copy

    sent, local, gathers = {}, {}, {}

    def some(at, count):
        return pl.ds(pl.multiple_of(at * half, 16), count)

    def begin(c):
        for index, (d, turned, near) in enumerate(sends):
            other = lax.div(met_at(me, GROUP * d + turned, owners), GROUP)
            rows = pl.ds(0, caps[0][c])
            if near:
                rows = some(row if turned == 0 else 1 - row, caps[1][c])
            source = outgoing_ref.at[c, other, rows]
            target = arrived.at[c, 1 if turned else 0, plane, rows]
            if d == 0 and turned == 0:
                sent[c, index] = pltpu.make_async_copy(source, target, own_sem.at[c])
                sent[c, index].start()
            else:
                sent[c, index] = send(
                    GROUP * d + turned, source, target, plane_send.at[c, index], plane_recv.at[c, index]
                )

    def region(c, near):
        if near:
            return near_planes, some(row, caps[1][c])
        return far_planes, pl.ds(0, caps[0][c])

    def forward(c, which, early=False):
        planes_at, rows = region(c, which in (2, 4))
        held_at = 1 if which in (3, 4) else 0
        source = first_ref if early else arrived.at[c]
        gathers[c, which] = send(
            GROUP // 2 if which == 0 else 1,
            source.at[held_at, planes_at, rows],
            arrived.at[c, held_at + (1 if which == 0 else 2), planes_at, rows],
            gather_send.at[c, which],
            gather_recv.at[c, which],
        )

    def forward_first():
        forward(0, 0, True)
        forward(0, 1, True)
        for index, (held_at, near) in enumerate([(0, False), (0, True), (1, True)]):
            if near and not split:
                continue
            planes_at, rows = region(0, near)
            local[index] = pltpu.make_async_copy(
                first_ref.at[held_at, planes_at, rows],
                arrived.at[0, held_at, planes_at, rows],
                own_sem.at[chunks + index],
            )
            local[index].start()
            if near:
                forward(0, 2 * held_at + 2, True)

    ahead = min(AHEAD, chunks - 1)
    forward_first()
    for c in range(1, 1 + ahead):
        begin(c)
    def blank(c, planes_at, rows):
        rest = arrived.at[c, :, planes_at, rows, :]
        rest[...] = jnp.full(rest.shape, GAP, jnp.bfloat16)

    for c in range(chunks):
        if caps[0][c] < most:
            blank(c, far_planes, pl.ds(caps[0][c], most - caps[0][c]))
        if split:
            blank(c, near_planes, some(1 - row, half))
            if caps[1][c] < half:
                start = pl.multiple_of(row * half + caps[1][c], 16)
                blank(c, near_planes, pl.ds(start, half - caps[1][c]))
    goal = goal_ref[...]
    width = min(512, kept)
    for base in range(0, kept, width):
        chosen = lax.broadcasted_iota(jnp.int32, (CH * W, width), 0) == goal[:, base : base + width]
        select[:, base : base + width] = chosen.astype(jnp.float32).astype(jnp.bfloat16)

    def compute(c):
        data = arrived[c].reshape(kept, wide)
        window = jnp.minimum(jnp.maximum(GAP / 2 - data, 0.0), 1.0)
        total = jnp.dot(select[...], data * window, preferred_element_type=jnp.float32)
        count = jnp.dot(select[...], window, preferred_element_type=jnp.float32)
        trace = total / jnp.maximum(count, 1.0)
        squares = trace * trace
        squares = sum(squares[:, k : k + 128] for k in range(0, wide, 128))
        part = jnp.dot(
            trace.astype(jnp.bfloat16),
            table[c * wide : (c + 1) * wide, :],
            preferred_element_type=jnp.float32,
        )
        if c == 0:
            energy[...], spectrum[...] = squares, part
        else:
            energy[...] += squares
            spectrum[...] += part

    for turn in range(1, chunks + 3):
        for stage in range(4):
            c = turn - stage
            if not 0 <= c < chunks:
                continue
            if stage == 0:
                if c + ahead < chunks:
                    begin(c + ahead)
                for index, (_, _, near) in enumerate(sends):
                    if not near:
                        (sent[c, index].wait_recv if sends[index][:2] != (0, 0) else sent[c, index].wait)()
                forward(c, 0)
                forward(c, 1)
                for index, (d, turned, near) in enumerate(sends):
                    if near:
                        (sent[c, index].wait_recv if d + turned else sent[c, index].wait)()
                if split:
                    forward(c, 2)
                    forward(c, 4)
            elif stage == 1:
                gathers[c, 0].wait_recv()
                forward(c, 3)
            elif stage == 2:
                for which in range(1, 5):
                    if (c, which) in gathers:
                        gathers[c, which].wait_recv()
            else:
                if c == 0:
                    fetch.wait()
                    for copy in local.values():
                        copy.wait()
                compute(c)

    second = masks_ref[0] ^ masks_ref[1] ^ last
    use_far = lax.div(second, 1 << (len(bits)))
    path = second + use_far * (last - 2 * second)
    size = CH // PIECES

    def choose(flag, yes, no):
        flag = jnp.full(yes.shape, flag.astype(jnp.float32), jnp.float32).astype(jnp.bfloat16)
        return yes * flag + no * (1 - flag)

    factor = lax.rsqrt(jnp.sum(energy[...], axis=1, keepdims=True) * (1.0 / nfft) + 1e-06)
    far = []

    def far_copy(q):
        rows = pl.ds(q * size, size)
        far.append(send(last, tile.at[rows], met_ref.at[rows], far_send.at[q], far_recv.at[q]))

    for q in range(PIECES):
        rows = slice(q * size, (q + 1) * size)
        for w in range(W):
            at = slice(w * CH + q * size, w * CH + (q + 1) * size)
            parts = spectrum[at, :] * factor[at]
            real_part, imag_part = parts[:, :F], parts[:, F:]
            amplitude = lax.rsqrt(
                jnp.maximum(real_part * real_part + imag_part * imag_part, nfft / 4.0)
            )
            real_part = (real_part * amplitude).astype(jnp.bfloat16)
            imag_part = (imag_part * amplitude).astype(jnp.bfloat16)
            base = 2 * F * w
            tile[rows, base : base + F] = real_part
            tile[rows, base + F : base + 2 * F] = imag_part
            own_ref[rows, base : base + F] = real_part.astype(jnp.float32)
            own_ref[rows, base + F : base + 2 * F] = imag_part.astype(jnp.float32)
        if q < FLIGHT:
            far_copy(q)

    hops = {}
    for turn in range(PIECES + LAG * len(bits)):
        for stage in range(len(bits) + 1):
            q = turn - LAG * stage
            if not 0 <= q < PIECES:
                continue
            rows = slice(q * size, (q + 1) * size)
            if stage == 0:
                far[q].wait_recv()
                if q + FLIGHT < PIECES:
                    far_copy(q + FLIGHT)
                value = choose(use_far, met_ref[rows], tile[rows])
            else:
                hops[stage - 1, q].wait_recv()
                taken = lax.rem(lax.div(path, 1 << bits[stage - 1]), 2)
                value = choose(taken, landing[stage - 1, rows], leaving[stage - 1, rows])
            if stage == len(bits):
                met_ref[CH + q * size : CH + (q + 1) * size] = value
            else:
                leaving[stage, rows] = value
                spot = pl.ds(q * size, size)
                hops[stage, q] = send(
                    1 << bits[stage],
                    leaving.at[stage, spot],
                    landing.at[stage, spot],
                    hop_send.at[stage, q],
                    hop_recv.at[stage, q],
                )
    abroad = [copy for (_, index), copy in sent.items() if sends[index][:2] != (0, 0)]
    for copy in abroad + list(gathers.values()) + far + list(hops.values()):
        copy.wait_send()


def correlate_kernel(masks_ref, own_ref, other_ref, table_ref, out_ref, turned, *, last):
    scale = 1.0 / math.sqrt(W * F)
    cosine, sine = table_ref[:, :F], table_ref[:, F:]
    far_round = (masks_ref[0] != last).astype(jnp.int32)
    slots, step = turned.shape[0], own_ref.shape[1]

    for index in range(step // 2):
        at = index % slots
        for half in range(2):
            mine = own_ref[0, index * 2 + half : index * 2 + half + 1, :].astype(jnp.bfloat16)
            rows = slice(half * LAGS, (half + 1) * LAGS)
            for w in range(W):
                base = 2 * F * w
                ur, ui = mine[:, base : base + F], mine[:, base + F : base + 2 * F]
                turned[at, rows, base : base + F] = cosine * ur + sine * ui
                turned[at, rows, base + F : base + 2 * F] = cosine * ui - sine * ur
        product = lax.dot_general(
            other_ref[...],
            turned[at],
            (((1,), (1,)), ((), ())),
            preferred_element_type=jnp.float32,
        )
        product = (product * scale).astype(jnp.bfloat16)
        for half in range(2):
            lags = slice(half * LAGS, (half + 1) * LAGS)
            out_ref[far_round, index * 2 + half] = product[:CH, lags]
            out_ref[1 - far_round, index * 2 + half] = product[CH:, lags]


def local(records, dest, slot, valid, masks):
    owners, parts = lax.axis_size("blk"), lax.axis_size("groups")
    held, nfft = records.shape
    rounds = masks.shape[0]
    planes, chunks = owners // GROUP, nfft // CHUNK
    most = max(16, GROUP * 2 * held // owners)
    width = 2 * F * W
    limit = 56 * 2**20
    outgoing, first, goal, level = pl.pallas_call(
        plan_kernel,
        out_shape=[
            jax.ShapeDtypeStruct((chunks, planes, most, CHUNK), jnp.bfloat16),
            jax.ShapeDtypeStruct((2, planes, most, CHUNK), jnp.bfloat16),
            jax.ShapeDtypeStruct((1, owners * most), jnp.int32),
            jax.ShapeDtypeStruct((1,), jnp.int32),
        ],
        in_specs=[VMEM] * 4,
        out_specs=[VMEM, VMEM, VMEM, SMEM],
        scratch_shapes=[
            pltpu.VMEM((planes, 2, 128), jnp.float32),
            pltpu.VMEM((owners, 2, 128), jnp.float32),
            pltpu.VMEM((parts, owners, 1, 128), jnp.float32),
            pltpu.SemaphoreType.DMA((owners,)),
            pltpu.SemaphoreType.DMA((owners,)),
            pltpu.SemaphoreType.DMA((2, parts, owners)),
            pltpu.SemaphoreType.DMA((2, planes + 2)),
            pltpu.SemaphoreType.DMA,
        ],
        compiler_params=pltpu.CompilerParams(
            vmem_limit_bytes=limit, collective_id=0, has_side_effects=True
        ),
        name="plan",
    )(records, dest.reshape(1, held), slot.reshape(1, held), valid.reshape(1, held))

    last = owners - 1
    hops = owners.bit_length() - 2

    def deliver(number, caps):
        def call(outgoing, first, goal, masks, table):
            return pl.pallas_call(
                functools.partial(deliver_kernel, caps),
                out_shape=[
                    jax.ShapeDtypeStruct((CH, width), jnp.float32),
                    jax.ShapeDtypeStruct((rounds * CH, width), jnp.bfloat16),
                ],
                in_specs=[HBM, HBM, VMEM, SMEM, HBM],
                out_specs=[VMEM] * 2,
                scratch_shapes=[
                    pltpu.VMEM((chunks, GROUP, planes, most, CHUNK), jnp.bfloat16),
                    pltpu.VMEM((CH * W, owners * most), jnp.bfloat16),
                    pltpu.VMEM((nfft, 2 * F), jnp.bfloat16),
                    pltpu.VMEM((CH * W, 2 * F), jnp.float32),
                    pltpu.VMEM((CH * W, 128), jnp.float32),
                    pltpu.VMEM((CH, width), jnp.bfloat16),
                    pltpu.VMEM((hops, CH, width), jnp.bfloat16),
                    pltpu.VMEM((hops, CH, width), jnp.bfloat16),
                    pltpu.SemaphoreType.DMA((chunks, planes + 2)),
                    pltpu.SemaphoreType.DMA((chunks, planes + 2)),
                    pltpu.SemaphoreType.DMA((chunks, 5)),
                    pltpu.SemaphoreType.DMA((chunks, 5)),
                    pltpu.SemaphoreType.DMA((chunks + 3,)),
                    pltpu.SemaphoreType.DMA,
                    pltpu.SemaphoreType.DMA((PIECES,)),
                    pltpu.SemaphoreType.DMA((PIECES,)),
                    pltpu.SemaphoreType.DMA((hops, PIECES)),
                    pltpu.SemaphoreType.DMA((hops, PIECES)),
                ],
                compiler_params=pltpu.CompilerParams(
                    vmem_limit_bytes=limit, collective_id=number, has_side_effects=True
                ),
                name=f"deliver{number}",
            )(outgoing, first, goal, masks, table)

        return call

    sizes = capacities(most, chunks)
    calls = [deliver(number + 1, caps) for number, caps in enumerate(sizes)]
    own, other = lax.switch(
        level[0], calls, outgoing, first, goal, masks, jnp.asarray(forward_table(nfft, F))
    )
    step = 32
    return pl.pallas_call(
        functools.partial(correlate_kernel, last=last),
        grid=(CH // step,),
        out_shape=jax.ShapeDtypeStruct((rounds, CH, CH, LAGS), jnp.bfloat16),
        in_specs=[
            SMEM,
            pl.BlockSpec((1, step, width), lambda i: (i, 0, 0)),
            pl.BlockSpec((rounds * CH, width), lambda i: (0, 0)),
            pl.BlockSpec((LAGS, 2 * F), lambda i: (0, 0)),
        ],
        out_specs=pl.BlockSpec((rounds, step, CH, LAGS), lambda i: (0, i, 0, 0)),
        scratch_shapes=[pltpu.VMEM((4, 2 * LAGS, width), jnp.bfloat16)],
        compiler_params=pltpu.CompilerParams(vmem_limit_bytes=limit),
        name="correlate",
    )(
        masks,
        own.reshape(CH // step, step, width),
        other,
        jnp.asarray(lag_table(nfft, F, LAGS)),
    )


def solution(mesh):
    return jax.shard_map(
        local,
        mesh=mesh,
        in_specs=(
            P(("groups", "blk"), None),
            P(("groups", "blk"), None),
            P(("groups", "blk"), None),
            P(("groups", "blk"), None),
            P(),
        ),
        out_specs=P(None, ("groups", "blk"), None, None),
        check_vma=False,
    )
```

```python
import functools
import math

import jax
import jax.numpy as jnp
import numpy as np
from jax import lax
from jax.experimental import pallas as pl
from jax.experimental.pallas import tpu as pltpu
from jax.sharding import PartitionSpec as P

CH = 128
F = 256
LAGS = 128
W = 2
GROUP = 4
CHUNK = 256
AHEAD = 2
PIECES = 8
FLIGHT = 4
LAG = 3
GAP = 64.0
LEVELS = (
    ((96, 96, 96, 80, 64, 64, 48, 32), (64, 64, 64, 64, 48, 48, 32, 16)),
    ((112, 112, 96, 80, 80, 64, 48, 32), (64, 64, 64, 64, 48, 48, 32, 32)),
    ((112, 112, 112, 96, 80, 64, 48, 32), (64, 64, 64, 64, 48, 48, 32, 32)),
    ((128, 128, 112, 96, 80, 80, 64, 48), (64, 64, 64, 64, 64, 48, 48, 32)),
)
VMEM = pl.BlockSpec(memory_space=pltpu.VMEM)
SMEM = pl.BlockSpec(memory_space=pltpu.SMEM)
HBM = pl.BlockSpec(memory_space=pl.ANY)
MESH = pl.DeviceIdType.MESH


def forward_table(nfft, bins):
    sample = np.arange(nfft, dtype=np.int64)[:, None]
    freq = np.arange(1, bins + 1, dtype=np.int64)[None, :]
    angle = (sample * freq % nfft).astype(np.float32) * np.float32(2.0 * math.pi / nfft)
    return np.concatenate([np.cos(angle), -np.sin(angle)], axis=1).astype(jnp.bfloat16)


def lag_table(nfft, bins, lags):
    shift = (np.arange(lags, dtype=np.int64) - lags // 2) % nfft
    freq = np.arange(1, bins + 1, dtype=np.int64)[None, :]
    angle = (freq * shift[:, None] % nfft).astype(np.float32) * np.float32(2.0 * math.pi / nfft)
    return np.concatenate([np.cos(angle), -np.sin(angle)], axis=1).astype(jnp.bfloat16)


def met_at(me, distance, owners):
    other = me
    for k in range(owners.bit_length() - 1):
        if distance >> k & 1:
            other = other + (1 << k) * (1 - 2 * lax.rem(lax.div(me, 1 << k), 2))
    return other


def gathered_at(distance):
    bits = GROUP.bit_length() - 1
    return sum((distance >> k & 1) << (bits - 1 - k) for k in range(bits))


def split_at(planes, most):
    return planes == 4 and most >= 32


def capacities(most, chunks):
    def scaled(level, bound, unit):
        rows = [-(-level[c * len(level) // chunks] * bound // (unit * 16)) * 16 for c in range(chunks)]
        return tuple(min(bound, max(16, r)) for r in rows)

    full = ((most,) * chunks, (most // 2,) * chunks)
    found = []
    for far, near in LEVELS:
        rows = (scaled(far, most, 128), scaled(near, most // 2, 64))
        if rows not in found and rows[0] != full[0]:
            found.append(rows)
    return found + [full]


def first_sends(planes, split):
    if not split:
        return [(d, 0, False) for d in range(planes - 1, -1, -1)]
    other = GROUP // 2
    return [(3, 0, False), (2, 0, False), (1, 0, True), (1, other, True), (0, other, True), (0, 0, True)]


def plan_kernel(
    records_ref, dest_ref, slot_ref, valid_ref,
    outgoing_ref, first_ref, goal_ref, level_ref,
    outbox, inbox, levels, send_sem, recv_sem, level_sems, first_sems, own_sem,
):
    chunks, planes, most, wide = outgoing_ref.shape
    owners = planes * GROUP
    held = records_ref.shape[0]
    me, part = lax.axis_index("blk"), lax.axis_index("groups")
    parts = levels.shape[0]
    shift = most.bit_length() - 1
    plane = lax.div(me, GROUP)

    barrier = pltpu.get_barrier_semaphore()
    for distance in range(1, owners):
        pl.semaphore_signal(
            barrier, inc=1, device_id={"blk": met_at(me, distance, owners)}, device_id_type=MESH
        )
    abroad = [
        (turn, distance, {"groups": lax.rem(part + turn, parts), "blk": met_at(me, distance, owners)})
        for turn in range(1, parts)
        for distance in range(owners)
    ]
    for _, _, other in abroad:
        pl.semaphore_signal(barrier, inc=1, device_id=other, device_id_type=MESH)

    dest, slot, valid = dest_ref[...], slot_ref[...], valid_ref[...]
    group, within = lax.div(dest, GROUP), lax.rem(dest, GROUP)
    key = valid * held + (held - 1 - lax.broadcasted_iota(jnp.int32, (1, held), 1))
    line = lax.broadcasted_iota(jnp.int32, (8, held), 0)
    split = split_at(planes, most)
    half = most // 2
    chip = lax.div(within, GROUP // 2)
    if split:
        near = (group >> 1) == lax.div(plane, 2)
    else:
        near = group < 0
    kind = group * 4 + jnp.where(near, 1 + chip, 0)
    columns = jnp.where(line == 0, kind, jnp.where(line == 1, key, valid)).astype(jnp.float32).T
    key, kind = key.astype(jnp.float32), kind.astype(jnp.float32)
    ahead = (columns[:, 1:2] > key) & (columns[:, 0:1] == kind)
    rank = jnp.sum(ahead.astype(jnp.float32), axis=0, keepdims=True).astype(jnp.int32)
    reach = lax.div(valid - 1, wide)
    level = jnp.zeros((1, held), jnp.float32)
    for far_rows, near_rows in capacities(most, chunks)[:-1]:
        limit = jnp.zeros((1, held), jnp.int32)
        for c in range(chunks):
            limit = jnp.where(reach == c, jnp.where(near, near_rows[c], far_rows[c]), limit)
        level = level + jnp.max((rank >= limit).astype(jnp.float32), axis=1, keepdims=True)
    levels[0, 0] = level[:, :128]
    rank = rank + jnp.where(near, chip * half, 0)

    lines = max(8, planes)
    named = lax.broadcasted_iota(jnp.int32, (lines, held), 0) == group
    ranked = (lax.broadcasted_iota(jnp.int32, (128, held), 0) == rank).astype(jnp.float32)
    ranked = ranked.astype(jnp.bfloat16)

    def spread(values):
        values = jnp.where(named, values, 0).astype(jnp.float32).astype(jnp.bfloat16)
        return lax.dot_general(
            values, ranked, (((1,), (1,)), ((), ())), preferred_element_type=jnp.float32
        )

    code = spread(within + 1) * 256.0 + spread(slot)
    for p in range(planes):
        outbox[p, 0:1, :] = code[p : p + 1]
        outbox[p, 1:2, :] = level[:, :128]

    spots = planes * most
    place = lax.broadcasted_iota(jnp.int32, (spots, held), 0) == group * most + rank
    place = place.astype(jnp.float32).astype(jnp.bfloat16)
    ends = columns[:, 2:3].astype(jnp.int32)

    def pack(c):
        window = lax.broadcasted_iota(jnp.int32, (held, wide), 1) + c * wide < ends
        window = window.astype(jnp.float32).astype(jnp.bfloat16)
        data = records_ref[:, c * wide : (c + 1) * wide] * window + (GAP - GAP * window)
        packed = jnp.dot(place, data, preferred_element_type=jnp.float32)
        outgoing_ref[c] = packed.astype(jnp.bfloat16).reshape(planes, most, wide)

    pack(0)
    pl.semaphore_wait(barrier, owners * parts - 1)
    copies = []
    for turn, distance, other in abroad:
        copies.append(
            pltpu.make_async_remote_copy(
                src_ref=levels.at[0, 0],
                dst_ref=levels.at[turn, distance],
                send_sem=level_sems.at[0, turn, distance],
                recv_sem=level_sems.at[1, turn, distance],
                device_id=other,
                device_id_type=MESH,
            )
        )
        copies[-1].start()
    for distance in range(owners - 1, 0, -1):
        other = met_at(me, distance, owners)
        copies.append(
            pltpu.make_async_remote_copy(
                src_ref=outbox.at[lax.div(other, GROUP)],
                dst_ref=inbox.at[gathered_at(distance % GROUP) * planes + plane],
                send_sem=send_sem.at[distance],
                recv_sem=recv_sem.at[distance],
                device_id={"blk": other},
                device_id_type=MESH,
            )
        )
        copies[-1].start()
    row = lax.rem(lax.div(me, GROUP // 2), 2)
    first = []
    for index, (d, turned, near) in enumerate(first_sends(planes, split)):
        other = met_at(me, GROUP * d + turned, owners)
        rows = pl.ds(0, most)
        if near:
            at = row if turned == 0 else 1 - row
            rows = pl.ds(pl.multiple_of(at * half, 16), half)
        source = outgoing_ref.at[0, lax.div(other, GROUP), rows]
        target = first_ref.at[1 if turned else 0, plane, rows]
        if d == 0 and turned == 0:
            first.append(pltpu.make_async_copy(source, target, own_sem))
        else:
            first.append(
                pltpu.make_async_remote_copy(
                    src_ref=source,
                    dst_ref=target,
                    send_sem=first_sems.at[0, index],
                    recv_sem=first_sems.at[1, index],
                    device_id={"blk": other},
                    device_id_type=MESH,
                )
            )
        first[-1].start()
    inbox[plane] = outbox[plane]

    for c in range(1, chunks):
        pack(c)

    kept = owners * most
    at = lax.broadcasted_iota(jnp.int32, (128, kept), 1)
    sown = lax.broadcasted_iota(jnp.int32, (128, kept), 0) == at - (at >> shift << shift)
    sown = sown.astype(jnp.float32).astype(jnp.bfloat16)
    for copy in copies:
        copy.wait()
    code = inbox[:, 0, :]
    level = jnp.max(inbox[:, 1, :], axis=0, keepdims=True)
    for turn, distance, _ in abroad:
        level = jnp.maximum(level, levels[turn, distance])
    level_ref[0] = jnp.max(level).astype(jnp.int32)
    owner = (code * (1.0 / 256.0)).astype(jnp.int32).astype(jnp.float32)
    slots = code - owner * 256.0
    at = lax.broadcasted_iota(jnp.int32, (owners, kept), 1)
    mine = lax.broadcasted_iota(jnp.int32, (owners, kept), 0) == at >> shift

    def line_up(values):
        values = jnp.dot(values.astype(jnp.bfloat16), sown, preferred_element_type=jnp.float32)
        return jnp.sum(jnp.where(mine, values, 0.0), axis=0, keepdims=True).astype(jnp.int32)

    slots = line_up(slots)
    goal = (slots & (W - 1)) * CH + (slots >> (W.bit_length() - 1))
    goal_ref[...] = jnp.where(line_up(owner) == lax.rem(me, GROUP) + 1, goal, -1)
    for copy in first:
        copy.wait()


def deliver_kernel(
    caps, outgoing_ref, first_ref, goal_ref, masks_ref, table_hbm,
    own_ref, met_ref,
    arrived, select, table, spectrum, energy, tile, leaving, landing,
    plane_send, plane_recv, gather_send, gather_recv, own_sem, table_sem,
    far_send, far_recv, hop_send, hop_recv,
):
    chunks, _, planes, most, wide = arrived.shape
    owners = planes * GROUP
    nfft = chunks * wide
    kept = owners * most
    me = lax.axis_index("blk")
    plane = lax.div(me, GROUP)
    last = owners - 1
    bits = list(range(owners.bit_length() - 3, -1, -1))
    split = split_at(planes, most)
    half = most // 2
    row = lax.rem(lax.div(me, GROUP // 2), 2)
    near_base = lax.div(plane, 2) * 2
    far_planes = pl.ds(2 - near_base, 2) if split else pl.ds(0, planes)
    near_planes = pl.ds(near_base, 2)

    barrier = pltpu.get_barrier_semaphore()
    sends = first_sends(planes, split)
    peers = {GROUP * d + turned for d, turned, _ in sends} - {0}
    peers |= {GROUP // 2, 1} | {1 << k for k in bits} | {last}
    for distance in sorted(peers):
        pl.semaphore_signal(
            barrier, inc=1, device_id={"blk": met_at(me, distance, owners)}, device_id_type=MESH
        )
    fetch = pltpu.make_async_copy(table_hbm, table, table_sem)
    fetch.start()
    pl.semaphore_wait(barrier, len(peers))

    def send(distance, source, target, send_sem, recv_sem):
        copy = pltpu.make_async_remote_copy(
            src_ref=source,
            dst_ref=target,
            send_sem=send_sem,
            recv_sem=recv_sem,
            device_id={"blk": met_at(me, distance, owners)},
            device_id_type=MESH,
        )
        copy.start()
        return copy

    sent, local, gathers = {}, {}, {}

    def some(at, count):
        return pl.ds(pl.multiple_of(at * half, 16), count)

    def begin(c):
        for index, (d, turned, near) in enumerate(sends):
            other = lax.div(met_at(me, GROUP * d + turned, owners), GROUP)
            rows = pl.ds(0, caps[0][c])
            if near:
                rows = some(row if turned == 0 else 1 - row, caps[1][c])
            source = outgoing_ref.at[c, other, rows]
            target = arrived.at[c, 1 if turned else 0, plane, rows]
            if d == 0 and turned == 0:
                sent[c, index] = pltpu.make_async_copy(source, target, own_sem.at[c])
                sent[c, index].start()
            else:
                sent[c, index] = send(
                    GROUP * d + turned, source, target, plane_send.at[c, index], plane_recv.at[c, index]
                )

    def region(c, near):
        if near:
            return near_planes, some(row, caps[1][c])
        return far_planes, pl.ds(0, caps[0][c])

    def forward(c, which, early=False):
        planes_at, rows = region(c, which in (2, 4))
        held_at = 1 if which in (3, 4) else 0
        source = first_ref if early else arrived.at[c]
        gathers[c, which] = send(
            GROUP // 2 if which == 0 else 1,
            source.at[held_at, planes_at, rows],
            arrived.at[c, held_at + (1 if which == 0 else 2), planes_at, rows],
            gather_send.at[c, which],
            gather_recv.at[c, which],
        )

    def forward_first():
        forward(0, 0, True)
        forward(0, 1, True)
        for index, (held_at, near) in enumerate([(0, False), (0, True), (1, True)]):
            if near and not split:
                continue
            planes_at, rows = region(0, near)
            local[index] = pltpu.make_async_copy(
                first_ref.at[held_at, planes_at, rows],
                arrived.at[0, held_at, planes_at, rows],
                own_sem.at[chunks + index],
            )
            local[index].start()
            if near:
                forward(0, 2 * held_at + 2, True)

    ahead = min(AHEAD, chunks - 1)
    forward_first()
    for c in range(1, 1 + ahead):
        begin(c)
    def blank(c, planes_at, rows):
        rest = arrived.at[c, :, planes_at, rows, :]
        rest[...] = jnp.full(rest.shape, GAP, jnp.bfloat16)

    for c in range(chunks):
        if caps[0][c] < most:
            blank(c, far_planes, pl.ds(caps[0][c], most - caps[0][c]))
        if split:
            blank(c, near_planes, some(1 - row, half))
            if caps[1][c] < half:
                start = pl.multiple_of(row * half + caps[1][c], 16)
                blank(c, near_planes, pl.ds(start, half - caps[1][c]))
    goal = goal_ref[...]
    width = min(512, kept)
    for base in range(0, kept, width):
        chosen = lax.broadcasted_iota(jnp.int32, (CH * W, width), 0) == goal[:, base : base + width]
        select[:, base : base + width] = chosen.astype(jnp.float32).astype(jnp.bfloat16)

    def compute(c):
        data = arrived[c].reshape(kept, wide)
        window = jnp.minimum(jnp.maximum(GAP / 2 - data, 0.0), 1.0)
        total = jnp.dot(select[...], data * window, preferred_element_type=jnp.float32)
        count = jnp.dot(select[...], window, preferred_element_type=jnp.float32)
        trace = total / jnp.maximum(count, 1.0)
        squares = trace * trace
        squares = sum(squares[:, k : k + 128] for k in range(0, wide, 128))
        part = jnp.dot(
            trace.astype(jnp.bfloat16),
            table[c * wide : (c + 1) * wide, :],
            preferred_element_type=jnp.float32,
        )
        if c == 0:
            energy[...], spectrum[...] = squares, part
        else:
            energy[...] += squares
            spectrum[...] += part

    for turn in range(1, chunks + 2):
        for stage in range(3):
            c = turn - stage
            if not 0 <= c < chunks:
                continue
            if stage == 0:
                if c + ahead < chunks:
                    begin(c + ahead)
                for index, (_, _, near) in enumerate(sends):
                    if not near:
                        (sent[c, index].wait_recv if sends[index][:2] != (0, 0) else sent[c, index].wait)()
                forward(c, 0)
                forward(c, 1)
                for index, (d, turned, near) in enumerate(sends):
                    if near:
                        (sent[c, index].wait_recv if d + turned else sent[c, index].wait)()
                if split:
                    forward(c, 2)
                    forward(c, 4)
            elif stage == 1:
                gathers[c, 0].wait_recv()
                forward(c, 3)
            else:
                for which in range(1, 5):
                    if (c, which) in gathers:
                        gathers[c, which].wait_recv()
                if c == 0:
                    fetch.wait()
                    for copy in local.values():
                        copy.wait()
                compute(c)

    second = masks_ref[0] ^ masks_ref[1] ^ last
    use_far = lax.div(second, 1 << (len(bits)))
    path = second + use_far * (last - 2 * second)
    size = CH // PIECES

    def choose(flag, yes, no):
        flag = jnp.full(yes.shape, flag.astype(jnp.float32), jnp.float32).astype(jnp.bfloat16)
        return yes * flag + no * (1 - flag)

    factor = lax.rsqrt(jnp.sum(energy[...], axis=1, keepdims=True) * (1.0 / nfft) + 1e-06)
    far = []

    def far_copy(q):
        rows = pl.ds(q * size, size)
        far.append(send(last, tile.at[rows], met_ref.at[rows], far_send.at[q], far_recv.at[q]))

    for q in range(PIECES):
        rows = slice(q * size, (q + 1) * size)
        for w in range(W):
            at = slice(w * CH + q * size, w * CH + (q + 1) * size)
            parts = spectrum[at, :] * factor[at]
            real_part, imag_part = parts[:, :F], parts[:, F:]
            amplitude = lax.rsqrt(
                jnp.maximum(real_part * real_part + imag_part * imag_part, nfft / 4.0)
            )
            real_part = (real_part * amplitude).astype(jnp.bfloat16)
            imag_part = (imag_part * amplitude).astype(jnp.bfloat16)
            base = 2 * F * w
            tile[rows, base : base + F] = real_part
            tile[rows, base + F : base + 2 * F] = imag_part
            own_ref[rows, base : base + F] = real_part.astype(jnp.float32)
            own_ref[rows, base + F : base + 2 * F] = imag_part.astype(jnp.float32)
        if q < FLIGHT:
            far_copy(q)

    hops = {}
    for turn in range(PIECES + LAG * len(bits)):
        for stage in range(len(bits) + 1):
            q = turn - LAG * stage
            if not 0 <= q < PIECES:
                continue
            rows = slice(q * size, (q + 1) * size)
            if stage == 0:
                far[q].wait_recv()
                if q + FLIGHT < PIECES:
                    far_copy(q + FLIGHT)
                value = choose(use_far, met_ref[rows], tile[rows])
            else:
                hops[stage - 1, q].wait_recv()
                taken = lax.rem(lax.div(path, 1 << bits[stage - 1]), 2)
                value = choose(taken, landing[stage - 1, rows], leaving[stage - 1, rows])
            if stage == len(bits):
                met_ref[CH + q * size : CH + (q + 1) * size] = value
            else:
                leaving[stage, rows] = value
                spot = pl.ds(q * size, size)
                hops[stage, q] = send(
                    1 << bits[stage],
                    leaving.at[stage, spot],
                    landing.at[stage, spot],
                    hop_send.at[stage, q],
                    hop_recv.at[stage, q],
                )
    abroad = [copy for (_, index), copy in sent.items() if sends[index][:2] != (0, 0)]
    for copy in abroad + list(gathers.values()) + far + list(hops.values()):
        copy.wait_send()


def correlate_kernel(masks_ref, own_ref, other_ref, table_ref, out_ref, turned, *, last):
    scale = 1.0 / math.sqrt(W * F)
    cosine, sine = table_ref[:, :F], table_ref[:, F:]
    far_round = (masks_ref[0] != last).astype(jnp.int32)
    slots, step = turned.shape[0], own_ref.shape[1]

    for index in range(step // 2):
        at = index % slots
        for half in range(2):
            mine = own_ref[0, index * 2 + half : index * 2 + half + 1, :].astype(jnp.bfloat16)
            rows = slice(half * LAGS, (half + 1) * LAGS)
            for w in range(W):
                base = 2 * F * w
                ur, ui = mine[:, base : base + F], mine[:, base + F : base + 2 * F]
                turned[at, rows, base : base + F] = cosine * ur + sine * ui
                turned[at, rows, base + F : base + 2 * F] = cosine * ui - sine * ur
        product = lax.dot_general(
            other_ref[...],
            turned[at],
            (((1,), (1,)), ((), ())),
            preferred_element_type=jnp.float32,
        )
        product = (product * scale).astype(jnp.bfloat16)
        for half in range(2):
            lags = slice(half * LAGS, (half + 1) * LAGS)
            out_ref[far_round, index * 2 + half] = product[:CH, lags]
            out_ref[1 - far_round, index * 2 + half] = product[CH:, lags]


def local(records, dest, slot, valid, masks):
    owners, parts = lax.axis_size("blk"), lax.axis_size("groups")
    held, nfft = records.shape
    rounds = masks.shape[0]
    planes, chunks = owners // GROUP, nfft // CHUNK
    most = max(16, GROUP * 2 * held // owners)
    width = 2 * F * W
    limit = 56 * 2**20
    outgoing, first, goal, level = pl.pallas_call(
        plan_kernel,
        out_shape=[
            jax.ShapeDtypeStruct((chunks, planes, most, CHUNK), jnp.bfloat16),
            jax.ShapeDtypeStruct((2, planes, most, CHUNK), jnp.bfloat16),
            jax.ShapeDtypeStruct((1, owners * most), jnp.int32),
            jax.ShapeDtypeStruct((1,), jnp.int32),
        ],
        in_specs=[VMEM] * 4,
        out_specs=[VMEM, VMEM, VMEM, SMEM],
        scratch_shapes=[
            pltpu.VMEM((planes, 2, 128), jnp.float32),
            pltpu.VMEM((owners, 2, 128), jnp.float32),
            pltpu.VMEM((parts, owners, 1, 128), jnp.float32),
            pltpu.SemaphoreType.DMA((owners,)),
            pltpu.SemaphoreType.DMA((owners,)),
            pltpu.SemaphoreType.DMA((2, parts, owners)),
            pltpu.SemaphoreType.DMA((2, planes + 2)),
            pltpu.SemaphoreType.DMA,
        ],
        compiler_params=pltpu.CompilerParams(
            vmem_limit_bytes=limit, collective_id=0, has_side_effects=True
        ),
        name="plan",
    )(records, dest.reshape(1, held), slot.reshape(1, held), valid.reshape(1, held))

    last = owners - 1
    hops = owners.bit_length() - 2

    def deliver(number, caps):
        def call(outgoing, first, goal, masks, table):
            return pl.pallas_call(
                functools.partial(deliver_kernel, caps),
                out_shape=[
                    jax.ShapeDtypeStruct((CH, width), jnp.float32),
                    jax.ShapeDtypeStruct((rounds * CH, width), jnp.bfloat16),
                ],
                in_specs=[HBM, HBM, VMEM, SMEM, HBM],
                out_specs=[VMEM] * 2,
                scratch_shapes=[
                    pltpu.VMEM((chunks, GROUP, planes, most, CHUNK), jnp.bfloat16),
                    pltpu.VMEM((CH * W, owners * most), jnp.bfloat16),
                    pltpu.VMEM((nfft, 2 * F), jnp.bfloat16),
                    pltpu.VMEM((CH * W, 2 * F), jnp.float32),
                    pltpu.VMEM((CH * W, 128), jnp.float32),
                    pltpu.VMEM((CH, width), jnp.bfloat16),
                    pltpu.VMEM((hops, CH, width), jnp.bfloat16),
                    pltpu.VMEM((hops, CH, width), jnp.bfloat16),
                    pltpu.SemaphoreType.DMA((chunks, planes + 2)),
                    pltpu.SemaphoreType.DMA((chunks, planes + 2)),
                    pltpu.SemaphoreType.DMA((chunks, 5)),
                    pltpu.SemaphoreType.DMA((chunks, 5)),
                    pltpu.SemaphoreType.DMA((chunks + 3,)),
                    pltpu.SemaphoreType.DMA,
                    pltpu.SemaphoreType.DMA((PIECES,)),
                    pltpu.SemaphoreType.DMA((PIECES,)),
                    pltpu.SemaphoreType.DMA((hops, PIECES)),
                    pltpu.SemaphoreType.DMA((hops, PIECES)),
                ],
                compiler_params=pltpu.CompilerParams(
                    vmem_limit_bytes=limit, collective_id=number, has_side_effects=True
                ),
                name=f"deliver{number}",
            )(outgoing, first, goal, masks, table)

        return call

    sizes = capacities(most, chunks)
    calls = [deliver(number + 1, caps) for number, caps in enumerate(sizes)]
    own, other = lax.switch(
        level[0], calls, outgoing, first, goal, masks, jnp.asarray(forward_table(nfft, F))
    )
    step = 32
    return pl.pallas_call(
        functools.partial(correlate_kernel, last=last),
        grid=(CH // step,),
        out_shape=jax.ShapeDtypeStruct((rounds, CH, CH, LAGS), jnp.bfloat16),
        in_specs=[
            SMEM,
            pl.BlockSpec((1, step, width), lambda i: (i, 0, 0)),
            pl.BlockSpec((rounds * CH, width), lambda i: (0, 0)),
            pl.BlockSpec((LAGS, 2 * F), lambda i: (0, 0)),
        ],
        out_specs=pl.BlockSpec((rounds, step, CH, LAGS), lambda i: (0, i, 0, 0)),
        scratch_shapes=[pltpu.VMEM((4, 2 * LAGS, width), jnp.bfloat16)],
        compiler_params=pltpu.CompilerParams(vmem_limit_bytes=limit),
        name="correlate",
    )(
        masks,
        own.reshape(CH // step, step, width),
        other,
        jnp.asarray(lag_table(nfft, F, LAGS)),
    )


def solution(mesh):
    return jax.shard_map(
        local,
        mesh=mesh,
        in_specs=(
            P(("groups", "blk"), None),
            P(("groups", "blk"), None),
            P(("groups", "blk"), None),
            P(("groups", "blk"), None),
            P(),
        ),
        out_specs=P(None, ("groups", "blk"), None, None),
        check_vma=False,
    )
```

```python
import functools
import math

import jax
import jax.numpy as jnp
import numpy as np
from jax import lax
from jax.experimental import pallas as pl
from jax.experimental.pallas import tpu as pltpu
from jax.sharding import PartitionSpec as P

CH = 128
F = 256
LAGS = 128
W = 2
GROUP = 4
CHUNK = 256
AHEAD = 2
PIECES = 8
FLIGHT = 4
LAG = 3
GAP = 64.0
LEVELS = (
    ((96, 96, 80, 80, 64, 48, 48, 32), (64, 64, 64, 48, 48, 32, 32, 16)),
    ((96, 96, 96, 80, 64, 64, 48, 32), (64, 64, 64, 64, 48, 48, 32, 16)),
    ((112, 112, 96, 80, 64, 64, 48, 32), (64, 64, 64, 64, 48, 48, 32, 32)),
    ((112, 112, 112, 96, 80, 64, 48, 32), (64, 64, 64, 64, 48, 48, 32, 32)),
    ((128, 128, 112, 96, 80, 80, 64, 48), (64, 64, 64, 64, 64, 48, 48, 32)),
)
VMEM = pl.BlockSpec(memory_space=pltpu.VMEM)
SMEM = pl.BlockSpec(memory_space=pltpu.SMEM)
HBM = pl.BlockSpec(memory_space=pl.ANY)
MESH = pl.DeviceIdType.MESH


def forward_table(nfft, bins):
    sample = np.arange(nfft, dtype=np.int64)[:, None]
    freq = np.arange(1, bins + 1, dtype=np.int64)[None, :]
    angle = (sample * freq % nfft).astype(np.float32) * np.float32(2.0 * math.pi / nfft)
    return np.concatenate([np.cos(angle), -np.sin(angle)], axis=1).astype(jnp.bfloat16)


def lag_table(nfft, bins, lags):
    shift = (np.arange(lags, dtype=np.int64) - lags // 2) % nfft
    freq = np.arange(1, bins + 1, dtype=np.int64)[None, :]
    angle = (freq * shift[:, None] % nfft).astype(np.float32) * np.float32(2.0 * math.pi / nfft)
    return np.concatenate([np.cos(angle), -np.sin(angle)], axis=1).astype(jnp.bfloat16)


def met_at(me, distance, owners):
    other = me
    for k in range(owners.bit_length() - 1):
        if distance >> k & 1:
            other = other + (1 << k) * (1 - 2 * lax.rem(lax.div(me, 1 << k), 2))
    return other


def gathered_at(distance):
    bits = GROUP.bit_length() - 1
    return sum((distance >> k & 1) << (bits - 1 - k) for k in range(bits))


def split_at(planes, most):
    return planes == 4 and most >= 32


def kept_at(planes, most):
    return GROUP * planes * most * (3 if split_at(planes, most) else 4) // 4


def capacities(most, chunks):
    def scaled(level, bound, unit):
        rows = [-(-level[c * len(level) // chunks] * bound // (unit * 16)) * 16 for c in range(chunks)]
        return tuple(min(bound, max(16, r)) for r in rows)

    full = ((most,) * chunks, (most // 2,) * chunks)
    found = []
    for far, near in LEVELS:
        rows = (scaled(far, most, 128), scaled(near, most // 2, 64))
        if rows not in found and rows[0] != full[0]:
            found.append(rows)
    return found + [full]


def first_sends(planes, split):
    if not split:
        return [(d, 0, False) for d in range(planes - 1, -1, -1)]
    other = GROUP // 2
    return [(3, 0, False), (2, 0, False), (1, 0, True), (1, other, True), (0, other, True), (0, 0, True)]


def plan_kernel(
    records_ref, dest_ref, slot_ref, valid_ref,
    outgoing_ref, first_ref, goal_ref, level_ref,
    outbox, inbox, levels, send_sem, recv_sem, level_sems, first_sems, own_sem,
):
    chunks, planes, most, wide = outgoing_ref.shape
    owners = planes * GROUP
    held = records_ref.shape[0]
    me, part = lax.axis_index("blk"), lax.axis_index("groups")
    parts = levels.shape[0]
    shift = most.bit_length() - 1
    plane = lax.div(me, GROUP)

    barrier = pltpu.get_barrier_semaphore()
    for distance in range(1, owners):
        pl.semaphore_signal(
            barrier, inc=1, device_id={"blk": met_at(me, distance, owners)}, device_id_type=MESH
        )
    abroad = [
        (turn, distance, {"groups": lax.rem(part + turn, parts), "blk": met_at(me, distance, owners)})
        for turn in range(1, parts)
        for distance in range(owners)
    ]
    for _, _, other in abroad:
        pl.semaphore_signal(barrier, inc=1, device_id=other, device_id_type=MESH)

    dest, slot, valid = dest_ref[...], slot_ref[...], valid_ref[...]
    group, within = lax.div(dest, GROUP), lax.rem(dest, GROUP)
    key = valid * held + (held - 1 - lax.broadcasted_iota(jnp.int32, (1, held), 1))
    line = lax.broadcasted_iota(jnp.int32, (8, held), 0)
    split = split_at(planes, most)
    half = most // 2
    chip = lax.div(within, GROUP // 2)
    if split:
        near = (group >> 1) == lax.div(plane, 2)
    else:
        near = group < 0
    kind = group * 4 + jnp.where(near, 1 + chip, 0)
    columns = jnp.where(line == 0, kind, jnp.where(line == 1, key, valid)).astype(jnp.float32).T
    key, kind = key.astype(jnp.float32), kind.astype(jnp.float32)
    ahead = (columns[:, 1:2] > key) & (columns[:, 0:1] == kind)
    rank = jnp.sum(ahead.astype(jnp.float32), axis=0, keepdims=True).astype(jnp.int32)
    reach = lax.div(valid - 1, wide)
    level = jnp.zeros((1, held), jnp.float32)
    for far_rows, near_rows in capacities(most, chunks)[:-1]:
        limit = jnp.zeros((1, held), jnp.int32)
        for c in range(chunks):
            limit = jnp.where(reach == c, jnp.where(near, near_rows[c], far_rows[c]), limit)
        level = level + jnp.max((rank >= limit).astype(jnp.float32), axis=1, keepdims=True)
    levels[0, 0] = level[:, :128]
    rank = rank + jnp.where(near, chip * half, 0)

    lines = max(8, planes)
    named = lax.broadcasted_iota(jnp.int32, (lines, held), 0) == group
    ranked = (lax.broadcasted_iota(jnp.int32, (128, held), 0) == rank).astype(jnp.float32)
    ranked = ranked.astype(jnp.bfloat16)

    def spread(values):
        values = jnp.where(named, values, 0).astype(jnp.float32).astype(jnp.bfloat16)
        return lax.dot_general(
            values, ranked, (((1,), (1,)), ((), ())), preferred_element_type=jnp.float32
        )

    code = spread(within + 1) * 256.0 + spread(slot)
    for p in range(planes):
        outbox[p, 0:1, :] = code[p : p + 1]
        outbox[p, 1:2, :] = level[:, :128]

    spots = planes * most
    place = lax.broadcasted_iota(jnp.int32, (spots, held), 0) == group * most + rank
    place = place.astype(jnp.float32).astype(jnp.bfloat16)
    ends = columns[:, 2:3].astype(jnp.int32)

    def pack(c):
        window = lax.broadcasted_iota(jnp.int32, (held, wide), 1) + c * wide < ends
        window = window.astype(jnp.float32).astype(jnp.bfloat16)
        data = records_ref[:, c * wide : (c + 1) * wide] * window + (GAP - GAP * window)
        packed = jnp.dot(place, data, preferred_element_type=jnp.float32)
        outgoing_ref[c] = packed.astype(jnp.bfloat16).reshape(planes, most, wide)

    pack(0)
    pl.semaphore_wait(barrier, owners * parts - 1)
    copies = []
    for turn, distance, other in abroad:
        copies.append(
            pltpu.make_async_remote_copy(
                src_ref=levels.at[0, 0],
                dst_ref=levels.at[turn, distance],
                send_sem=level_sems.at[0, turn, distance],
                recv_sem=level_sems.at[1, turn, distance],
                device_id=other,
                device_id_type=MESH,
            )
        )
        copies[-1].start()
    for distance in range(owners - 1, 0, -1):
        other = met_at(me, distance, owners)
        copies.append(
            pltpu.make_async_remote_copy(
                src_ref=outbox.at[lax.div(other, GROUP)],
                dst_ref=inbox.at[gathered_at(distance % GROUP) * planes + plane],
                send_sem=send_sem.at[distance],
                recv_sem=recv_sem.at[distance],
                device_id={"blk": other},
                device_id_type=MESH,
            )
        )
        copies[-1].start()
    row = lax.rem(lax.div(me, GROUP // 2), 2)
    first = []
    for index, (d, turned, near) in enumerate(first_sends(planes, split)):
        other = met_at(me, GROUP * d + turned, owners)
        rows = pl.ds(0, most)
        if near:
            at = row if turned == 0 else 1 - row
            rows = pl.ds(pl.multiple_of(at * half, 16), half)
        source = outgoing_ref.at[0, lax.div(other, GROUP), rows]
        target = first_ref.at[1 if turned else 0, plane, rows]
        if d == 0 and turned == 0:
            first.append(pltpu.make_async_copy(source, target, own_sem))
        else:
            first.append(
                pltpu.make_async_remote_copy(
                    src_ref=source,
                    dst_ref=target,
                    send_sem=first_sems.at[0, index],
                    recv_sem=first_sems.at[1, index],
                    device_id={"blk": other},
                    device_id_type=MESH,
                )
            )
        first[-1].start()
    inbox[plane] = outbox[plane]

    for c in range(1, chunks):
        pack(c)

    kept = goal_ref.shape[1]
    at = lax.broadcasted_iota(jnp.int32, (1, kept), 1)
    source, spot = at >> shift, at & (most - 1)
    if split:
        near_base = lax.div(plane, 2) * 2
        far_base = 2 - near_base
        rest = at - GROUP * 2 * most
        source = jnp.where(
            rest < 0,
            (at >> (shift + 1)) * planes + far_base + ((at >> shift) & 1),
            (rest >> shift) * planes + near_base + ((rest >> (shift - 1)) & 1),
        )
        spot = jnp.where(rest < 0, spot, row * half + (rest & (half - 1)))
    sown = lax.broadcasted_iota(jnp.int32, (128, kept), 0) == spot
    sown = sown.astype(jnp.float32).astype(jnp.bfloat16)
    for copy in copies:
        copy.wait()
    code = inbox[:, 0, :]
    level = jnp.max(inbox[:, 1, :], axis=0, keepdims=True)
    for turn, distance, _ in abroad:
        level = jnp.maximum(level, levels[turn, distance])
    level_ref[0] = jnp.max(level).astype(jnp.int32)
    owner = (code * (1.0 / 256.0)).astype(jnp.int32).astype(jnp.float32)
    slots = code - owner * 256.0
    mine = lax.broadcasted_iota(jnp.int32, (owners, kept), 0) == source

    def line_up(values):
        values = jnp.dot(values.astype(jnp.bfloat16), sown, preferred_element_type=jnp.float32)
        return jnp.sum(jnp.where(mine, values, 0.0), axis=0, keepdims=True).astype(jnp.int32)

    slots = line_up(slots)
    goal = (slots & (W - 1)) * CH + (slots >> (W.bit_length() - 1))
    goal_ref[...] = jnp.where(line_up(owner) == lax.rem(me, GROUP) + 1, goal, -1)
    for copy in first:
        copy.wait()


def deliver_kernel(
    caps, outgoing_ref, first_ref, goal_ref, masks_ref, table_hbm,
    own_ref, met_ref,
    arrived, select, table, spectrum, energy, tile, leaving, landing,
    plane_send, plane_recv, gather_send, gather_recv, own_sem, table_sem,
    far_send, far_recv, hop_send, hop_recv,
):
    chunks, _, planes, most, wide = arrived.shape
    owners = planes * GROUP
    nfft = chunks * wide
    kept = goal_ref.shape[1]
    me = lax.axis_index("blk")
    plane = lax.div(me, GROUP)
    last = owners - 1
    bits = list(range(owners.bit_length() - 3, -1, -1))
    split = split_at(planes, most)
    half = most // 2
    row = lax.rem(lax.div(me, GROUP // 2), 2)
    near_base = lax.div(plane, 2) * 2
    far_planes = pl.ds(2 - near_base, 2) if split else pl.ds(0, planes)
    near_planes = pl.ds(near_base, 2)

    barrier = pltpu.get_barrier_semaphore()
    sends = first_sends(planes, split)
    peers = {GROUP * d + turned for d, turned, _ in sends} - {0}
    peers |= {GROUP // 2, 1} | {1 << k for k in bits} | {last}
    for distance in sorted(peers):
        pl.semaphore_signal(
            barrier, inc=1, device_id={"blk": met_at(me, distance, owners)}, device_id_type=MESH
        )
    fetch = pltpu.make_async_copy(table_hbm, table, table_sem)
    fetch.start()
    pl.semaphore_wait(barrier, len(peers))

    def send(distance, source, target, send_sem, recv_sem):
        copy = pltpu.make_async_remote_copy(
            src_ref=source,
            dst_ref=target,
            send_sem=send_sem,
            recv_sem=recv_sem,
            device_id={"blk": met_at(me, distance, owners)},
            device_id_type=MESH,
        )
        copy.start()
        return copy

    sent, local, gathers = {}, {}, {}

    def some(at, count):
        return pl.ds(pl.multiple_of(at * half, 16), count)

    def begin(c):
        for index, (d, turned, near) in enumerate(sends):
            other = lax.div(met_at(me, GROUP * d + turned, owners), GROUP)
            rows = pl.ds(0, caps[0][c])
            if near:
                rows = some(row if turned == 0 else 1 - row, caps[1][c])
            source = outgoing_ref.at[c, other, rows]
            target = arrived.at[c, 1 if turned else 0, plane, rows]
            if d == 0 and turned == 0:
                sent[c, index] = pltpu.make_async_copy(source, target, own_sem.at[c])
                sent[c, index].start()
            else:
                sent[c, index] = send(
                    GROUP * d + turned, source, target, plane_send.at[c, index], plane_recv.at[c, index]
                )

    def region(c, near):
        if near:
            return near_planes, some(row, caps[1][c])
        return far_planes, pl.ds(0, caps[0][c])

    def forward(c, which, early=False):
        planes_at, rows = region(c, which in (2, 4))
        held_at = 1 if which in (3, 4) else 0
        source = first_ref if early else arrived.at[c]
        gathers[c, which] = send(
            GROUP // 2 if which == 0 else 1,
            source.at[held_at, planes_at, rows],
            arrived.at[c, held_at + (1 if which == 0 else 2), planes_at, rows],
            gather_send.at[c, which],
            gather_recv.at[c, which],
        )

    def forward_first():
        forward(0, 0, True)
        forward(0, 1, True)
        for index, (held_at, near) in enumerate([(0, False), (0, True), (1, True)]):
            if near and not split:
                continue
            planes_at, rows = region(0, near)
            local[index] = pltpu.make_async_copy(
                first_ref.at[held_at, planes_at, rows],
                arrived.at[0, held_at, planes_at, rows],
                own_sem.at[chunks + index],
            )
            local[index].start()
            if near:
                forward(0, 2 * held_at + 2, True)

    ahead = min(AHEAD, chunks - 1)
    forward_first()
    for c in range(1, 1 + ahead):
        begin(c)
    def blank(c, planes_at, rows):
        rest = arrived.at[c, :, planes_at, rows, :]
        rest[...] = jnp.full(rest.shape, GAP, jnp.bfloat16)

    for c in range(chunks):
        if caps[0][c] < most:
            blank(c, far_planes, pl.ds(caps[0][c], most - caps[0][c]))
        if split:
            if caps[1][c] < half:
                start = pl.multiple_of(row * half + caps[1][c], 16)
                blank(c, near_planes, pl.ds(start, half - caps[1][c]))
    goal = goal_ref[...]
    width = min(512, kept)
    for base in range(0, kept, width):
        chosen = lax.broadcasted_iota(jnp.int32, (CH * W, width), 0) == goal[:, base : base + width]
        select[:, base : base + width] = chosen.astype(jnp.float32).astype(jnp.bfloat16)

    def compute(c):
        if split:
            data = jnp.concatenate(
                [
                    arrived[c, :, far_planes].reshape(2 * GROUP * most, wide),
                    arrived[c, :, near_planes, some(row, half)].reshape(2 * GROUP * half, wide),
                ],
                axis=0,
            )
        else:
            data = arrived[c].reshape(kept, wide)
        window = jnp.minimum(jnp.maximum(GAP / 2 - data, 0.0), 1.0)
        total = jnp.dot(select[...], data * window, preferred_element_type=jnp.float32)
        count = jnp.dot(select[...], window, preferred_element_type=jnp.float32)
        trace = total / jnp.maximum(count, 1.0)
        squares = trace * trace
        squares = sum(squares[:, k : k + 128] for k in range(0, wide, 128))
        part = jnp.dot(
            trace.astype(jnp.bfloat16),
            table[c * wide : (c + 1) * wide, :],
            preferred_element_type=jnp.float32,
        )
        if c == 0:
            energy[...], spectrum[...] = squares, part
        else:
            energy[...] += squares
            spectrum[...] += part

    for turn in range(1, chunks + 2):
        for stage in range(3):
            c = turn - stage
            if not 0 <= c < chunks:
                continue
            if stage == 0:
                if c + ahead < chunks:
                    begin(c + ahead)
                for index, (_, _, near) in enumerate(sends):
                    if not near:
                        (sent[c, index].wait_recv if sends[index][:2] != (0, 0) else sent[c, index].wait)()
                forward(c, 0)
                forward(c, 1)
                for index, (d, turned, near) in enumerate(sends):
                    if near:
                        (sent[c, index].wait_recv if d + turned else sent[c, index].wait)()
                if split:
                    forward(c, 2)
                    forward(c, 4)
            elif stage == 1:
                gathers[c, 0].wait_recv()
                forward(c, 3)
            else:
                for which in range(1, 5):
                    if (c, which) in gathers:
                        gathers[c, which].wait_recv()
                if c == 0:
                    fetch.wait()
                    for copy in local.values():
                        copy.wait()
                compute(c)

    second = masks_ref[0] ^ masks_ref[1] ^ last
    use_far = lax.div(second, 1 << (len(bits)))
    path = second + use_far * (last - 2 * second)
    size = CH // PIECES

    def choose(flag, yes, no):
        flag = jnp.full(yes.shape, flag.astype(jnp.float32), jnp.float32).astype(jnp.bfloat16)
        return yes * flag + no * (1 - flag)

    factor = lax.rsqrt(jnp.sum(energy[...], axis=1, keepdims=True) * (1.0 / nfft) + 1e-06)
    far = []

    def far_copy(q):
        rows = pl.ds(q * size, size)
        far.append(send(last, tile.at[rows], met_ref.at[rows], far_send.at[q], far_recv.at[q]))

    for q in range(PIECES):
        rows = slice(q * size, (q + 1) * size)
        for w in range(W):
            at = slice(w * CH + q * size, w * CH + (q + 1) * size)
            parts = spectrum[at, :] * factor[at]
            real_part, imag_part = parts[:, :F], parts[:, F:]
            amplitude = lax.rsqrt(
                jnp.maximum(real_part * real_part + imag_part * imag_part, nfft / 4.0)
            )
            real_part = (real_part * amplitude).astype(jnp.bfloat16)
            imag_part = (imag_part * amplitude).astype(jnp.bfloat16)
            base = 2 * F * w
            tile[rows, base : base + F] = real_part
            tile[rows, base + F : base + 2 * F] = imag_part
            own_ref[rows, base : base + F] = real_part.astype(jnp.float32)
            own_ref[rows, base + F : base + 2 * F] = imag_part.astype(jnp.float32)
        if q < FLIGHT:
            far_copy(q)

    hops = {}
    for turn in range(PIECES + LAG * len(bits)):
        for stage in range(len(bits) + 1):
            q = turn - LAG * stage
            if not 0 <= q < PIECES:
                continue
            rows = slice(q * size, (q + 1) * size)
            if stage == 0:
                far[q].wait_recv()
                if q + FLIGHT < PIECES:
                    far_copy(q + FLIGHT)
                value = choose(use_far, met_ref[rows], tile[rows])
            else:
                hops[stage - 1, q].wait_recv()
                taken = lax.rem(lax.div(path, 1 << bits[stage - 1]), 2)
                value = choose(taken, landing[stage - 1, rows], leaving[stage - 1, rows])
            if stage == len(bits):
                met_ref[CH + q * size : CH + (q + 1) * size] = value
            else:
                leaving[stage, rows] = value
                spot = pl.ds(q * size, size)
                hops[stage, q] = send(
                    1 << bits[stage],
                    leaving.at[stage, spot],
                    landing.at[stage, spot],
                    hop_send.at[stage, q],
                    hop_recv.at[stage, q],
                )
    abroad = [copy for (_, index), copy in sent.items() if sends[index][:2] != (0, 0)]
    for copy in abroad + list(gathers.values()) + far + list(hops.values()):
        copy.wait_send()


def correlate_kernel(masks_ref, own_ref, other_ref, table_ref, out_ref, turned, *, last):
    scale = 1.0 / math.sqrt(W * F)
    cosine, sine = table_ref[:, :F], table_ref[:, F:]
    far_round = (masks_ref[0] != last).astype(jnp.int32)
    slots, step = turned.shape[0], own_ref.shape[1]

    for index in range(step // 2):
        at = index % slots
        for half in range(2):
            mine = own_ref[0, index * 2 + half : index * 2 + half + 1, :].astype(jnp.bfloat16)
            rows = slice(half * LAGS, (half + 1) * LAGS)
            for w in range(W):
                base = 2 * F * w
                ur, ui = mine[:, base : base + F], mine[:, base + F : base + 2 * F]
                turned[at, rows, base : base + F] = cosine * ur + sine * ui
                turned[at, rows, base + F : base + 2 * F] = cosine * ui - sine * ur
        product = lax.dot_general(
            other_ref[...],
            turned[at],
            (((1,), (1,)), ((), ())),
            preferred_element_type=jnp.float32,
        )
        product = (product * scale).astype(jnp.bfloat16)
        for half in range(2):
            lags = slice(half * LAGS, (half + 1) * LAGS)
            out_ref[far_round, index * 2 + half] = product[:CH, lags]
            out_ref[1 - far_round, index * 2 + half] = product[CH:, lags]


def local(records, dest, slot, valid, masks):
    owners, parts = lax.axis_size("blk"), lax.axis_size("groups")
    held, nfft = records.shape
    rounds = masks.shape[0]
    planes, chunks = owners // GROUP, nfft // CHUNK
    most = max(16, GROUP * 2 * held // owners)
    width = 2 * F * W
    limit = 56 * 2**20
    outgoing, first, goal, level = pl.pallas_call(
        plan_kernel,
        out_shape=[
            jax.ShapeDtypeStruct((chunks, planes, most, CHUNK), jnp.bfloat16),
            jax.ShapeDtypeStruct((2, planes, most, CHUNK), jnp.bfloat16),
            jax.ShapeDtypeStruct((1, kept_at(planes, most)), jnp.int32),
            jax.ShapeDtypeStruct((1,), jnp.int32),
        ],
        in_specs=[VMEM] * 4,
        out_specs=[VMEM, VMEM, VMEM, SMEM],
        scratch_shapes=[
            pltpu.VMEM((planes, 2, 128), jnp.float32),
            pltpu.VMEM((owners, 2, 128), jnp.float32),
            pltpu.VMEM((parts, owners, 1, 128), jnp.float32),
            pltpu.SemaphoreType.DMA((owners,)),
            pltpu.SemaphoreType.DMA((owners,)),
            pltpu.SemaphoreType.DMA((2, parts, owners)),
            pltpu.SemaphoreType.DMA((2, planes + 2)),
            pltpu.SemaphoreType.DMA,
        ],
        compiler_params=pltpu.CompilerParams(
            vmem_limit_bytes=limit, collective_id=0, has_side_effects=True
        ),
        name="plan",
    )(records, dest.reshape(1, held), slot.reshape(1, held), valid.reshape(1, held))

    last = owners - 1
    hops = owners.bit_length() - 2

    def deliver(number, caps):
        def call(outgoing, first, goal, masks, table):
            return pl.pallas_call(
                functools.partial(deliver_kernel, caps),
                out_shape=[
                    jax.ShapeDtypeStruct((CH, width), jnp.float32),
                    jax.ShapeDtypeStruct((rounds * CH, width), jnp.bfloat16),
                ],
                in_specs=[HBM, HBM, VMEM, SMEM, HBM],
                out_specs=[VMEM] * 2,
                scratch_shapes=[
                    pltpu.VMEM((chunks, GROUP, planes, most, CHUNK), jnp.bfloat16),
                    pltpu.VMEM((CH * W, kept_at(planes, most)), jnp.bfloat16),
                    pltpu.VMEM((nfft, 2 * F), jnp.bfloat16),
                    pltpu.VMEM((CH * W, 2 * F), jnp.float32),
                    pltpu.VMEM((CH * W, 128), jnp.float32),
                    pltpu.VMEM((CH, width), jnp.bfloat16),
                    pltpu.VMEM((hops, CH, width), jnp.bfloat16),
                    pltpu.VMEM((hops, CH, width), jnp.bfloat16),
                    pltpu.SemaphoreType.DMA((chunks, planes + 2)),
                    pltpu.SemaphoreType.DMA((chunks, planes + 2)),
                    pltpu.SemaphoreType.DMA((chunks, 5)),
                    pltpu.SemaphoreType.DMA((chunks, 5)),
                    pltpu.SemaphoreType.DMA((chunks + 3,)),
                    pltpu.SemaphoreType.DMA,
                    pltpu.SemaphoreType.DMA((PIECES,)),
                    pltpu.SemaphoreType.DMA((PIECES,)),
                    pltpu.SemaphoreType.DMA((hops, PIECES)),
                    pltpu.SemaphoreType.DMA((hops, PIECES)),
                ],
                compiler_params=pltpu.CompilerParams(
                    vmem_limit_bytes=limit, collective_id=number, has_side_effects=True
                ),
                name=f"deliver{number}",
            )(outgoing, first, goal, masks, table)

        return call

    sizes = capacities(most, chunks)
    calls = [deliver(number + 1, caps) for number, caps in enumerate(sizes)]
    own, other = lax.switch(
        level[0], calls, outgoing, first, goal, masks, jnp.asarray(forward_table(nfft, F))
    )
    step = 32
    return pl.pallas_call(
        functools.partial(correlate_kernel, last=last),
        grid=(CH // step,),
        out_shape=jax.ShapeDtypeStruct((rounds, CH, CH, LAGS), jnp.bfloat16),
        in_specs=[
            SMEM,
            pl.BlockSpec((1, step, width), lambda i: (i, 0, 0)),
            pl.BlockSpec((rounds * CH, width), lambda i: (0, 0)),
            pl.BlockSpec((LAGS, 2 * F), lambda i: (0, 0)),
        ],
        out_specs=pl.BlockSpec((rounds, step, CH, LAGS), lambda i: (0, i, 0, 0)),
        scratch_shapes=[pltpu.VMEM((4, 2 * LAGS, width), jnp.bfloat16)],
        compiler_params=pltpu.CompilerParams(vmem_limit_bytes=limit),
        name="correlate",
    )(
        masks,
        own.reshape(CH // step, step, width),
        other,
        jnp.asarray(lag_table(nfft, F, LAGS)),
    )


def solution(mesh):
    return jax.shard_map(
        local,
        mesh=mesh,
        in_specs=(
            P(("groups", "blk"), None),
            P(("groups", "blk"), None),
            P(("groups", "blk"), None),
            P(("groups", "blk"), None),
            P(),
        ),
        out_specs=P(None, ("groups", "blk"), None, None),
        check_vma=False,
    )
```

```python
import functools
import math

import jax
import jax.numpy as jnp
import numpy as np
from jax import lax
from jax.experimental import pallas as pl
from jax.experimental.pallas import tpu as pltpu
from jax.sharding import PartitionSpec as P

CH = 128
F = 256
LAGS = 128
W = 2
GROUP = 4
CHUNK = 256
AHEAD = 2
PIECES = 8
FLIGHT = 4
LAG = 3
GAP = 64.0
LEVELS = (
    ((96, 96, 96, 80, 64, 64, 48, 32), (64, 64, 64, 64, 48, 48, 32, 16)),
    ((112, 112, 96, 80, 64, 64, 48, 32), (64, 64, 64, 64, 48, 48, 32, 32)),
    ((112, 112, 112, 96, 80, 64, 48, 32), (64, 64, 64, 64, 48, 48, 32, 32)),
    ((128, 128, 112, 96, 80, 80, 64, 48), (64, 64, 64, 64, 64, 48, 48, 32)),
)
VMEM = pl.BlockSpec(memory_space=pltpu.VMEM)
SMEM = pl.BlockSpec(memory_space=pltpu.SMEM)
HBM = pl.BlockSpec(memory_space=pl.ANY)
MESH = pl.DeviceIdType.MESH


def forward_table(nfft, bins):
    sample = np.arange(nfft, dtype=np.int64)[:, None]
    freq = np.arange(1, bins + 1, dtype=np.int64)[None, :]
    angle = (sample * freq % nfft).astype(np.float32) * np.float32(2.0 * math.pi / nfft)
    return np.concatenate([np.cos(angle), -np.sin(angle)], axis=1).astype(jnp.bfloat16)


def lag_table(nfft, bins, lags):
    shift = (np.arange(lags, dtype=np.int64) - lags // 2) % nfft
    freq = np.arange(1, bins + 1, dtype=np.int64)[None, :]
    angle = (freq * shift[:, None] % nfft).astype(np.float32) * np.float32(2.0 * math.pi / nfft)
    return np.concatenate([np.cos(angle), -np.sin(angle)], axis=1).astype(jnp.bfloat16)


def met_at(me, distance, owners):
    other = me
    for k in range(owners.bit_length() - 1):
        if distance >> k & 1:
            other = other + (1 << k) * (1 - 2 * lax.rem(lax.div(me, 1 << k), 2))
    return other


def gathered_at(distance):
    bits = GROUP.bit_length() - 1
    return sum((distance >> k & 1) << (bits - 1 - k) for k in range(bits))


def split_at(planes, most):
    return planes == 4 and most >= 32


def kept_at(planes, most):
    return GROUP * planes * most * (3 if split_at(planes, most) else 4) // 4


def capacities(most, chunks):
    def scaled(level, bound, unit):
        rows = [-(-level[c * len(level) // chunks] * bound // (unit * 16)) * 16 for c in range(chunks)]
        return tuple(min(bound, max(16, r)) for r in rows)

    full = ((most,) * chunks, (most // 2,) * chunks)
    found = []
    for far, near in LEVELS:
        rows = (scaled(far, most, 128), scaled(near, most // 2, 64))
        if rows not in found and rows[0] != full[0]:
            found.append(rows)
    return found + [full]


def first_sends(planes, split):
    if not split:
        return [(d, 0, False) for d in range(planes - 1, -1, -1)]
    other = GROUP // 2
    return [(3, 0, False), (2, 0, False), (1, 0, True), (1, other, True), (0, other, True), (0, 0, True)]


def plan_kernel(
    records_ref, dest_ref, slot_ref, valid_ref,
    outgoing_ref, first_ref, goal_ref, level_ref,
    outbox, inbox, levels, send_sem, recv_sem, level_sems, first_sems, own_sem,
):
    chunks, planes, most, wide = outgoing_ref.shape
    owners = planes * GROUP
    held = records_ref.shape[0]
    me, part = lax.axis_index("blk"), lax.axis_index("groups")
    parts = levels.shape[0]
    shift = most.bit_length() - 1
    plane = lax.div(me, GROUP)

    barrier = pltpu.get_barrier_semaphore()
    for distance in range(1, owners):
        pl.semaphore_signal(
            barrier, inc=1, device_id={"blk": met_at(me, distance, owners)}, device_id_type=MESH
        )
    abroad = [
        (turn, distance, {"groups": lax.rem(part + turn, parts), "blk": met_at(me, distance, owners)})
        for turn in range(1, parts)
        for distance in range(owners)
    ]
    for _, _, other in abroad:
        pl.semaphore_signal(barrier, inc=1, device_id=other, device_id_type=MESH)

    dest, slot, valid = dest_ref[...], slot_ref[...], valid_ref[...]
    group, within = lax.div(dest, GROUP), lax.rem(dest, GROUP)
    key = valid * held + (held - 1 - lax.broadcasted_iota(jnp.int32, (1, held), 1))
    line = lax.broadcasted_iota(jnp.int32, (8, held), 0)
    split = split_at(planes, most)
    half = most // 2
    chip = lax.div(within, GROUP // 2)
    if split:
        near = (group >> 1) == lax.div(plane, 2)
    else:
        near = group < 0
    kind = group * 4 + jnp.where(near, 1 + chip, 0)
    columns = jnp.where(line == 0, kind, jnp.where(line == 1, key, valid)).astype(jnp.float32).T
    key, kind = key.astype(jnp.float32), kind.astype(jnp.float32)
    ahead = (columns[:, 1:2] > key) & (columns[:, 0:1] == kind)
    rank = jnp.sum(ahead.astype(jnp.float32), axis=0, keepdims=True).astype(jnp.int32)
    reach = lax.div(valid - 1, wide)
    level = jnp.zeros((1, held), jnp.float32)
    for far_rows, near_rows in capacities(most, chunks)[:-1]:
        limit = jnp.zeros((1, held), jnp.int32)
        for c in range(chunks):
            limit = jnp.where(reach == c, jnp.where(near, near_rows[c], far_rows[c]), limit)
        level = level + jnp.max((rank >= limit).astype(jnp.float32), axis=1, keepdims=True)
    levels[0, 0] = level[:, :128]
    rank = rank + jnp.where(near, chip * half, 0)

    lines = max(8, planes)
    named = lax.broadcasted_iota(jnp.int32, (lines, held), 0) == group
    ranked = (lax.broadcasted_iota(jnp.int32, (128, held), 0) == rank).astype(jnp.float32)
    ranked = ranked.astype(jnp.bfloat16)

    def spread(values):
        values = jnp.where(named, values, 0).astype(jnp.float32).astype(jnp.bfloat16)
        return lax.dot_general(
            values, ranked, (((1,), (1,)), ((), ())), preferred_element_type=jnp.float32
        )

    code = spread(within + 1) * 256.0 + spread(slot)
    for p in range(planes):
        outbox[p, 0:1, :] = code[p : p + 1]
        outbox[p, 1:2, :] = level[:, :128]

    spots = planes * most
    place = lax.broadcasted_iota(jnp.int32, (spots, held), 0) == group * most + rank
    place = place.astype(jnp.float32).astype(jnp.bfloat16)
    ends = columns[:, 2:3].astype(jnp.int32)

    def pack(c):
        window = lax.broadcasted_iota(jnp.int32, (held, wide), 1) + c * wide < ends
        window = window.astype(jnp.float32).astype(jnp.bfloat16)
        data = records_ref[:, c * wide : (c + 1) * wide] * window + (GAP - GAP * window)
        packed = jnp.dot(place, data, preferred_element_type=jnp.float32)
        outgoing_ref[c] = packed.astype(jnp.bfloat16).reshape(planes, most, wide)

    pack(0)
    pl.semaphore_wait(barrier, owners * parts - 1)
    copies = []
    for turn, distance, other in abroad:
        copies.append(
            pltpu.make_async_remote_copy(
                src_ref=levels.at[0, 0],
                dst_ref=levels.at[turn, distance],
                send_sem=level_sems.at[0, turn, distance],
                recv_sem=level_sems.at[1, turn, distance],
                device_id=other,
                device_id_type=MESH,
            )
        )
        copies[-1].start()
    for distance in range(owners - 1, 0, -1):
        other = met_at(me, distance, owners)
        copies.append(
            pltpu.make_async_remote_copy(
                src_ref=outbox.at[lax.div(other, GROUP)],
                dst_ref=inbox.at[gathered_at(distance % GROUP) * planes + plane],
                send_sem=send_sem.at[distance],
                recv_sem=recv_sem.at[distance],
                device_id={"blk": other},
                device_id_type=MESH,
            )
        )
        copies[-1].start()
    row = lax.rem(lax.div(me, GROUP // 2), 2)
    first = []
    for index, (d, turned, near) in enumerate(first_sends(planes, split)):
        other = met_at(me, GROUP * d + turned, owners)
        rows = pl.ds(0, most)
        if near:
            at = row if turned == 0 else 1 - row
            rows = pl.ds(pl.multiple_of(at * half, 16), half)
        source = outgoing_ref.at[0, lax.div(other, GROUP), rows]
        target = first_ref.at[1 if turned else 0, plane, rows]
        if d == 0 and turned == 0:
            first.append(pltpu.make_async_copy(source, target, own_sem))
        else:
            first.append(
                pltpu.make_async_remote_copy(
                    src_ref=source,
                    dst_ref=target,
                    send_sem=first_sems.at[0, index],
                    recv_sem=first_sems.at[1, index],
                    device_id={"blk": other},
                    device_id_type=MESH,
                )
            )
        first[-1].start()
    inbox[plane] = outbox[plane]

    for c in range(1, chunks):
        pack(c)

    kept = goal_ref.shape[1]
    at = lax.broadcasted_iota(jnp.int32, (1, kept), 1)
    source, spot = at >> shift, at & (most - 1)
    if split:
        near_base = lax.div(plane, 2) * 2
        far_base = 2 - near_base
        rest = at - GROUP * 2 * most
        source = jnp.where(
            rest < 0,
            (at >> (shift + 1)) * planes + far_base + ((at >> shift) & 1),
            (rest >> shift) * planes + near_base + ((rest >> (shift - 1)) & 1),
        )
        spot = jnp.where(rest < 0, spot, row * half + (rest & (half - 1)))
    sown = lax.broadcasted_iota(jnp.int32, (128, kept), 0) == spot
    sown = sown.astype(jnp.float32).astype(jnp.bfloat16)
    for copy in copies:
        copy.wait()
    code = inbox[:, 0, :]
    level = jnp.max(inbox[:, 1, :], axis=0, keepdims=True)
    for turn, distance, _ in abroad:
        level = jnp.maximum(level, levels[turn, distance])
    level_ref[0] = jnp.max(level).astype(jnp.int32)
    owner = (code * (1.0 / 256.0)).astype(jnp.int32).astype(jnp.float32)
    slots = code - owner * 256.0
    mine = lax.broadcasted_iota(jnp.int32, (owners, kept), 0) == source

    def line_up(values):
        values = jnp.dot(values.astype(jnp.bfloat16), sown, preferred_element_type=jnp.float32)
        return jnp.sum(jnp.where(mine, values, 0.0), axis=0, keepdims=True).astype(jnp.int32)

    slots = line_up(slots)
    goal = (slots & (W - 1)) * CH + (slots >> (W.bit_length() - 1))
    goal_ref[...] = jnp.where(line_up(owner) == lax.rem(me, GROUP) + 1, goal, -1)
    for copy in first:
        copy.wait()


def deliver_kernel(
    caps, outgoing_ref, first_ref, goal_ref, masks_ref, table_hbm,
    own_ref, met_ref,
    arrived, select, table, spectrum, energy, tile, leaving, landing,
    plane_send, plane_recv, gather_send, gather_recv, own_sem, table_sem,
    far_send, far_recv, hop_send, hop_recv,
):
    chunks, _, planes, most, wide = arrived.shape
    owners = planes * GROUP
    nfft = chunks * wide
    kept = goal_ref.shape[1]
    me = lax.axis_index("blk")
    plane = lax.div(me, GROUP)
    last = owners - 1
    bits = list(range(owners.bit_length() - 3, -1, -1))
    split = split_at(planes, most)
    half = most // 2
    row = lax.rem(lax.div(me, GROUP // 2), 2)
    near_base = lax.div(plane, 2) * 2
    far_planes = pl.ds(2 - near_base, 2) if split else pl.ds(0, planes)
    near_planes = pl.ds(near_base, 2)

    barrier = pltpu.get_barrier_semaphore()
    sends = first_sends(planes, split)
    peers = {GROUP * d + turned for d, turned, _ in sends} - {0}
    peers |= {GROUP // 2, 1} | {1 << k for k in bits} | {last}
    for distance in sorted(peers):
        pl.semaphore_signal(
            barrier, inc=1, device_id={"blk": met_at(me, distance, owners)}, device_id_type=MESH
        )
    fetch = pltpu.make_async_copy(table_hbm, table, table_sem)
    fetch.start()
    pl.semaphore_wait(barrier, len(peers))

    def send(distance, source, target, send_sem, recv_sem):
        copy = pltpu.make_async_remote_copy(
            src_ref=source,
            dst_ref=target,
            send_sem=send_sem,
            recv_sem=recv_sem,
            device_id={"blk": met_at(me, distance, owners)},
            device_id_type=MESH,
        )
        copy.start()
        return copy

    sent, local, gathers = {}, {}, {}

    def some(at, count):
        return pl.ds(pl.multiple_of(at * half, 16), count)

    def begin(c):
        for index, (d, turned, near) in enumerate(sends):
            other = lax.div(met_at(me, GROUP * d + turned, owners), GROUP)
            rows = pl.ds(0, caps[0][c])
            if near:
                rows = some(row if turned == 0 else 1 - row, caps[1][c])
            source = outgoing_ref.at[c, other, rows]
            target = arrived.at[c, 1 if turned else 0, plane, rows]
            if d == 0 and turned == 0:
                sent[c, index] = pltpu.make_async_copy(source, target, own_sem.at[c])
                sent[c, index].start()
            else:
                sent[c, index] = send(
                    GROUP * d + turned, source, target, plane_send.at[c, index], plane_recv.at[c, index]
                )

    def region(c, near):
        if near:
            return near_planes, some(row, caps[1][c])
        return far_planes, pl.ds(0, caps[0][c])

    def forward(c, which, early=False):
        planes_at, rows = region(c, which in (2, 4))
        held_at = 1 if which in (3, 4) else 0
        source = first_ref if early else arrived.at[c]
        gathers[c, which] = send(
            GROUP // 2 if which == 0 else 1,
            source.at[held_at, planes_at, rows],
            arrived.at[c, held_at + (1 if which == 0 else 2), planes_at, rows],
            gather_send.at[c, which],
            gather_recv.at[c, which],
        )

    def forward_first():
        forward(0, 0, True)
        forward(0, 1, True)
        for index, (held_at, near) in enumerate([(0, False), (0, True), (1, True)]):
            if near and not split:
                continue
            planes_at, rows = region(0, near)
            local[index] = pltpu.make_async_copy(
                first_ref.at[held_at, planes_at, rows],
                arrived.at[0, held_at, planes_at, rows],
                own_sem.at[chunks + index],
            )
            local[index].start()
            if near:
                forward(0, 2 * held_at + 2, True)

    ahead = min(AHEAD, chunks - 1)
    forward_first()
    for c in range(1, 1 + ahead):
        begin(c)
    def blank(c, planes_at, rows):
        rest = arrived.at[c, :, planes_at, rows, :]
        rest[...] = jnp.full(rest.shape, GAP, jnp.bfloat16)

    for c in range(chunks):
        if caps[0][c] < most:
            blank(c, far_planes, pl.ds(caps[0][c], most - caps[0][c]))
        if split:
            if caps[1][c] < half:
                start = pl.multiple_of(row * half + caps[1][c], 16)
                blank(c, near_planes, pl.ds(start, half - caps[1][c]))
    goal = goal_ref[...]
    width = min(512, kept)
    for base in range(0, kept, width):
        chosen = lax.broadcasted_iota(jnp.int32, (CH * W, width), 0) == goal[:, base : base + width]
        select[:, base : base + width] = chosen.astype(jnp.float32).astype(jnp.bfloat16)

    def compute(c):
        if split:
            data = jnp.concatenate(
                [
                    arrived[c, :, far_planes].reshape(2 * GROUP * most, wide),
                    arrived[c, :, near_planes, some(row, half)].reshape(2 * GROUP * half, wide),
                ],
                axis=0,
            )
        else:
            data = arrived[c].reshape(kept, wide)
        window = jnp.minimum(jnp.maximum(GAP / 2 - data, 0.0), 1.0)
        total = jnp.dot(select[...], data * window, preferred_element_type=jnp.float32)
        count = jnp.dot(select[...], window, preferred_element_type=jnp.float32)
        trace = total / jnp.maximum(count, 1.0)
        squares = trace * trace
        squares = sum(squares[:, k : k + 128] for k in range(0, wide, 128))
        part = jnp.dot(
            trace.astype(jnp.bfloat16),
            table[c * wide : (c + 1) * wide, :],
            preferred_element_type=jnp.float32,
        )
        if c == 0:
            energy[...], spectrum[...] = squares, part
        else:
            energy[...] += squares
            spectrum[...] += part

    for turn in range(1, chunks + 2):
        for stage in range(3):
            c = turn - stage
            if not 0 <= c < chunks:
                continue
            if stage == 0:
                if c + ahead < chunks:
                    begin(c + ahead)
                for index, (_, _, near) in enumerate(sends):
                    if not near:
                        (sent[c, index].wait_recv if sends[index][:2] != (0, 0) else sent[c, index].wait)()
                forward(c, 0)
                forward(c, 1)
                for index, (d, turned, near) in enumerate(sends):
                    if near:
                        (sent[c, index].wait_recv if d + turned else sent[c, index].wait)()
                if split:
                    forward(c, 2)
                    forward(c, 4)
            elif stage == 1:
                gathers[c, 0].wait_recv()
                forward(c, 3)
            else:
                for which in range(1, 5):
                    if (c, which) in gathers:
                        gathers[c, which].wait_recv()
                if c == 0:
                    fetch.wait()
                    for copy in local.values():
                        copy.wait()
                compute(c)

    second = masks_ref[0] ^ masks_ref[1] ^ last
    use_far = lax.div(second, 1 << (len(bits)))
    path = second + use_far * (last - 2 * second)
    size = CH // PIECES

    def choose(flag, yes, no):
        flag = jnp.full(yes.shape, flag.astype(jnp.float32), jnp.float32).astype(jnp.bfloat16)
        return yes * flag + no * (1 - flag)

    factor = lax.rsqrt(jnp.sum(energy[...], axis=1, keepdims=True) * (1.0 / nfft) + 1e-06)
    far = []

    def far_copy(q):
        rows = pl.ds(q * size, size)
        far.append(send(last, tile.at[rows], met_ref.at[rows], far_send.at[q], far_recv.at[q]))

    for q in range(PIECES):
        rows = slice(q * size, (q + 1) * size)
        for w in range(W):
            at = slice(w * CH + q * size, w * CH + (q + 1) * size)
            parts = spectrum[at, :] * factor[at]
            real_part, imag_part = parts[:, :F], parts[:, F:]
            amplitude = lax.rsqrt(
                jnp.maximum(real_part * real_part + imag_part * imag_part, nfft / 4.0)
            )
            real_part = (real_part * amplitude).astype(jnp.bfloat16)
            imag_part = (imag_part * amplitude).astype(jnp.bfloat16)
            base = 2 * F * w
            tile[rows, base : base + F] = real_part
            tile[rows, base + F : base + 2 * F] = imag_part
            own_ref[rows, base : base + F] = real_part.astype(jnp.float32)
            own_ref[rows, base + F : base + 2 * F] = imag_part.astype(jnp.float32)
        if q < FLIGHT:
            far_copy(q)

    hops = {}
    for turn in range(PIECES + LAG * len(bits)):
        for stage in range(len(bits) + 1):
            q = turn - LAG * stage
            if not 0 <= q < PIECES:
                continue
            rows = slice(q * size, (q + 1) * size)
            if stage == 0:
                far[q].wait_recv()
                if q + FLIGHT < PIECES:
                    far_copy(q + FLIGHT)
                value = choose(use_far, met_ref[rows], tile[rows])
            else:
                hops[stage - 1, q].wait_recv()
                taken = lax.rem(lax.div(path, 1 << bits[stage - 1]), 2)
                value = choose(taken, landing[stage - 1, rows], leaving[stage - 1, rows])
            if stage == len(bits):
                met_ref[CH + q * size : CH + (q + 1) * size] = value
            else:
                leaving[stage, rows] = value
                spot = pl.ds(q * size, size)
                hops[stage, q] = send(
                    1 << bits[stage],
                    leaving.at[stage, spot],
                    landing.at[stage, spot],
                    hop_send.at[stage, q],
                    hop_recv.at[stage, q],
                )
    abroad = [copy for (_, index), copy in sent.items() if sends[index][:2] != (0, 0)]
    for copy in abroad + list(gathers.values()) + far + list(hops.values()):
        copy.wait_send()


def correlate_kernel(masks_ref, own_ref, other_ref, table_ref, out_ref, turned, *, last):
    scale = 1.0 / math.sqrt(W * F)
    cosine, sine = table_ref[:, :F], table_ref[:, F:]
    far_round = (masks_ref[0] != last).astype(jnp.int32)
    slots, step = turned.shape[0], own_ref.shape[1]

    for index in range(step // 2):
        at = index % slots
        for half in range(2):
            mine = own_ref[0, index * 2 + half : index * 2 + half + 1, :].astype(jnp.bfloat16)
            rows = slice(half * LAGS, (half + 1) * LAGS)
            for w in range(W):
                base = 2 * F * w
                ur, ui = mine[:, base : base + F], mine[:, base + F : base + 2 * F]
                turned[at, rows, base : base + F] = cosine * ur + sine * ui
                turned[at, rows, base + F : base + 2 * F] = cosine * ui - sine * ur
        product = lax.dot_general(
            other_ref[...],
            turned[at],
            (((1,), (1,)), ((), ())),
            preferred_element_type=jnp.float32,
        )
        product = (product * scale).astype(jnp.bfloat16)
        for half in range(2):
            lags = slice(half * LAGS, (half + 1) * LAGS)
            out_ref[far_round, index * 2 + half] = product[:CH, lags]
            out_ref[1 - far_round, index * 2 + half] = product[CH:, lags]


def local(records, dest, slot, valid, masks):
    owners, parts = lax.axis_size("blk"), lax.axis_size("groups")
    held, nfft = records.shape
    rounds = masks.shape[0]
    planes, chunks = owners // GROUP, nfft // CHUNK
    most = max(16, GROUP * 2 * held // owners)
    width = 2 * F * W
    limit = 56 * 2**20
    outgoing, first, goal, level = pl.pallas_call(
        plan_kernel,
        out_shape=[
            jax.ShapeDtypeStruct((chunks, planes, most, CHUNK), jnp.bfloat16),
            jax.ShapeDtypeStruct((2, planes, most, CHUNK), jnp.bfloat16),
            jax.ShapeDtypeStruct((1, kept_at(planes, most)), jnp.int32),
            jax.ShapeDtypeStruct((1,), jnp.int32),
        ],
        in_specs=[VMEM] * 4,
        out_specs=[VMEM, VMEM, VMEM, SMEM],
        scratch_shapes=[
            pltpu.VMEM((planes, 2, 128), jnp.float32),
            pltpu.VMEM((owners, 2, 128), jnp.float32),
            pltpu.VMEM((parts, owners, 1, 128), jnp.float32),
            pltpu.SemaphoreType.DMA((owners,)),
            pltpu.SemaphoreType.DMA((owners,)),
            pltpu.SemaphoreType.DMA((2, parts, owners)),
            pltpu.SemaphoreType.DMA((2, planes + 2)),
            pltpu.SemaphoreType.DMA,
        ],
        compiler_params=pltpu.CompilerParams(
            vmem_limit_bytes=limit, collective_id=0, has_side_effects=True
        ),
        name="plan",
    )(records, dest.reshape(1, held), slot.reshape(1, held), valid.reshape(1, held))

    last = owners - 1
    hops = owners.bit_length() - 2

    def deliver(number, caps):
        def call(outgoing, first, goal, masks, table):
            return pl.pallas_call(
                functools.partial(deliver_kernel, caps),
                out_shape=[
                    jax.ShapeDtypeStruct((CH, width), jnp.float32),
                    jax.ShapeDtypeStruct((rounds * CH, width), jnp.bfloat16),
                ],
                in_specs=[HBM, HBM, VMEM, SMEM, HBM],
                out_specs=[VMEM] * 2,
                scratch_shapes=[
                    pltpu.VMEM((chunks, GROUP, planes, most, CHUNK), jnp.bfloat16),
                    pltpu.VMEM((CH * W, kept_at(planes, most)), jnp.bfloat16),
                    pltpu.VMEM((nfft, 2 * F), jnp.bfloat16),
                    pltpu.VMEM((CH * W, 2 * F), jnp.float32),
                    pltpu.VMEM((CH * W, 128), jnp.float32),
                    pltpu.VMEM((CH, width), jnp.bfloat16),
                    pltpu.VMEM((hops, CH, width), jnp.bfloat16),
                    pltpu.VMEM((hops, CH, width), jnp.bfloat16),
                    pltpu.SemaphoreType.DMA((chunks, planes + 2)),
                    pltpu.SemaphoreType.DMA((chunks, planes + 2)),
                    pltpu.SemaphoreType.DMA((chunks, 5)),
                    pltpu.SemaphoreType.DMA((chunks, 5)),
                    pltpu.SemaphoreType.DMA((chunks + 3,)),
                    pltpu.SemaphoreType.DMA,
                    pltpu.SemaphoreType.DMA((PIECES,)),
                    pltpu.SemaphoreType.DMA((PIECES,)),
                    pltpu.SemaphoreType.DMA((hops, PIECES)),
                    pltpu.SemaphoreType.DMA((hops, PIECES)),
                ],
                compiler_params=pltpu.CompilerParams(
                    vmem_limit_bytes=limit, collective_id=number, has_side_effects=True
                ),
                name=f"deliver{number}",
            )(outgoing, first, goal, masks, table)

        return call

    sizes = capacities(most, chunks)
    calls = [deliver(number + 1, caps) for number, caps in enumerate(sizes)]
    own, other = lax.switch(
        level[0], calls, outgoing, first, goal, masks, jnp.asarray(forward_table(nfft, F))
    )
    step = 32
    return pl.pallas_call(
        functools.partial(correlate_kernel, last=last),
        grid=(CH // step,),
        out_shape=jax.ShapeDtypeStruct((rounds, CH, CH, LAGS), jnp.bfloat16),
        in_specs=[
            SMEM,
            pl.BlockSpec((1, step, width), lambda i: (i, 0, 0)),
            pl.BlockSpec((rounds * CH, width), lambda i: (0, 0)),
            pl.BlockSpec((LAGS, 2 * F), lambda i: (0, 0)),
        ],
        out_specs=pl.BlockSpec((rounds, step, CH, LAGS), lambda i: (0, i, 0, 0)),
        scratch_shapes=[pltpu.VMEM((4, 2 * LAGS, width), jnp.bfloat16)],
        compiler_params=pltpu.CompilerParams(vmem_limit_bytes=limit),
        name="correlate",
    )(
        masks,
        own.reshape(CH // step, step, width),
        other,
        jnp.asarray(lag_table(nfft, F, LAGS)),
    )


def solution(mesh):
    return jax.shard_map(
        local,
        mesh=mesh,
        in_specs=(
            P(("groups", "blk"), None),
            P(("groups", "blk"), None),
            P(("groups", "blk"), None),
            P(("groups", "blk"), None),
            P(),
        ),
        out_specs=P(None, ("groups", "blk"), None, None),
        check_vma=False,
    )
```

```python
import functools
import math

import jax
import jax.numpy as jnp
import numpy as np
from jax import lax
from jax.experimental import pallas as pl
from jax.experimental.pallas import tpu as pltpu
from jax.sharding import PartitionSpec as P

CH = 128
F = 256
LAGS = 128
W = 2
GROUP = 4
CHUNK = 256
AHEAD = 2
PIECES = 8
FLIGHT = 4
LAG = 3
GAP = 64.0
LEVELS = (
    ((96, 96, 96, 80, 64, 64, 48, 32), (64, 64, 64, 64, 48, 48, 32, 16)),
    ((112, 112, 96, 80, 64, 64, 48, 32), (64, 64, 64, 64, 48, 48, 32, 32)),
    ((112, 112, 112, 96, 80, 64, 48, 32), (64, 64, 64, 64, 48, 48, 32, 32)),
    ((128, 128, 112, 96, 80, 80, 64, 48), (64, 64, 64, 64, 64, 48, 48, 32)),
)
VMEM = pl.BlockSpec(memory_space=pltpu.VMEM)
SMEM = pl.BlockSpec(memory_space=pltpu.SMEM)
HBM = pl.BlockSpec(memory_space=pl.ANY)
MESH = pl.DeviceIdType.MESH


def forward_table(nfft, bins):
    sample = np.arange(nfft, dtype=np.int64)[:, None]
    freq = np.arange(1, bins + 1, dtype=np.int64)[None, :]
    angle = (sample * freq % nfft).astype(np.float32) * np.float32(2.0 * math.pi / nfft)
    return np.concatenate([np.cos(angle), -np.sin(angle)], axis=1).astype(jnp.bfloat16)


def lag_table(nfft, bins, lags):
    shift = (np.arange(lags, dtype=np.int64) - lags // 2) % nfft
    freq = np.arange(1, bins + 1, dtype=np.int64)[None, :]
    angle = (freq * shift[:, None] % nfft).astype(np.float32) * np.float32(2.0 * math.pi / nfft)
    return np.concatenate([np.cos(angle), -np.sin(angle)], axis=1).astype(jnp.bfloat16)


def met_at(me, distance, owners):
    other = me
    for k in range(owners.bit_length() - 1):
        if distance >> k & 1:
            other = other + (1 << k) * (1 - 2 * lax.rem(lax.div(me, 1 << k), 2))
    return other


def gathered_at(distance):
    bits = GROUP.bit_length() - 1
    return sum((distance >> k & 1) << (bits - 1 - k) for k in range(bits))


def split_at(planes, most):
    return planes == 4 and most >= 32


def kept_at(planes, most):
    return GROUP * planes * most * (3 if split_at(planes, most) else 4) // 4


def capacities(most, chunks):
    def scaled(level, bound, unit):
        rows = [-(-level[c * len(level) // chunks] * bound // (unit * 16)) * 16 for c in range(chunks)]
        return tuple(min(bound, max(16, r)) for r in rows)

    full = ((most,) * chunks, (most // 2,) * chunks)
    found = []
    for far, near in LEVELS:
        rows = (scaled(far, most, 128), scaled(near, most // 2, 64))
        if rows not in found and rows[0] != full[0]:
            found.append(rows)
    return found + [full]


def first_sends(planes, split):
    if not split:
        return [(d, 0, False) for d in range(planes - 1, -1, -1)]
    other = GROUP // 2
    return [(3, 0, False), (2, 0, False), (1, 0, True), (1, other, True), (0, other, True), (0, 0, True)]


def plan_kernel(
    records_ref, dest_ref, slot_ref, valid_ref,
    outgoing_ref, first_ref, goal_ref, level_ref,
    outbox, inbox, levels, send_sem, recv_sem, level_sems, first_sems, own_sem,
):
    chunks, planes, most, wide = outgoing_ref.shape
    owners = planes * GROUP
    held = records_ref.shape[0]
    me, part = lax.axis_index("blk"), lax.axis_index("groups")
    parts = levels.shape[0]
    shift = most.bit_length() - 1
    plane = lax.div(me, GROUP)

    barrier = pltpu.get_barrier_semaphore()
    for distance in range(1, owners):
        pl.semaphore_signal(
            barrier, inc=1, device_id={"blk": met_at(me, distance, owners)}, device_id_type=MESH
        )
    abroad = [
        (turn, distance, {"groups": lax.rem(part + turn, parts), "blk": met_at(me, distance, owners)})
        for turn in range(1, parts)
        for distance in range(owners)
    ]
    for _, _, other in abroad:
        pl.semaphore_signal(barrier, inc=1, device_id=other, device_id_type=MESH)

    dest, slot, valid = dest_ref[...], slot_ref[...], valid_ref[...]
    group, within = lax.div(dest, GROUP), lax.rem(dest, GROUP)
    key = valid * held + (held - 1 - lax.broadcasted_iota(jnp.int32, (1, held), 1))
    line = lax.broadcasted_iota(jnp.int32, (8, held), 0)
    split = split_at(planes, most)
    half = most // 2
    chip = lax.div(within, GROUP // 2)
    if split:
        near = (group >> 1) == lax.div(plane, 2)
    else:
        near = group < 0
    kind = group * 4 + jnp.where(near, 1 + chip, 0)
    columns = jnp.where(line == 0, kind, jnp.where(line == 1, key, valid)).astype(jnp.float32).T
    key, kind = key.astype(jnp.float32), kind.astype(jnp.float32)
    ahead = (columns[:, 1:2] > key) & (columns[:, 0:1] == kind)
    rank = jnp.sum(ahead.astype(jnp.float32), axis=0, keepdims=True).astype(jnp.int32)
    reach = lax.div(valid - 1, wide)
    level = jnp.zeros((1, held), jnp.float32)
    for far_rows, near_rows in capacities(most, chunks)[:-1]:
        limit = jnp.zeros((1, held), jnp.int32)
        for c in range(chunks):
            limit = jnp.where(reach == c, jnp.where(near, near_rows[c], far_rows[c]), limit)
        level = level + jnp.max((rank >= limit).astype(jnp.float32), axis=1, keepdims=True)
    levels[0, 0] = level[:, :128]
    rank = rank + jnp.where(near, chip * half, 0)

    lines = max(8, planes)
    named = lax.broadcasted_iota(jnp.int32, (lines, held), 0) == group
    ranked = (lax.broadcasted_iota(jnp.int32, (128, held), 0) == rank).astype(jnp.float32)
    ranked = ranked.astype(jnp.bfloat16)

    def spread(values):
        values = jnp.where(named, values, 0).astype(jnp.float32).astype(jnp.bfloat16)
        return lax.dot_general(
            values, ranked, (((1,), (1,)), ((), ())), preferred_element_type=jnp.float32
        )

    code = spread(within + 1) * 256.0 + spread(slot)
    for p in range(planes):
        outbox[p, 0:1, :] = code[p : p + 1]
        outbox[p, 1:2, :] = level[:, :128]

    spots = planes * most
    place = lax.broadcasted_iota(jnp.int32, (spots, held), 0) == group * most + rank
    place = place.astype(jnp.float32).astype(jnp.bfloat16)
    ends = columns[:, 2:3].astype(jnp.int32)

    def pack(c):
        window = lax.broadcasted_iota(jnp.int32, (held, wide), 1) + c * wide < ends
        window = window.astype(jnp.float32).astype(jnp.bfloat16)
        data = records_ref[:, c * wide : (c + 1) * wide] * window + (GAP - GAP * window)
        packed = jnp.dot(place, data, preferred_element_type=jnp.float32)
        outgoing_ref[c] = packed.astype(jnp.bfloat16).reshape(planes, most, wide)

    pack(0)
    pl.semaphore_wait(barrier, owners * parts - 1)
    copies = []
    for turn, distance, other in abroad:
        copies.append(
            pltpu.make_async_remote_copy(
                src_ref=levels.at[0, 0],
                dst_ref=levels.at[turn, distance],
                send_sem=level_sems.at[0, turn, distance],
                recv_sem=level_sems.at[1, turn, distance],
                device_id=other,
                device_id_type=MESH,
            )
        )
        copies[-1].start()
    for distance in range(owners - 1, 0, -1):
        other = met_at(me, distance, owners)
        copies.append(
            pltpu.make_async_remote_copy(
                src_ref=outbox.at[lax.div(other, GROUP)],
                dst_ref=inbox.at[gathered_at(distance % GROUP) * planes + plane],
                send_sem=send_sem.at[distance],
                recv_sem=recv_sem.at[distance],
                device_id={"blk": other},
                device_id_type=MESH,
            )
        )
        copies[-1].start()
    row = lax.rem(lax.div(me, GROUP // 2), 2)
    first = []
    for index, (d, turned, near) in enumerate(first_sends(planes, split)):
        other = met_at(me, GROUP * d + turned, owners)
        rows = pl.ds(0, most)
        if near:
            at = row if turned == 0 else 1 - row
            rows = pl.ds(pl.multiple_of(at * half, 16), half)
        source = outgoing_ref.at[0, lax.div(other, GROUP), rows]
        target = first_ref.at[1 if turned else 0, plane, rows]
        if d == 0 and turned == 0:
            first.append(pltpu.make_async_copy(source, target, own_sem))
        else:
            first.append(
                pltpu.make_async_remote_copy(
                    src_ref=source,
                    dst_ref=target,
                    send_sem=first_sems.at[0, index],
                    recv_sem=first_sems.at[1, index],
                    device_id={"blk": other},
                    device_id_type=MESH,
                )
            )
        first[-1].start()
    inbox[plane] = outbox[plane]

    for c in range(1, chunks):
        pack(c)

    kept = goal_ref.shape[1]
    at = lax.broadcasted_iota(jnp.int32, (1, kept), 1)
    source, spot = at >> shift, at & (most - 1)
    if split:
        near_base = lax.div(plane, 2) * 2
        far_base = 2 - near_base
        rest = at - GROUP * 2 * most
        source = jnp.where(
            rest < 0,
            (at >> (shift + 1)) * planes + far_base + ((at >> shift) & 1),
            (rest >> shift) * planes + near_base + ((rest >> (shift - 1)) & 1),
        )
        spot = jnp.where(rest < 0, spot, row * half + (rest & (half - 1)))
    sown = lax.broadcasted_iota(jnp.int32, (128, kept), 0) == spot
    sown = sown.astype(jnp.float32).astype(jnp.bfloat16)
    for copy in copies:
        copy.wait()
    code = inbox[:, 0, :]
    level = jnp.max(inbox[:, 1, :], axis=0, keepdims=True)
    for turn, distance, _ in abroad:
        level = jnp.maximum(level, levels[turn, distance])
    level_ref[0] = jnp.max(level).astype(jnp.int32)
    owner = (code * (1.0 / 256.0)).astype(jnp.int32).astype(jnp.float32)
    slots = code - owner * 256.0
    mine = lax.broadcasted_iota(jnp.int32, (owners, kept), 0) == source

    def line_up(values):
        values = jnp.dot(values.astype(jnp.bfloat16), sown, preferred_element_type=jnp.float32)
        return jnp.sum(jnp.where(mine, values, 0.0), axis=0, keepdims=True).astype(jnp.int32)

    slots = line_up(slots)
    goal = (slots & (W - 1)) * CH + (slots >> (W.bit_length() - 1))
    goal_ref[...] = jnp.where(line_up(owner) == lax.rem(me, GROUP) + 1, goal, -1)
    for copy in first:
        copy.wait()


def deliver_kernel(
    caps, outgoing_ref, first_ref, goal_ref, masks_ref, table_hbm,
    own_ref, met_ref,
    arrived, select, table, spectrum, energy, tile, leaving, landing,
    plane_send, plane_recv, gather_send, gather_recv, own_sem, table_sem,
    far_send, far_recv, hop_send, hop_recv,
):
    chunks, _, planes, most, wide = arrived.shape
    owners = planes * GROUP
    nfft = chunks * wide
    kept = goal_ref.shape[1]
    me = lax.axis_index("blk")
    plane = lax.div(me, GROUP)
    last = owners - 1
    bits = list(range(owners.bit_length() - 3, -1, -1))
    split = split_at(planes, most)
    half = most // 2
    row = lax.rem(lax.div(me, GROUP // 2), 2)
    near_base = lax.div(plane, 2) * 2
    far_planes = pl.ds(2 - near_base, 2) if split else pl.ds(0, planes)
    near_planes = pl.ds(near_base, 2)

    barrier = pltpu.get_barrier_semaphore()
    sends = first_sends(planes, split)
    peers = {GROUP * d + turned for d, turned, _ in sends} - {0}
    peers |= {GROUP // 2, 1} | {1 << k for k in bits} | {last}
    for distance in sorted(peers):
        pl.semaphore_signal(
            barrier, inc=1, device_id={"blk": met_at(me, distance, owners)}, device_id_type=MESH
        )
    fetch = pltpu.make_async_copy(table_hbm, table, table_sem)
    fetch.start()
    pl.semaphore_wait(barrier, len(peers))

    def send(distance, source, target, send_sem, recv_sem):
        copy = pltpu.make_async_remote_copy(
            src_ref=source,
            dst_ref=target,
            send_sem=send_sem,
            recv_sem=recv_sem,
            device_id={"blk": met_at(me, distance, owners)},
            device_id_type=MESH,
        )
        copy.start()
        return copy

    sent, local, gathers = {}, {}, {}

    def some(at, count):
        return pl.ds(pl.multiple_of(at * half, 16), count)

    def begin(c):
        for index, (d, turned, near) in enumerate(sends):
            other = lax.div(met_at(me, GROUP * d + turned, owners), GROUP)
            rows = pl.ds(0, caps[0][c])
            if near:
                rows = some(row if turned == 0 else 1 - row, caps[1][c])
            source = outgoing_ref.at[c, other, rows]
            target = arrived.at[c, 1 if turned else 0, plane, rows]
            if d == 0 and turned == 0:
                sent[c, index] = pltpu.make_async_copy(source, target, own_sem.at[c])
                sent[c, index].start()
            else:
                sent[c, index] = send(
                    GROUP * d + turned, source, target, plane_send.at[c, index], plane_recv.at[c, index]
                )

    def region(c, near):
        if near:
            return near_planes, some(row, caps[1][c])
        return far_planes, pl.ds(0, caps[0][c])

    def forward(c, which, early=False):
        planes_at, rows = region(c, which in (2, 4))
        held_at = 1 if which in (3, 4) else 0
        source = first_ref if early else arrived.at[c]
        gathers[c, which] = send(
            GROUP // 2 if which == 0 else 1,
            source.at[held_at, planes_at, rows],
            arrived.at[c, held_at + (1 if which == 0 else 2), planes_at, rows],
            gather_send.at[c, which],
            gather_recv.at[c, which],
        )

    def forward_first():
        forward(0, 0, True)
        forward(0, 1, True)
        for index, (held_at, near) in enumerate([(0, False), (0, True), (1, True)]):
            if near and not split:
                continue
            planes_at, rows = region(0, near)
            local[index] = pltpu.make_async_copy(
                first_ref.at[held_at, planes_at, rows],
                arrived.at[0, held_at, planes_at, rows],
                own_sem.at[chunks + index],
            )
            local[index].start()
            if near:
                forward(0, 2 * held_at + 2, True)

    ahead = min(AHEAD, chunks - 1)
    for c in range(1, 1 + ahead):
        begin(c)
    forward_first()
    def blank(c, planes_at, rows):
        rest = arrived.at[c, :, planes_at, rows, :]
        rest[...] = jnp.full(rest.shape, GAP, jnp.bfloat16)

    for c in range(chunks):
        if caps[0][c] < most:
            blank(c, far_planes, pl.ds(caps[0][c], most - caps[0][c]))
        if split:
            if caps[1][c] < half:
                start = pl.multiple_of(row * half + caps[1][c], 16)
                blank(c, near_planes, pl.ds(start, half - caps[1][c]))
    goal = goal_ref[...]
    width = min(512, kept)
    for base in range(0, kept, width):
        chosen = lax.broadcasted_iota(jnp.int32, (CH * W, width), 0) == goal[:, base : base + width]
        select[:, base : base + width] = chosen.astype(jnp.float32).astype(jnp.bfloat16)

    def compute(c):
        if split:
            data = jnp.concatenate(
                [
                    arrived[c, :, far_planes].reshape(2 * GROUP * most, wide),
                    arrived[c, :, near_planes, some(row, half)].reshape(2 * GROUP * half, wide),
                ],
                axis=0,
            )
        else:
            data = arrived[c].reshape(kept, wide)
        window = jnp.minimum(jnp.maximum(GAP / 2 - data, 0.0), 1.0)
        total = jnp.dot(select[...], data * window, preferred_element_type=jnp.float32)
        count = jnp.dot(select[...], window, preferred_element_type=jnp.float32)
        trace = total / jnp.maximum(count, 1.0)
        squares = trace * trace
        squares = sum(squares[:, k : k + 128] for k in range(0, wide, 128))
        part = jnp.dot(
            trace.astype(jnp.bfloat16),
            table[c * wide : (c + 1) * wide, :],
            preferred_element_type=jnp.float32,
        )
        if c == 0:
            energy[...], spectrum[...] = squares, part
        else:
            energy[...] += squares
            spectrum[...] += part

    for turn in range(1, chunks + 2):
        for stage in range(3):
            c = turn - stage
            if not 0 <= c < chunks:
                continue
            if stage == 0:
                if c + ahead < chunks:
                    begin(c + ahead)
                for index, (_, _, near) in enumerate(sends):
                    if not near:
                        (sent[c, index].wait_recv if sends[index][:2] != (0, 0) else sent[c, index].wait)()
                forward(c, 0)
                forward(c, 1)
                for index, (d, turned, near) in enumerate(sends):
                    if near:
                        (sent[c, index].wait_recv if d + turned else sent[c, index].wait)()
                if split:
                    forward(c, 2)
                    forward(c, 4)
            elif stage == 1:
                gathers[c, 0].wait_recv()
                forward(c, 3)
            else:
                for which in range(1, 5):
                    if (c, which) in gathers:
                        gathers[c, which].wait_recv()
                if c == 0:
                    fetch.wait()
                    for copy in local.values():
                        copy.wait()
                compute(c)

    second = masks_ref[0] ^ masks_ref[1] ^ last
    use_far = lax.div(second, 1 << (len(bits)))
    path = second + use_far * (last - 2 * second)
    size = CH // PIECES

    def choose(flag, yes, no):
        flag = jnp.full(yes.shape, flag.astype(jnp.float32), jnp.float32).astype(jnp.bfloat16)
        return yes * flag + no * (1 - flag)

    factor = lax.rsqrt(jnp.sum(energy[...], axis=1, keepdims=True) * (1.0 / nfft) + 1e-06)
    far = []

    def far_copy(q):
        rows = pl.ds(q * size, size)
        far.append(send(last, tile.at[rows], met_ref.at[rows], far_send.at[q], far_recv.at[q]))

    for q in range(PIECES):
        rows = slice(q * size, (q + 1) * size)
        for w in range(W):
            at = slice(w * CH + q * size, w * CH + (q + 1) * size)
            parts = spectrum[at, :] * factor[at]
            real_part, imag_part = parts[:, :F], parts[:, F:]
            amplitude = lax.rsqrt(
                jnp.maximum(real_part * real_part + imag_part * imag_part, nfft / 4.0)
            )
            real_part = (real_part * amplitude).astype(jnp.bfloat16)
            imag_part = (imag_part * amplitude).astype(jnp.bfloat16)
            base = 2 * F * w
            tile[rows, base : base + F] = real_part
            tile[rows, base + F : base + 2 * F] = imag_part
            own_ref[rows, base : base + F] = real_part.astype(jnp.float32)
            own_ref[rows, base + F : base + 2 * F] = imag_part.astype(jnp.float32)
        if q < FLIGHT:
            far_copy(q)

    hops = {}
    for turn in range(PIECES + LAG * len(bits)):
        for stage in range(len(bits) + 1):
            q = turn - LAG * stage
            if not 0 <= q < PIECES:
                continue
            rows = slice(q * size, (q + 1) * size)
            if stage == 0:
                far[q].wait_recv()
                if q + FLIGHT < PIECES:
                    far_copy(q + FLIGHT)
                value = choose(use_far, met_ref[rows], tile[rows])
            else:
                hops[stage - 1, q].wait_recv()
                taken = lax.rem(lax.div(path, 1 << bits[stage - 1]), 2)
                value = choose(taken, landing[stage - 1, rows], leaving[stage - 1, rows])
            if stage == len(bits):
                met_ref[CH + q * size : CH + (q + 1) * size] = value
            else:
                leaving[stage, rows] = value
                spot = pl.ds(q * size, size)
                hops[stage, q] = send(
                    1 << bits[stage],
                    leaving.at[stage, spot],
                    landing.at[stage, spot],
                    hop_send.at[stage, q],
                    hop_recv.at[stage, q],
                )
    abroad = [copy for (_, index), copy in sent.items() if sends[index][:2] != (0, 0)]
    for copy in abroad + list(gathers.values()) + far + list(hops.values()):
        copy.wait_send()


def correlate_kernel(masks_ref, own_ref, other_ref, table_ref, out_ref, turned, *, last):
    scale = 1.0 / math.sqrt(W * F)
    cosine, sine = table_ref[:, :F], table_ref[:, F:]
    far_round = (masks_ref[0] != last).astype(jnp.int32)
    slots, step = turned.shape[0], own_ref.shape[1]

    for index in range(step // 2):
        at = index % slots
        for half in range(2):
            mine = own_ref[0, index * 2 + half : index * 2 + half + 1, :].astype(jnp.bfloat16)
            rows = slice(half * LAGS, (half + 1) * LAGS)
            for w in range(W):
                base = 2 * F * w
                ur, ui = mine[:, base : base + F], mine[:, base + F : base + 2 * F]
                turned[at, rows, base : base + F] = cosine * ur + sine * ui
                turned[at, rows, base + F : base + 2 * F] = cosine * ui - sine * ur
        product = lax.dot_general(
            other_ref[...],
            turned[at],
            (((1,), (1,)), ((), ())),
            preferred_element_type=jnp.float32,
        )
        product = (product * scale).astype(jnp.bfloat16)
        for half in range(2):
            lags = slice(half * LAGS, (half + 1) * LAGS)
            out_ref[far_round, index * 2 + half] = product[:CH, lags]
            out_ref[1 - far_round, index * 2 + half] = product[CH:, lags]


def local(records, dest, slot, valid, masks):
    owners, parts = lax.axis_size("blk"), lax.axis_size("groups")
    held, nfft = records.shape
    rounds = masks.shape[0]
    planes, chunks = owners // GROUP, nfft // CHUNK
    most = max(16, GROUP * 2 * held // owners)
    width = 2 * F * W
    limit = 56 * 2**20
    outgoing, first, goal, level = pl.pallas_call(
        plan_kernel,
        out_shape=[
            jax.ShapeDtypeStruct((chunks, planes, most, CHUNK), jnp.bfloat16),
            jax.ShapeDtypeStruct((2, planes, most, CHUNK), jnp.bfloat16),
            jax.ShapeDtypeStruct((1, kept_at(planes, most)), jnp.int32),
            jax.ShapeDtypeStruct((1,), jnp.int32),
        ],
        in_specs=[VMEM] * 4,
        out_specs=[VMEM, VMEM, VMEM, SMEM],
        scratch_shapes=[
            pltpu.VMEM((planes, 2, 128), jnp.float32),
            pltpu.VMEM((owners, 2, 128), jnp.float32),
            pltpu.VMEM((parts, owners, 1, 128), jnp.float32),
            pltpu.SemaphoreType.DMA((owners,)),
            pltpu.SemaphoreType.DMA((owners,)),
            pltpu.SemaphoreType.DMA((2, parts, owners)),
            pltpu.SemaphoreType.DMA((2, planes + 2)),
            pltpu.SemaphoreType.DMA,
        ],
        compiler_params=pltpu.CompilerParams(
            vmem_limit_bytes=limit, collective_id=0, has_side_effects=True
        ),
        name="plan",
    )(records, dest.reshape(1, held), slot.reshape(1, held), valid.reshape(1, held))

    last = owners - 1
    hops = owners.bit_length() - 2

    def deliver(number, caps):
        def call(outgoing, first, goal, masks, table):
            return pl.pallas_call(
                functools.partial(deliver_kernel, caps),
                out_shape=[
                    jax.ShapeDtypeStruct((CH, width), jnp.float32),
                    jax.ShapeDtypeStruct((rounds * CH, width), jnp.bfloat16),
                ],
                in_specs=[HBM, HBM, VMEM, SMEM, HBM],
                out_specs=[VMEM] * 2,
                scratch_shapes=[
                    pltpu.VMEM((chunks, GROUP, planes, most, CHUNK), jnp.bfloat16),
                    pltpu.VMEM((CH * W, kept_at(planes, most)), jnp.bfloat16),
                    pltpu.VMEM((nfft, 2 * F), jnp.bfloat16),
                    pltpu.VMEM((CH * W, 2 * F), jnp.float32),
                    pltpu.VMEM((CH * W, 128), jnp.float32),
                    pltpu.VMEM((CH, width), jnp.bfloat16),
                    pltpu.VMEM((hops, CH, width), jnp.bfloat16),
                    pltpu.VMEM((hops, CH, width), jnp.bfloat16),
                    pltpu.SemaphoreType.DMA((chunks, planes + 2)),
                    pltpu.SemaphoreType.DMA((chunks, planes + 2)),
                    pltpu.SemaphoreType.DMA((chunks, 5)),
                    pltpu.SemaphoreType.DMA((chunks, 5)),
                    pltpu.SemaphoreType.DMA((chunks + 3,)),
                    pltpu.SemaphoreType.DMA,
                    pltpu.SemaphoreType.DMA((PIECES,)),
                    pltpu.SemaphoreType.DMA((PIECES,)),
                    pltpu.SemaphoreType.DMA((hops, PIECES)),
                    pltpu.SemaphoreType.DMA((hops, PIECES)),
                ],
                compiler_params=pltpu.CompilerParams(
                    vmem_limit_bytes=limit, collective_id=number, has_side_effects=True
                ),
                name=f"deliver{number}",
            )(outgoing, first, goal, masks, table)

        return call

    sizes = capacities(most, chunks)
    calls = [deliver(number + 1, caps) for number, caps in enumerate(sizes)]
    own, other = lax.switch(
        level[0], calls, outgoing, first, goal, masks, jnp.asarray(forward_table(nfft, F))
    )
    step = 32
    return pl.pallas_call(
        functools.partial(correlate_kernel, last=last),
        grid=(CH // step,),
        out_shape=jax.ShapeDtypeStruct((rounds, CH, CH, LAGS), jnp.bfloat16),
        in_specs=[
            SMEM,
            pl.BlockSpec((1, step, width), lambda i: (i, 0, 0)),
            pl.BlockSpec((rounds * CH, width), lambda i: (0, 0)),
            pl.BlockSpec((LAGS, 2 * F), lambda i: (0, 0)),
        ],
        out_specs=pl.BlockSpec((rounds, step, CH, LAGS), lambda i: (0, i, 0, 0)),
        scratch_shapes=[pltpu.VMEM((4, 2 * LAGS, width), jnp.bfloat16)],
        compiler_params=pltpu.CompilerParams(vmem_limit_bytes=limit),
        name="correlate",
    )(
        masks,
        own.reshape(CH // step, step, width),
        other,
        jnp.asarray(lag_table(nfft, F, LAGS)),
    )


def solution(mesh):
    return jax.shard_map(
        local,
        mesh=mesh,
        in_specs=(
            P(("groups", "blk"), None),
            P(("groups", "blk"), None),
            P(("groups", "blk"), None),
            P(("groups", "blk"), None),
            P(),
        ),
        out_specs=P(None, ("groups", "blk"), None, None),
        check_vma=False,
    )
```
